32 devices in a mesh: region: 4 (over y, x), tile: 8 (over z, core).
Axes of the slice: x: 2, y: 2, z: 4, core: 2. Of those that a mesh axis runs over, the one named last changes fastest.
Arguments:
- features: bfloat16 [128, 32, 512], P(('region', 'tile')), may hold values from -6 to 6
- voxel_mask: int32 [128, 512], P(('region', 'tile')), may hold values 0 or 1
- brick_cell: int32 [128], P(('region', 'tile')), may hold values from -1 to 7, as said below
- conv_one: bfloat16 [27, 32, 32], replicated, may hold values from -0.3125 to 0.3125
- conv_two: bfloat16 [27, 32, 32], replicated, may hold values from -0.3125 to 0.3125
- down_weight: bfloat16 [8, 32, 64], replicated, may hold values from -0.375 to 0.375
- cotangent: bfloat16 [128, 4096], P(('region', 'tile')), may hold values from -6 to 6
Outputs:
- down: bfloat16 [128, 4096], P(('region', 'tile'))
- grad_features: bfloat16 [128, 32, 512], P(('region', 'tile'))
- grad_conv_one: float32 [27, 32, 32], replicated
- grad_conv_two: float32 [27, 32, 32], replicated
- grad_down: float32 [8, 32, 64], replicated
The draws below stay inside these ranges and needn't reach their ends.
Inputs may be any that keep to these rules, and one draw needn't show every extreme that they name: `brick_cell`: entries come in blocks of 4, one block a device in the order of the slots. The live entries of a block name distinct brick cells of that device's box; -1 marks an empty slot, and in at least one block every entry is live.
All inputs are finite; a program needn't handle non-finite values. No bound on the sum of `voxel_mask` on one device may be relied on, other than what follows from the above.
Results may differ from the reference program's by a relative error of at most 0.0053.
Values may be sent and summed in bfloat16 or wider, within the bound.
No kernel may reach another device: no remote copies, remote signals or barrier semaphores. Data moves between devices by JAX's collectives and lax.ppermute only.
A program may use at most 192 MiB of HBM per device.

```python
import jax
import jax.numpy as jnp
from jax import lax

CHANNELS = 32
DOWN_CH = 64
BR_DEV = 4
TOTAL_BRICKS = 128
N_REGION = 4
N_TILE = 8


def draw_brick_cell(key, part):
    device_count = TOTAL_BRICKS // BR_DEV
    key_count, key_full, key_cells, key_slots = jax.random.split(key, 4)
    lowest = max(BR_DEV // 4, 1)
    counts = jax.random.randint(key_count, (device_count,), lowest, BR_DEV + 1)
    fullest = jax.random.randint(key_full, (), 0, device_count)
    counts = jnp.where(jnp.arange(device_count) == fullest, BR_DEV, counts)
    cell_scores = jax.random.randint(key_cells, (device_count, 2 * BR_DEV), 0, 1 << 20) * (2 * BR_DEV) + jnp.arange(2 * BR_DEV)[None, :]
    chosen = jnp.argsort(cell_scores, axis=1)[:, :BR_DEV]
    slot_scores = jax.random.randint(key_slots, (device_count, BR_DEV), 0, 1 << 20) * BR_DEV + jnp.arange(BR_DEV)[None, :]
    slot_rank = jnp.argsort(jnp.argsort(slot_scores, axis=1), axis=1)
    cell_list = jnp.where(slot_rank < counts[:, None], chosen, -1)
    return cell_list.reshape(-1).astype(jnp.int32)


def place_ends(result, key, smallest, high):
    place = [jax.random.randint(jax.random.fold_in(key, axis), (), 0, length) for axis, length in enumerate(result.shape)]
    main_axis = result.shape.index(max(result.shape))
    next_to = place[:main_axis] + [(place[main_axis] + 1) % result.shape[main_axis]] + place[main_axis + 1:]
    return result.at[tuple(place)].set(smallest).at[tuple(next_to)].set(high)


def block_levels(stream_key, shape, cuts, smallest, high):
    level, own = 1.0, jax.random.fold_in(stream_key, 6)
    for position, shards_of in cuts:
        steps = jnp.exp(jax.random.uniform(jax.random.fold_in(own, position), (shards_of,), jnp.float32, smallest / len(cuts), high / len(cuts)))
        level = level * jnp.repeat(steps, shape[position] // shards_of).reshape([-1 if axis == position else 1 for axis in range(len(shape))])
    return level


def scatter_about(rng, extent, scale, reach, cuts=(), held_as=jnp.bfloat16):
    factor_of = block_levels(rng, extent, cuts, -0.22, 0.18) if cuts else 1.0
    values = jax.random.normal(rng, extent, jnp.float32) * scale * factor_of
    return jnp.minimum(jnp.maximum(values, -reach), reach).astype(held_as)


def setup_inputs(seed: int = 0) -> dict:
    key_list = jax.random.split(jax.random.key(seed), 8)
    features = scatter_about(key_list[0], (TOTAL_BRICKS, CHANNELS, 512), 1.0, 6.0, ((0, 32),))
    voxel_mask = place_ends((jax.random.randint(key_list[1], (TOTAL_BRICKS, 512), 0, 4) < 3).astype(jnp.int32), jax.random.fold_in(key_list[1], 1), 0, 1)
    brick_cell = draw_brick_cell(jax.random.fold_in(key_list[7], 71), 0)
    conv_one = scatter_about(key_list[3], (27, CHANNELS, CHANNELS), (13 * CHANNELS) ** -0.5, 0.3125)
    conv_two = scatter_about(key_list[4], (27, CHANNELS, CHANNELS), (13 * CHANNELS) ** -0.5, 0.3125)
    down_weight = scatter_about(key_list[5], (8, CHANNELS, DOWN_CH), (8 * CHANNELS) ** -0.5, 0.375)
    cotangent = scatter_about(key_list[6], (TOTAL_BRICKS, DOWN_CH * 64), 1.0, 6.0, ((0, 32),))
    return dict(features=features, voxel_mask=voxel_mask, brick_cell=brick_cell, conv_one=conv_one, conv_two=conv_two, down_weight=down_weight, cotangent=cotangent)


def global_tables(brick_cell):
    slot_ids = jnp.arange(TOTAL_BRICKS, dtype=jnp.int32)
    device_ids = slot_ids // BR_DEV
    region_ids = device_ids // N_TILE
    tile_ids = device_ids % N_TILE
    live_slot = brick_cell >= 0
    cell_index = jnp.maximum(brick_cell, 0)
    brick_x = 2 * region_ids + cell_index // BR_DEV
    brick_z = cell_index % BR_DEV
    size_y = 8 * N_TILE + 2
    size_z = 8 * BR_DEV + 2
    voxel_index = jnp.arange(512, dtype=jnp.int32)
    global_x = 8 * brick_x[:, None] + voxel_index[None, :] // 64
    global_y = 8 * tile_ids[:, None] + voxel_index[None, :] // 8 % 8
    global_z = 8 * brick_z[:, None] + voxel_index[None, :] % 8
    base_index = ((global_x + 1) * size_y + global_y + 1) * size_z + global_z + 1
    offsets = [(shift_x * size_y + shift_y) * size_z + shift_z for shift_x in (-1, 0, 1) for shift_y in (-1, 0, 1) for shift_z in (-1, 0, 1)]
    grid_owner = jnp.full((2 * N_REGION, N_TILE, BR_DEV), TOTAL_BRICKS, dtype=jnp.int32)
    grid_owner = grid_owner.at[jnp.where(live_slot, brick_x, 2 * N_REGION), tile_ids, brick_z].set(slot_ids, mode='drop')
    return (live_slot, base_index, jnp.array(offsets, dtype=jnp.int32), grid_owner)

def global_field(values, grid_owner):
    channel_count = values.shape[1]
    padding = jnp.zeros((1, channel_count, 512), values.dtype)
    bricks = jnp.concatenate([values, padding], axis=0)[grid_owner]
    bricks = bricks.reshape(2 * N_REGION, N_TILE, BR_DEV, channel_count, 8, 8, 8)
    bricks = bricks.transpose(3, 0, 4, 1, 5, 2, 6)
    field = bricks.reshape(channel_count, 16 * N_REGION, 8 * N_TILE, 8 * BR_DEV)
    field = jnp.pad(field, ((0, 0), (1, 1), (1, 1), (1, 1)))
    return field.reshape(channel_count, -1)

def device_blocks(base_index):
    return base_index.reshape(TOTAL_BRICKS // BR_DEV, BR_DEV * 512)

def apply_conv(flat, base_index, offsets, weights, sign):
    weights_wide = weights.astype(jnp.float32)

    def one_block(block_index):
        index_all = (block_index[None, :] + sign * offsets[:, None]).reshape(-1)
        columns = jnp.take(flat, index_all, axis=1).reshape(flat.shape[0], 27, -1).astype(jnp.float32)
        if sign > 0:
            return jnp.einsum('ikn,kio->on', columns, weights_wide)
        return jnp.einsum('okn,kio->in', columns, weights_wide)
    planes = lax.map(one_block, device_blocks(base_index))
    count = planes.shape[1]
    planes = planes.reshape(TOTAL_BRICKS // BR_DEV, count, BR_DEV, 512).transpose(0, 2, 1, 3)
    return planes.reshape(TOTAL_BRICKS, count, 512)

def weight_grad(flat, base_index, offsets, grads):
    count = grads.shape[1]
    grad_blocks = grads.reshape(TOTAL_BRICKS // BR_DEV, BR_DEV, count, 512).transpose(0, 2, 1, 3)
    grad_blocks = grad_blocks.reshape(TOTAL_BRICKS // BR_DEV, count, BR_DEV * 512)

    def add_block(total, pair):
        block_index, block_grad = pair
        index_all = (block_index[None, :] + offsets[:, None]).reshape(-1)
        columns = jnp.take(flat, index_all, axis=1).reshape(flat.shape[0], 27, -1).astype(jnp.float32)
        return (total + jnp.einsum('ikn,on->kio', columns, block_grad.astype(jnp.float32)), None)
    start = jnp.zeros((27, flat.shape[0], count), jnp.float32)
    total, _ = lax.scan(add_block, start, (device_blocks(base_index), grad_blocks))
    return total

def reference(features, voxel_mask, brick_cell, conv_one, conv_two, down_weight, cotangent):
    live_slot, base_index, offsets, grid_owner = global_tables(brick_cell)
    mask_slot = (voxel_mask.astype(jnp.float32) * live_slot[:, None].astype(jnp.float32))[:, None, :]
    inputs = features * mask_slot.astype(jnp.bfloat16)
    input_flat = global_field(inputs, grid_owner)
    first_pre = apply_conv(input_flat, base_index, offsets, conv_one, 1) * mask_slot
    hidden = jax.nn.silu(first_pre).astype(jnp.bfloat16)
    hidden_flat = global_field(hidden, grid_owner)
    second_pre = apply_conv(hidden_flat, base_index, offsets, conv_two, 1) * mask_slot
    summed = (inputs.astype(jnp.float32) + second_pre).astype(jnp.bfloat16)
    shaped = summed.reshape(TOTAL_BRICKS, CHANNELS, 4, 2, 4, 2, 4, 2).astype(jnp.float32)
    kernel = down_weight.reshape(2, 2, 2, CHANNELS, DOWN_CH).astype(jnp.float32)
    down = jnp.einsum('tcxaybzd,abdco->toxyz', shaped, kernel).reshape(TOTAL_BRICKS, -1).astype(jnp.bfloat16)
    upstream = cotangent.reshape(TOTAL_BRICKS, DOWN_CH, 4, 4, 4).astype(jnp.float32)
    back_sum = jnp.einsum('toxyz,abdco->tcxaybzd', upstream, kernel).reshape(TOTAL_BRICKS, CHANNELS, 512)
    down_grad = jnp.einsum('tcxaybzd,toxyz->abdco', shaped, upstream).reshape(8, CHANNELS, DOWN_CH)
    second_grad = (back_sum * mask_slot).astype(jnp.bfloat16)
    grad_flat = global_field(second_grad, grid_owner)
    weight_two = weight_grad(hidden_flat, base_index, offsets, second_grad)
    spread = apply_conv(grad_flat, base_index, offsets, conv_two, -1)
    sigmoid_value = jax.nn.sigmoid(first_pre)
    first_grad = (spread * sigmoid_value * (1.0 + first_pre * (1.0 - sigmoid_value)) * mask_slot).astype(jnp.bfloat16)
    first_flat = global_field(first_grad, grid_owner)
    weight_one = weight_grad(input_flat, base_index, offsets, first_grad)
    input_grad = (back_sum + apply_conv(first_flat, base_index, offsets, conv_one, -1)) * mask_slot
    scale = (TOTAL_BRICKS * 512.0) ** (-0.5)
    return (down, input_grad.astype(jnp.bfloat16), weight_one * scale, weight_two * scale, down_grad * scale)
```

```python
import functools
import math

import jax
import jax.numpy as jnp
from jax import lax
from jax.experimental import pallas as pl
from jax.experimental.pallas import tpu as pltpu
from jax.sharding import PartitionSpec as P


BF = jnp.bfloat16
F32 = jnp.float32
I32 = jnp.int32
NN = (((1,), (0,)), ((), ()))
NT = (((1,), (1,)), ((), ()))
AXES = ("region", "tile")
VMEM_LIMIT = 56 * 1024 * 1024


def dot(lhs, rhs, dims=NN):
    return lax.dot_general(lhs, rhs, dims, preferred_element_type=F32)


def iota(shape, dim):
    return lax.broadcasted_iota(I32, shape, dim)


def parity_fields(v):
    return v & 1, (v >> 6) & 1, (v >> 3) & 1


def octant_rows(first=0):
    e = iota((8, 512), 0)
    d, a, b = parity_fields(iota((8, 512), 1))
    return (d == (e >> 2)) & (a == ((e >> 1) & 1)) & (b == (e & 1))


def row_codes():
    row = iota((512, 128), 0)
    code = ((row >> 6) & 3) * 16 + ((row >> 4) & 3) * 4 + (row & 3)
    cell = (row >> 8) * 4 + ((row >> 2) & 3)
    return code, cell


def place_fine(cell_ref, place):
    code, cell = row_codes()
    for q in range(4):
        code_q = jnp.where(cell == cell_ref[q], code, -1)
        for t in range(4):
            v = iota((1, 128), 1) + 128 * t
            vcode = (v >> 7) * 16 + ((v >> 4) & 3) * 4 + ((v >> 1) & 3)
            first = q * 512 + t * 128
            place[:, first : first + 128] = jnp.where(code_q == vcode, 1.0, 0.0).astype(BF)


def coarse_tile(cell_ref, t):
    code, cell = row_codes()
    lane = iota((512, 128), 1)
    wanted = jnp.where(lane < 64, cell_ref[2 * t], cell_ref[2 * t + 1])
    return jnp.where((cell == wanted) & (code == (lane & 63)), 1.0, 0.0).astype(BF)


def gather_kernel(cell_ref, feat_ref, vmask_ref, cot_ref, own, xlo, xhi, ylo, yhi, ll, lh, hl, hh, lhs, rhs):
    place_fine(cell_ref, lhs)
    for t in range(2):
        lhs[:, 2048 + t * 128 : 2048 + t * 128 + 128] = coarse_tile(cell_ref, t)
    match = octant_rows()
    for q in range(4):
        cols = slice(q * 512, q * 512 + 512)
        m8 = jnp.where(match, vmask_ref[q : q + 1, :].astype(F32), 0.0)
        x = feat_ref[q].astype(F32)
        for e in range(8):
            rhs[e * 32 : e * 32 + 32, cols] = (x * m8[e : e + 1, :]).astype(BF)
        rhs[256:320, cols] = jnp.zeros((64, 512), BF)
        rhs[320:336, cols] = jnp.concatenate([m8, jnp.zeros((8, 512), F32)], axis=0).astype(BF)
        rhs[336:384, cols] = jnp.zeros((48, 512), BF)
    rhs[0:256, 2048:2304] = jnp.zeros((256, 256), BF)
    rhs[256:320, 2048:2304] = cot_ref[...]
    rhs[320:384, 2048:2304] = jnp.zeros((64, 256), BF)
    field = dot(lhs[...], rhs[...], NT).astype(BF).reshape(8, 4, 16, 384)
    own[...] = field
    xlo[...] = field[0]
    xhi[...] = field[7]
    ylo[...] = field[:, 0]
    yhi[...] = field[:, 3]
    ll[...] = field[0, 0]
    lh[...] = field[0, 3]
    hl[...] = field[7, 0]
    hh[...] = field[7, 3]


def tap_of(far, source, target):
    position = source if far == 0 else (2 if source == 0 else -1)
    tap = position - target
    return tap if -1 <= tap <= 1 else None


def weights_kernel(w1_ref, w2_ref, dw_ref, big1, big1t, big2, big2t, down_mat, rep, tiles, tiles_t):
    lane = iota((32, 128), 1)
    spread = jnp.where((lane & 31) == iota((32, 128), 0), 1.0, 0.0).astype(BF)
    eye = jnp.where(iota((32, 32), 0) == iota((32, 32), 1), 1.0, 0.0).astype(BF)
    group = [jnp.where((lane >> 5) == g, 1.0, 0.0).astype(BF) for g in range(4)]
    for w_ref, big, big_t in ((w1_ref, big1, big1t), (w2_ref, big2, big2t)):
        tiles[...] = dot(w_ref[...], spread).astype(BF)
        w3 = w_ref[...].reshape(27, 32, 32)
        for j in range(4):
            rep[:, j] = w3
        tiles_t[...] = dot(eye, rep[...].reshape(27 * 128, 32), NT).astype(BF)
        for s in range(8):
            sx, sy, sz = s >> 2, (s >> 1) & 1, s & 1
            for e in range(8):
                d, a, b = e >> 2, (e >> 1) & 1, e & 1
                first = s * 256 + e * 32
                for td in range(2):
                    plain = None
                    turned = None
                    for g in range(4):
                        taps = (tap_of(sx, a, g >> 1), tap_of(sy, b, g & 1), tap_of(sz, d, td))
                        if None in taps:
                            continue
                        k = 9 * (taps[0] + 1) + 3 * (taps[1] + 1) + taps[2] + 1
                        back = 26 - k
                        term = tiles[k * 32 : k * 32 + 32, :] * group[g]
                        term_t = tiles_t[:, back * 128 : back * 128 + 128] * group[g]
                        plain = term if plain is None else plain + term
                        turned = term_t if turned is None else turned + term_t
                    zero = jnp.zeros((32, 128), BF)
                    big[first : first + 32, td * 128 : td * 128 + 128] = zero if plain is None else plain
                    big_t[first : first + 32, td * 128 : td * 128 + 128] = zero if turned is None else turned
    for e in range(8):
        d, a, b = e >> 2, (e >> 1) & 1, e & 1
        down_mat[e * 32 : e * 32 + 32, 0:64] = dw_ref[4 * a + 2 * b + d]
    down_mat[0:256, 64:128] = jnp.zeros((256, 64), BF)
    unit = iota((256, 128), 1) - 64 == (iota((256, 128), 0) >> 5)
    down_mat[256:512, :] = jnp.where(unit, 1.0, 0.0).astype(BF)


def lane_picks():
    lane = iota((16, 512), 1)
    low_a = jnp.where(((lane >> 6) & 1) == 0, 1.0, 0.0).astype(BF) > 0.5
    low_b = jnp.where(((lane >> 5) & 1) == 0, 1.0, 0.0).astype(BF) > 0.5
    return low_a[None], low_b[None]


def put_field(store, x, y0, value):
    ny = value.shape[0]
    z = iota((ny, 16, 128), 1)
    store[x, y0 : y0 + ny, :, 0:256] = value
    up = pltpu.roll(value[:, :, 0:128].astype(F32), 15, 1)
    store[x, y0 : y0 + ny, :, 256:384] = jnp.where(z == 15, 0.0, up).astype(BF)
    dn = pltpu.roll(value[:, :, 128:256].astype(F32), 1, 1)
    store[x, y0 : y0 + ny, :, 384:512] = jnp.where(z == 0, 0.0, dn).astype(BF)


def clear_edges(store):
    store[0] = jnp.zeros((8, 16, 512), BF)
    store[11] = jnp.zeros((8, 16, 512), BF)

    def edge(x, carry):
        store[x, 0] = jnp.zeros((16, 512), BF)
        store[x, 7] = jnp.zeros((16, 512), BF)
        return carry

    lax.fori_loop(1, 11, edge, 0)


def widen(store, wide, x, at, y0, ny, picks):
    low_a, low_b = picks
    low_a = jnp.broadcast_to(low_a, (ny, 16, 512))
    low_b = jnp.broadcast_to(low_b, (ny, 16, 512))

    def at_y(dx, dy):
        return store[x + dx, y0 + dy : y0 + dy + ny]

    wide[at, :, :, 0:512] = at_y(0, 0)
    wide[at, :, :, 512:1024] = jnp.where(low_b, at_y(0, 1), at_y(0, -1))
    wide[at, :, :, 1024:1536] = jnp.where(low_a, at_y(1, 0), at_y(-1, 0))
    upper = jnp.where(low_b, at_y(1, 1), at_y(1, -1))
    lower = jnp.where(low_b, at_y(-1, 1), at_y(-1, -1))
    wide[at, :, :, 1536:2048] = jnp.where(low_a, upper, lower)


def fold_taps(products, terms, first_tap, held):
    lane = iota((32, 128), 1)
    for k in range(27):
        tap = (k // 9 - 1, k // 3 % 3 - 1, k % 3 - 1)
        total = None
        for g in range(4):
            part = None
            for td in range(2):
                far, source, target = [], [], []
                for t, parity in ((tap[0], g >> 1), (tap[1], g & 1)):
                    b = parity if t == 0 else 1 - parity
                    far.append(0 if 0 <= b + t <= 1 else 1)
                    target.append(b)
                pos = td + tap[2]
                far_z = 0 if 0 <= pos <= 1 else 1
                source_d = pos & 1
                s = far[0] * 4 + far[1] * 2 + far_z
                rows = (td * 4 + target[0] * 2 + target[1]) * 32
                cols = s * 256 + source_d * 128
                block = products[rows : rows + 32, cols : cols + 128]
                part = block if part is None else part + block
            total = part if total is None else jnp.where((lane >> 5) == g, part, total)
        total = total + pltpu.roll(total, 64, 1)
        total = total + pltpu.roll(total, 32, 1)
        slot = (first_tap + k) % 4
        held = total if held is None else jnp.where((lane >> 5) == slot, total, held)
        if slot == 3:
            row = (first_tap + k) // 4 * 32
            terms[row : row + 32, :] = held.astype(terms.dtype)
            held = None
    return held


def main_kernel(own, xlo, xhi, ylo, yhi, ll, lh, hl, hh, big1, big2, big2t, down_mat,
                terms, fg_out, bkm_out, mask_out, sum_out,
                field, ex, eg, eh, mk, ax, ag, ah, turned, products):
    picks = lane_picks()
    field[1:9, 1:5] = own[...]
    field[0, 1:5] = xlo[...]
    field[9, 1:5] = xhi[...]
    field[1:9, 0] = ylo[...]
    field[1:9, 5] = yhi[...]
    field[0, 0] = ll[...]
    field[0, 5] = lh[...]
    field[9, 0] = hl[...]
    field[9, 5] = hh[...]
    for store in (ex, eg, eh):
        clear_edges(store)

    def start(x, carry):
        row = field[x]
        put_field(ex, x + 1, 1, row[:, :, 0:256])
        both = dot(row[:, :, 256:384].reshape(96, 128), down_mat[...], NT)
        mask = both[:, 256:512]
        bkm = both[:, 0:256] * mask
        mk[x] = mask.astype(BF).reshape(6, 16, 256)
        products[pl.ds(pl.multiple_of(x * 96, 32), 96), 0:256] = bkm
        put_field(eg, x + 1, 1, bkm.astype(BF).reshape(6, 16, 256))
        return carry

    lax.fori_loop(0, 10, start, 0)

    def save(x, carry):
        bkm_out[x] = products[pl.ds(pl.multiple_of((x + 1) * 96 + 16, 16), 64), 0:256].reshape(4, 16, 256)
        mask_out[x] = mk[x + 1, 1:5]
        return carry

    lax.fori_loop(0, 8, save, 0)

    def first(i, carry):
        for j in range(2):
            widen(ex, ax, 2 * i + j + 1, 2 * i + j, 1, 6, picks)
            widen(eg, ag, 2 * i + j + 1, j, 1, 6, picks)
        mask = mk[pl.ds(2 * i, 2)].reshape(192, 256).astype(F32)
        pre = dot(ax[pl.ds(2 * i, 2)].reshape(192, 2048), big1[...]) * mask
        spread = dot(ag[...].reshape(192, 2048), big2t[...])
        s = jax.nn.sigmoid(pre)
        hidden = (pre * s).astype(BF).reshape(2, 6, 16, 256)
        grad = (spread * s * (1.0 + pre * (1.0 - s)) * mask).astype(BF).reshape(2, 6, 16, 256)
        for j in range(2):
            put_field(eh, 2 * i + j + 1, 1, hidden[j])
            fg_out[2 * i + j] = grad[j]
        return carry

    lax.fori_loop(0, 5, first, 0)

    def second(i, carry):
        for j in range(4):
            widen(eh, ah, 4 * i + j + 2, 4 * i + j, 2, 4, picks)
        pre = dot(ah[pl.ds(4 * i, 4)].reshape(256, 2048), big2[...])
        mask = mk[pl.ds(4 * i + 1, 4), 1:5].reshape(256, 256).astype(F32)
        inputs = field[pl.ds(4 * i + 1, 4), 1:5, :, 0:256].reshape(256, 256).astype(F32)
        summed = (inputs + pre * mask).astype(BF)
        sum_out[pl.ds(pl.multiple_of(256 * i, 256), 256), :] = summed
        return carry

    lax.fori_loop(0, 2, second, 0)

    held = None
    for source, grads in ((1, fg_out[1:9, 1:5]), (2, eg[2:10, 2:6, :, 0:256])):
        turned[...] = grads.reshape(512, 256).astype(F32).T.astype(BF)
        for s in range(8):
            cols = slice(s * 256, s * 256 + 256)
            wide = (ax[1:9, 1:5, :, cols] if source == 1 else ah[:, :, :, cols]).reshape(512, 256)
            products[0:256, cols] = dot(turned[...], wide)
        held = fold_taps(products, terms, 27 * (source - 1), held)
    terms[416:448, :] = held.astype(terms.dtype)
    cot = field[1:9, 1:5, :, 256:384].reshape(512, 128).astype(F32).T.astype(BF)
    grad_down = dot(cot, sum_out[...])
    terms[448:512, :] = grad_down[0:64, 0:128].astype(terms.dtype)
    terms[512:576, :] = grad_down[0:64, 128:256].astype(terms.dtype)
    rest = terms.shape[0] - 576
    if rest:
        terms[576:, :] = jnp.zeros((rest, 128), terms.dtype)


def tail_kernel(cell_ref, fg, bkm, mask, summed, big1t, down_mat, grad_features, down, ef, af, place, dense):
    picks = lane_picks()
    clear_edges(ef)

    def start(x, carry):
        put_field(ef, x + 1, 1, fg[x])
        return carry

    lax.fori_loop(0, 10, start, 0)

    def last(i, carry):
        for j in range(4):
            widen(ef, af, 4 * i + j + 2, j, 2, 4, picks)
        spread = dot(af[...].reshape(256, 2048), big1t[...])
        rows = pl.ds(4 * i, 4)
        grad = bkm[rows].reshape(256, 256) + spread * mask[rows].reshape(256, 256).astype(F32)
        dense[pl.ds(pl.multiple_of(256 * i, 256), 256), :] = grad.astype(BF)
        return carry

    lax.fori_loop(0, 2, last, 0)
    place_fine(cell_ref, place)
    turned = dense[...].astype(F32).T.astype(BF)
    pick = jnp.where(octant_rows(), 1.0, 0.0)
    for q in range(4):
        moved = dot(turned, place[:, q * 512 : q * 512 + 512])
        total = moved[0:32] * pick[0:1]
        for e in range(1, 8):
            total = total + moved[e * 32 : e * 32 + 32] * pick[e : e + 1]
        grad_features[q] = total.astype(BF)
    lowered = dot(summed[...], down_mat[0:256, :]).T.astype(BF)
    for t in range(2):
        moved = dot(lowered, coarse_tile(cell_ref, t))
        down[:, t * 128 : t * 128 + 128] = moved[0:64].astype(BF)


def reduce_kernel(parts, out):
    count = parts.shape[0]
    total = parts[0].astype(F32)
    for i in range(1, count):
        total = total + parts[i].astype(F32)
    total = total.astype(out.dtype)
    for i in range(count):
        out[i] = total


def finish_kernel(scale, sums, one, two, down):
    for m in range(14):
        block = (sums[m * 32 : m * 32 + 32, :].astype(F32) * scale).T
        for g in range(4):
            k = 4 * m + g
            if k < 27:
                one[k] = block[g * 32 : g * 32 + 32]
            elif k < 54:
                two[k - 27] = block[g * 32 : g * 32 + 32]
    for half in range(2):
        block = (sums[448 + 64 * half : 512 + 64 * half, :].astype(F32) * scale).T
        for g in range(4):
            down[4 * (g >> 1) + 2 * (g & 1) + half] = block[g * 32 : g * 32 + 32]


def vmem_call(kernel, outs, ins, scratch=(), smem_first=False, flops=0):
    specs = [pl.BlockSpec(memory_space=pltpu.VMEM) for _ in ins]
    if smem_first:
        specs[0] = pl.BlockSpec(memory_space=pltpu.SMEM)
    moved = sum(math.prod(x.shape) * x.dtype.itemsize for x in tuple(ins) + tuple(outs))
    return pl.pallas_call(
        kernel,
        out_shape=tuple(outs),
        in_specs=specs,
        out_specs=tuple(pl.BlockSpec(memory_space=pltpu.VMEM) for _ in outs),
        scratch_shapes=list(scratch),
        compiler_params=pltpu.CompilerParams(vmem_limit_bytes=VMEM_LIMIT),
        cost_estimate=pl.CostEstimate(flops=flops, bytes_accessed=moved, transcendentals=0),
    )(*ins)


def bf(*shape):
    return jax.ShapeDtypeStruct(shape, BF)


def f32(*shape):
    return jax.ShapeDtypeStruct(shape, F32)


def neighbours(regions, tiles, dx, dy):
    pairs = []
    for r in range(regions):
        for t in range(tiles):
            if 0 <= r + dx < regions and 0 <= t + dy < tiles:
                pairs.append(((r + dx) * tiles + t + dy, r * tiles + t))
    return pairs


def on_device(features, voxel_mask, brick_cell, conv_one, conv_two, down_weight, cotangent):
    regions, tiles = lax.axis_size("region"), lax.axis_size("tile")
    devices = regions * tiles
    slots = features.shape[0]
    cot = cotangent.reshape(slots, 64, 64).transpose(1, 0, 2).reshape(64, slots * 64)
    pieces = vmem_call(
        gather_kernel,
        [bf(8, 4, 16, 384), bf(4, 16, 384), bf(4, 16, 384), bf(8, 16, 384), bf(8, 16, 384)] + [bf(16, 384)] * 4,
        (brick_cell, features, voxel_mask, cot),
        [pltpu.VMEM((512, 2304), BF), pltpu.VMEM((384, 2304), BF)],
        smem_first=True,
        flops=2 * 512 * 2304 * 384,
    )
    own, xlo, xhi, ylo, yhi, ll, lh, hl, hh = pieces

    def fetch(piece, dx, dy):
        return lax.ppermute(piece, AXES, neighbours(regions, tiles, dx, dy))

    halos = (
        fetch(xhi, -1, 0), fetch(xlo, 1, 0), fetch(yhi, 0, -1), fetch(ylo, 0, 1),
        fetch(hh, -1, -1), fetch(hl, -1, 1), fetch(lh, 1, -1), fetch(ll, 1, 1),
    )
    big1, big1t, big2, big2t, down_mat = vmem_call(
        weights_kernel,
        [bf(2048, 256)] * 4 + [bf(512, 128)],
        (conv_one.reshape(864, 32), conv_two.reshape(864, 32), down_weight),
        [pltpu.VMEM((27, 4, 32, 32), BF), pltpu.VMEM((864, 128), BF), pltpu.VMEM((32, 3456), BF)],
        flops=2 * 2 * 32 * 3456 * 256,
    )
    chunk = -(-(-(-576 // devices)) // 8) * 8
    terms, fg, bkm, mask, summed = vmem_call(
        main_kernel,
        [bf(devices * chunk, 128), bf(10, 6, 16, 256), f32(8, 4, 16, 256), bf(8, 4, 16, 256), bf(512, 256)],
        (own,) + halos + (big1, big2, big2t, down_mat),
        [
            pltpu.VMEM((10, 6, 16, 384), BF),
            pltpu.VMEM((12, 8, 16, 512), BF),
            pltpu.VMEM((12, 8, 16, 512), BF),
            pltpu.VMEM((12, 8, 16, 512), BF),
            pltpu.VMEM((10, 6, 16, 256), BF),
            pltpu.VMEM((10, 6, 16, 2048), BF),
            pltpu.VMEM((2, 6, 16, 2048), BF),
            pltpu.VMEM((8, 4, 16, 2048), BF),
            pltpu.VMEM((256, 512), BF),
            pltpu.VMEM((960, 2048), F32),
        ],
        flops=2 * 2048 * 256 * (960 * 2 + 512 * 3),
    )
    parts = lax.all_to_all(terms.reshape(devices, chunk, 128), AXES, 0, 0, tiled=True)
    (total,) = vmem_call(reduce_kernel, [f32(devices, chunk, 128)], (parts,))
    sums = lax.all_to_all(total, AXES, 0, 0, tiled=True)
    grad_features, down = vmem_call(
        tail_kernel,
        [bf(slots, 32, 512), bf(64, slots * 64)],
        (brick_cell, fg, bkm, mask, summed, big1t, down_mat),
        [
            pltpu.VMEM((12, 8, 16, 512), BF),
            pltpu.VMEM((4, 4, 16, 2048), BF),
            pltpu.VMEM((512, 2048), BF),
            pltpu.VMEM((512, 256), BF),
        ],
        smem_first=True,
        flops=2 * 2048 * 512 * 512,
    )
    down = down.reshape(64, slots, 64).transpose(1, 0, 2).reshape(slots, 4096)
    scale = 1.0 / math.sqrt(devices * slots * 512.0)
    grad_one, grad_two, grad_down = vmem_call(
        functools.partial(finish_kernel, scale),
        [f32(27, 32, 32), f32(27, 32, 32), f32(8, 32, 64)],
        (sums.reshape(devices * chunk, 128),),
    )
    return down, grad_features, grad_one, grad_two, grad_down


def solution(mesh):
    in_specs = (
        P(AXES, None, None),
        P(AXES, None),
        P(AXES),
        P(),
        P(),
        P(),
        P(AXES, None),
    )
    out_specs = (P(AXES, None), P(AXES, None, None), P(), P(), P())
    return jax.shard_map(
        on_device, mesh=mesh, in_specs=in_specs, out_specs=out_specs, check_vma=False
    )
```

```python
import functools
import math

import jax
import jax.numpy as jnp
from jax import lax
from jax.experimental import pallas as pl
from jax.experimental.pallas import tpu as pltpu
from jax.sharding import PartitionSpec as P


BF = jnp.bfloat16
F32 = jnp.float32
I32 = jnp.int32
NN = (((1,), (0,)), ((), ()))
NT = (((1,), (1,)), ((), ()))
AXES = ("region", "tile")


def dot(lhs, rhs, dims=NN):
    return lax.dot_general(lhs, rhs, dims, preferred_element_type=F32)


def iota(shape, dim):
    return lax.broadcasted_iota(I32, shape, dim)


def parity_fields(v):
    return v & 1, (v >> 6) & 1, (v >> 3) & 1


def octant_rows(first=0):
    e = iota((8, 512), 0)
    d, a, b = parity_fields(iota((8, 512), 1))
    return (d == (e >> 2)) & (a == ((e >> 1) & 1)) & (b == (e & 1))


def row_codes():
    row = iota((512, 128), 0)
    code = ((row >> 6) & 3) * 16 + ((row >> 4) & 3) * 4 + (row & 3)
    cell = (row >> 8) * 4 + ((row >> 2) & 3)
    return code, cell


def place_fine(cell_ref, place):
    code, cell = row_codes()
    for q in range(4):
        code_q = jnp.where(cell == cell_ref[q], code, -1)
        for t in range(4):
            v = iota((1, 128), 1) + 128 * t
            vcode = (v >> 7) * 16 + ((v >> 4) & 3) * 4 + ((v >> 1) & 3)
            first = q * 512 + t * 128
            place[:, first : first + 128] = jnp.where(code_q == vcode, 1.0, 0.0).astype(BF)


def coarse_tile(cell_ref, t):
    code, cell = row_codes()
    lane = iota((512, 128), 1)
    wanted = jnp.where(lane < 64, cell_ref[2 * t], cell_ref[2 * t + 1])
    return jnp.where((cell == wanted) & (code == (lane & 63)), 1.0, 0.0).astype(BF)


def gather_kernel(cell_ref, feat_ref, vmask_ref, cot_ref, own, faces, ylo, yhi, lhs, rhs, shuffle):
    place_fine(cell_ref, lhs)
    for t in range(2):
        lhs[:, 2048 + t * 128 : 2048 + t * 128 + 128] = coarse_tile(cell_ref, t)
    match = octant_rows()
    for q in range(4):
        cols = slice(q * 512, q * 512 + 512)
        m8 = jnp.where(match, vmask_ref[q : q + 1, :].astype(F32), 0.0)
        x = feat_ref[q].astype(F32)
        for e in range(8):
            rhs[e * 32 : e * 32 + 32, cols] = (x * m8[e : e + 1, :]).astype(BF)
        rhs[256:320, cols] = jnp.zeros((64, 512), BF)
        rhs[320:336, cols] = jnp.concatenate([m8, jnp.zeros((8, 512), F32)], axis=0).astype(BF)
        rhs[336:384, cols] = jnp.zeros((48, 512), BF)
    rhs[0:256, 2048:2304] = jnp.zeros((256, 256), BF)
    for j in range(32):
        shuffle[j, 0:4, :] = cot_ref[:, j * 128 : j * 128 + 128].astype(F32)
    low = iota((32, 128), 1) < 64
    for t in range(2):
        first, second = shuffle[:, 2 * t, :], shuffle[:, 2 * t + 1, :]
        cols = slice(2048 + t * 128, 2176 + t * 128)
        rhs[256:288, cols] = jnp.where(low, first, pltpu.roll(second, 64, 1)).astype(BF)
        rhs[288:320, cols] = jnp.where(low, pltpu.roll(first, 64, 1), second).astype(BF)
    rhs[320:384, 2048:2304] = jnp.zeros((64, 256), BF)
    field = dot(lhs[...], rhs[...], NT).astype(BF).reshape(8, 4, 16, 384)
    own[...] = field
    ylo[...] = field[:, 0]
    yhi[...] = field[:, 3]
    here = lax.axis_index("region")
    for p in range(faces.shape[0]):
        faces[p] = own[jnp.where(p < here, 0, 7)]


def x_halo(faces, place):
    here = lax.axis_index("region")
    count = faces.shape[0]
    for at, there in ((0, here - 1), (9, here + 1)):
        inside = (there >= 0) & (there < count)

        @pl.when(inside)
        def _():
            place(at, faces[jnp.clip(there, 0, count - 1)])

        @pl.when(jnp.logical_not(inside))
        def _():
            place(at, jnp.zeros(faces.shape[1:], BF))


def extend_kernel(faces, ylo, yhi, low, high):
    low[1:9] = ylo[...]
    high[1:9] = yhi[...]

    def place(at, face):
        low[at] = face[0]
        high[at] = face[3]

    x_halo(faces, place)


def tap_of(far, source, target):
    position = source if far == 0 else (2 if source == 0 else -1)
    tap = position - target
    return tap if -1 <= tap <= 1 else None


def weights_kernel(w1_ref, w2_ref, dw_ref, big1, big1t, big2, big2t, down_mat, rep, tiles, tiles_t):
    lane = iota((32, 128), 1)
    spread = jnp.where((lane & 31) == iota((32, 128), 0), 1.0, 0.0).astype(BF)
    eye = jnp.where(iota((32, 32), 0) == iota((32, 32), 1), 1.0, 0.0).astype(BF)
    group = [jnp.where((lane >> 5) == g, 1.0, 0.0).astype(BF) for g in range(4)]
    for w_ref, big, big_t in ((w1_ref, big1, big1t), (w2_ref, big2, big2t)):
        tiles[...] = dot(w_ref[...], spread).astype(BF)
        w3 = w_ref[...].reshape(27, 32, 32)
        for j in range(4):
            rep[:, j] = w3
        tiles_t[...] = dot(eye, rep[...].reshape(27 * 128, 32), NT).astype(BF)
        for s in range(8):
            sx, sy, sz = s >> 2, (s >> 1) & 1, s & 1
            for e in range(8):
                d, a, b = e >> 2, (e >> 1) & 1, e & 1
                first = s * 256 + e * 32
                for td in range(2):
                    plain = None
                    turned = None
                    for g in range(4):
                        taps = (tap_of(sx, a, g >> 1), tap_of(sy, b, g & 1), tap_of(sz, d, td))
                        if None in taps:
                            continue
                        k = 9 * (taps[0] + 1) + 3 * (taps[1] + 1) + taps[2] + 1
                        back = 26 - k
                        term = tiles[k * 32 : k * 32 + 32, :] * group[g]
                        term_t = tiles_t[:, back * 128 : back * 128 + 128] * group[g]
                        plain = term if plain is None else plain + term
                        turned = term_t if turned is None else turned + term_t
                    zero = jnp.zeros((32, 128), BF)
                    big[first : first + 32, td * 128 : td * 128 + 128] = zero if plain is None else plain
                    big_t[first : first + 32, td * 128 : td * 128 + 128] = zero if turned is None else turned
    column = iota((64, 64), 1)
    order = jnp.where(iota((64, 64), 0) == 2 * (column & 31) + (column >> 5), 1.0, 0.0).astype(BF)
    ordered = dot(dw_ref[...].reshape(256, 64), order).astype(BF)
    for e in range(8):
        k = 4 * ((e >> 1) & 1) + 2 * (e & 1) + (e >> 2)
        down_mat[e * 32 : e * 32 + 32, 0:64] = ordered[k * 32 : k * 32 + 32]
    down_mat[0:256, 64:128] = jnp.zeros((256, 64), BF)
    unit = iota((256, 128), 1) - 64 == (iota((256, 128), 0) >> 5)
    down_mat[256:512, :] = jnp.where(unit, 1.0, 0.0).astype(BF)


def lane_picks():
    lane = iota((16, 512), 1)
    low_a = jnp.where(((lane >> 6) & 1) == 0, 1.0, 0.0).astype(BF) > 0.5
    low_b = jnp.where(((lane >> 5) & 1) == 0, 1.0, 0.0).astype(BF) > 0.5
    return low_a[None], low_b[None]


def put_field(store, x, y0, value):
    ny = value.shape[0]
    z = iota((ny, 16, 128), 1)
    store[x, y0 : y0 + ny, :, 0:256] = value
    up = pltpu.roll(value[:, :, 0:128].astype(F32), 15, 1)
    store[x, y0 : y0 + ny, :, 256:384] = jnp.where(z == 15, 0.0, up).astype(BF)
    dn = pltpu.roll(value[:, :, 128:256].astype(F32), 1, 1)
    store[x, y0 : y0 + ny, :, 384:512] = jnp.where(z == 0, 0.0, dn).astype(BF)


def clear_edges(store):
    store[0] = jnp.zeros((8, 16, 512), BF)
    store[11] = jnp.zeros((8, 16, 512), BF)

    def edge(x, carry):
        store[x, 0] = jnp.zeros((16, 512), BF)
        store[x, 7] = jnp.zeros((16, 512), BF)
        return carry

    lax.fori_loop(1, 11, edge, 0)


def widen(store, wide, x, at, y0, ny, picks):
    low_a, low_b = picks
    low_a = jnp.broadcast_to(low_a, (ny, 16, 512))
    low_b = jnp.broadcast_to(low_b, (ny, 16, 512))

    def at_y(dx, dy):
        return store[x + dx, y0 + dy : y0 + dy + ny]

    wide[at, :, :, 0:512] = at_y(0, 0)
    wide[at, :, :, 512:1024] = jnp.where(low_b, at_y(0, 1), at_y(0, -1))
    wide[at, :, :, 1024:1536] = jnp.where(low_a, at_y(1, 0), at_y(-1, 0))
    upper = jnp.where(low_b, at_y(1, 1), at_y(1, -1))
    lower = jnp.where(low_b, at_y(-1, 1), at_y(-1, -1))
    wide[at, :, :, 1536:2048] = jnp.where(low_a, upper, lower)


def fold_taps(products, terms, first_tap, held):
    lane = iota((32, 128), 1)
    for k in range(27):
        tap = (k // 9 - 1, k // 3 % 3 - 1, k % 3 - 1)
        total = None
        for g in range(4):
            part = None
            for td in range(2):
                far, source, target = [], [], []
                for t, parity in ((tap[0], g >> 1), (tap[1], g & 1)):
                    b = parity if t == 0 else 1 - parity
                    far.append(0 if 0 <= b + t <= 1 else 1)
                    target.append(b)
                pos = td + tap[2]
                far_z = 0 if 0 <= pos <= 1 else 1
                source_d = pos & 1
                s = far[0] * 4 + far[1] * 2 + far_z
                rows = (td * 4 + target[0] * 2 + target[1]) * 32
                cols = s * 256 + source_d * 128
                block = products[rows : rows + 32, cols : cols + 128]
                part = block if part is None else part + block
            total = part if total is None else jnp.where((lane >> 5) == g, part, total)
        total = total + pltpu.roll(total, 64, 1)
        total = total + pltpu.roll(total, 32, 1)
        slot = (first_tap + k) % 4
        held = total if held is None else jnp.where((lane >> 5) == slot, total, held)
        if slot == 3:
            row = (first_tap + k) // 4 * 32
            terms[row : row + 32, :] = held.astype(terms.dtype)
            held = None
    return held


def main_kernel(own, faces, ylo, yhi, big1, big2, big2t, down_mat,
                terms, ef, bk, mk, summed,
                field, ex, eg, eh, ax, ag, ah, turned, products, mixed):
    picks = lane_picks()
    field[1:9, 1:5] = own[...]
    field[:, 0] = ylo[...]
    field[:, 5] = yhi[...]

    def place(at, face):
        field[at, 1:5] = face

    x_halo(faces, place)
    for store in (ex, eg, eh, ef):
        clear_edges(store)

    def start(x, carry):
        row = field[x]
        put_field(ex, x + 1, 1, row[:, :, 0:256])
        both = dot(row[:, :, 256:384].reshape(96, 128), down_mat[...], NT)
        mask = both[:, 256:512]
        bkm = both[:, 0:256] * mask
        mk[x] = mask.astype(BF).reshape(6, 16, 256)
        bk[x] = bkm.reshape(6, 16, 256)
        put_field(eg, x + 1, 1, bkm.astype(BF).reshape(6, 16, 256))
        return carry

    lax.fori_loop(0, 10, start, 0)

    def first(i, carry):
        for j in range(2):
            widen(ex, ax, 2 * i + j + 1, 2 * i + j, 1, 6, picks)
            widen(eg, ag, 2 * i + j + 1, j, 1, 6, picks)
        mask = mk[pl.ds(2 * i, 2)].reshape(192, 256).astype(F32)
        pre = dot(ax[pl.ds(2 * i, 2)].reshape(192, 2048), big1[...]) * mask
        spread = dot(ag[...].reshape(192, 2048), big2t[...])
        s = jax.nn.sigmoid(pre)
        hidden = (pre * s).astype(BF).reshape(2, 6, 16, 256)
        grad = (spread * s * (1.0 + pre * (1.0 - s)) * mask).astype(BF).reshape(2, 6, 16, 256)
        for j in range(2):
            put_field(eh, 2 * i + j + 1, 1, hidden[j])
            put_field(ef, 2 * i + j + 1, 1, grad[j])
        return carry

    lax.fori_loop(0, 5, first, 0)

    def second(i, carry):
        for j in range(4):
            widen(eh, ah, 4 * i + j + 2, 4 * i + j, 2, 4, picks)
        pre = dot(ah[pl.ds(4 * i, 4)].reshape(256, 2048), big2[...])
        mask = mk[pl.ds(4 * i + 1, 4), 1:5].reshape(256, 256).astype(F32)
        inputs = field[pl.ds(4 * i + 1, 4), 1:5, :, 0:256].reshape(256, 256).astype(F32)
        summed[pl.ds(pl.multiple_of(256 * i, 256), 256), :] = (inputs + pre * mask).astype(BF)
        return carry

    lax.fori_loop(0, 2, second, 0)

    held = None
    for source, grads in ((1, ef), (2, eg)):
        turned[...] = grads[2:10, 2:6, :, 0:256].reshape(512, 256).astype(F32).T.astype(BF)
        for s in range(8):
            cols = slice(s * 256, s * 256 + 256)
            wide = (ax[1:9, 1:5, :, cols] if source == 1 else ah[:, :, :, cols]).reshape(512, 256)
            products[0:256, cols] = dot(turned[...], wide)
        held = fold_taps(products, terms, 27 * (source - 1), held)
    terms[416:448, :] = held.astype(terms.dtype)
    cot = field[1:9, 1:5, :, 256:384].reshape(512, 128).astype(F32).T.astype(BF)
    grad_down = dot(cot, summed[...])
    for half in range(2):
        for odd in range(2):
            part = grad_down[odd * 32 : odd * 32 + 32, half * 128 : half * 128 + 128]
            mixed[pl.ds(half * 64 + odd, 32, stride=2), :] = part
    terms[448:576, :] = mixed[...].astype(terms.dtype)
    rest = terms.shape[0] - 576
    if rest:
        terms[576:, :] = jnp.zeros((rest, 128), terms.dtype)


def tail_kernel(cell_ref, ef, bk, mk, summed, big1t, down_mat, grad_features, down, ah, turned, dense, place_mat, shuffle):
    picks = lane_picks()

    def last(i, carry):
        for j in range(4):
            widen(ef, ah, 4 * i + j + 2, j, 2, 4, picks)
        spread = dot(ah[...].reshape(256, 2048), big1t[...])
        rows = pl.ds(4 * i + 1, 4)
        mask = mk[rows, 1:5].reshape(256, 256).astype(F32)
        grad = bk[rows, 1:5].reshape(256, 256) + spread * mask
        dense[pl.ds(pl.multiple_of(256 * i, 256), 256), :] = grad.astype(BF)
        return carry

    lax.fori_loop(0, 2, last, 0)
    place_fine(cell_ref, place_mat)
    turned[...] = dense[...].astype(F32).T.astype(BF)
    pick = jnp.where(octant_rows(), 1.0, 0.0)
    for q in range(4):
        moved = dot(turned[...], place_mat[:, q * 512 : q * 512 + 512])
        total = moved[0:32] * pick[0:1]
        for e in range(1, 8):
            total = total + moved[e * 32 : e * 32 + 32] * pick[e : e + 1]
        grad_features[q] = total.astype(BF)
    lowered = dot(summed[...], down_mat[0:256, :]).T.astype(BF)
    low = iota((32, 128), 1) < 64
    for t in range(2):
        moved = dot(lowered, coarse_tile(cell_ref, t))
        even, odd = moved[0:32], moved[32:64]
        shuffle[:, 2 * t, :] = jnp.where(low, even, pltpu.roll(odd, 64, 1))
        shuffle[:, 2 * t + 1, :] = jnp.where(low, pltpu.roll(even, 64, 1), odd)
    for j in range(32):
        down[:, j * 128 : j * 128 + 128] = shuffle[j, 0:4, :].astype(BF)


def reduce_kernel(parts, out):
    count = parts.shape[0]
    total = parts[0].astype(F32)
    for i in range(1, count):
        total = total + parts[i].astype(F32)
    total = total.astype(out.dtype)
    for i in range(out.shape[0]):
        out[i] = total


def finish_kernel(scale, sums, one, two, down):
    for m in range(14):
        block = (sums[m * 32 : m * 32 + 32, :].astype(F32) * scale).T
        for g in range(4):
            k = 4 * m + g
            if k < 27:
                one[k] = block[g * 32 : g * 32 + 32]
            elif k < 54:
                two[k - 27] = block[g * 32 : g * 32 + 32]
    for half in range(2):
        block = (sums[448 + 64 * half : 512 + 64 * half, :].astype(F32) * scale).T
        for g in range(4):
            down[4 * (g >> 1) + 2 * (g & 1) + half] = block[g * 32 : g * 32 + 32]


def vmem_call(kernel, outs, ins, scratch=(), smem_first=False, flops=0, limit=48):
    specs = [pl.BlockSpec(memory_space=pltpu.VMEM) for _ in ins]
    if smem_first:
        specs[0] = pl.BlockSpec(memory_space=pltpu.SMEM)
    moved = sum(math.prod(x.shape) * x.dtype.itemsize for x in tuple(ins) + tuple(outs))
    return pl.pallas_call(
        kernel,
        out_shape=tuple(outs),
        in_specs=specs,
        out_specs=tuple(pl.BlockSpec(memory_space=pltpu.VMEM) for _ in outs),
        scratch_shapes=list(scratch),
        compiler_params=pltpu.CompilerParams(vmem_limit_bytes=limit * 1024 * 1024),
        cost_estimate=pl.CostEstimate(flops=flops, bytes_accessed=moved, transcendentals=0),
    )(*ins)


def bf(*shape):
    return jax.ShapeDtypeStruct(shape, BF)


def f32(*shape):
    return jax.ShapeDtypeStruct(shape, F32)


def on_device(features, voxel_mask, brick_cell, conv_one, conv_two, down_weight, cotangent):
    regions, tiles = lax.axis_size("region"), lax.axis_size("tile")
    devices = regions * tiles
    slots = features.shape[0]
    own, faces, ylo, yhi = vmem_call(
        gather_kernel,
        [bf(8, 4, 16, 384), bf(regions, 4, 16, 384), bf(8, 16, 384), bf(8, 16, 384)],
        (brick_cell, features, voxel_mask, cotangent),
        [pltpu.VMEM((512, 2304), BF), pltpu.VMEM((384, 2304), BF), pltpu.VMEM((32, 8, 128), F32)],
        smem_first=True,
        flops=2 * 512 * 2304 * 384,
        limit=16,
    )
    faces = lax.all_to_all(faces, "region", 0, 0, tiled=True)
    low, high = vmem_call(extend_kernel, [bf(10, 16, 384), bf(10, 16, 384)], (faces, ylo, yhi), limit=4)
    ups = [(i, i + 1) for i in range(tiles - 1)]
    ylo = lax.ppermute(high, "tile", ups)
    yhi = lax.ppermute(low, "tile", [(j, i) for i, j in ups])
    big1, big1t, big2, big2t, down_mat = vmem_call(
        weights_kernel,
        [bf(2048, 256)] * 4 + [bf(512, 128)],
        (conv_one.reshape(864, 32), conv_two.reshape(864, 32), down_weight),
        [pltpu.VMEM((27, 4, 32, 32), BF), pltpu.VMEM((864, 128), BF), pltpu.VMEM((32, 3456), BF)],
        flops=2 * 2 * 32 * 3456 * 256,
        limit=16,
    )
    chunk = -(-576 // (16 * tiles)) * 16
    terms, ef, bk, mk, summed = vmem_call(
        main_kernel,
        [bf(tiles * chunk, 128), bf(12, 8, 16, 512), f32(10, 6, 16, 256), bf(10, 6, 16, 256), bf(512, 256)],
        (own, faces, ylo, yhi, big1, big2, big2t, down_mat),
        [
            pltpu.VMEM((10, 6, 16, 384), BF),
            pltpu.VMEM((12, 8, 16, 512), BF),
            pltpu.VMEM((12, 8, 16, 512), BF),
            pltpu.VMEM((12, 8, 16, 512), BF),
            pltpu.VMEM((10, 6, 16, 2048), BF),
            pltpu.VMEM((2, 6, 16, 2048), BF),
            pltpu.VMEM((8, 4, 16, 2048), BF),
            pltpu.VMEM((256, 512), BF),
            pltpu.VMEM((256, 2048), F32),
            pltpu.VMEM((128, 128), F32),
        ],
        flops=2 * 2048 * 256 * (960 * 2 + 512 * 3),
        limit=32,
    )
    parts = lax.all_to_all(terms.reshape(tiles, chunk, 128), "tile", 0, 0, tiled=True)
    (total,) = vmem_call(reduce_kernel, [f32(regions, chunk, 128)], (parts,), limit=4)
    parts = lax.all_to_all(total, "region", 0, 0, tiled=True)
    (total,) = vmem_call(reduce_kernel, [bf(tiles, chunk, 128)], (parts,), limit=4)
    sums = lax.all_to_all(total, "tile", 0, 0, tiled=True)
    grad_features, down = vmem_call(
        tail_kernel,
        [bf(slots, 32, 512), bf(slots, 4096)],
        (brick_cell, ef, bk, mk, summed, big1t, down_mat),
        [
            pltpu.VMEM((4, 4, 16, 2048), BF),
            pltpu.VMEM((256, 512), BF),
            pltpu.VMEM((512, 256), BF),
            pltpu.VMEM((512, 2048), BF),
            pltpu.VMEM((32, 8, 128), F32),
        ],
        smem_first=True,
        flops=2 * 2048 * 512 * 512,
        limit=16,
    )
    scale = 1.0 / math.sqrt(devices * slots * 512.0)
    grad_one, grad_two, grad_down = vmem_call(
        functools.partial(finish_kernel, scale),
        [f32(27, 32, 32), f32(27, 32, 32), f32(8, 32, 64)],
        (sums.reshape(tiles * chunk, 128),),
        limit=8,
    )
    return down, grad_features, grad_one, grad_two, grad_down


def solution(mesh):
    in_specs = (
        P(AXES, None, None),
        P(AXES, None),
        P(AXES),
        P(),
        P(),
        P(),
        P(AXES, None),
    )
    out_specs = (P(AXES, None), P(AXES, None, None), P(), P(), P())
    return jax.shard_map(
        on_device, mesh=mesh, in_specs=in_specs, out_specs=out_specs, check_vma=False
    )
```

```python
import functools
import math

import jax
import jax.numpy as jnp
from jax import lax
from jax.experimental import pallas as pl
from jax.experimental.pallas import tpu as pltpu
from jax.sharding import PartitionSpec as P


BF = jnp.bfloat16
F32 = jnp.float32
I32 = jnp.int32
NN = (((1,), (0,)), ((), ()))
NT = (((1,), (1,)), ((), ()))
AXES = ("region", "tile")


def dot(lhs, rhs, dims=NN):
    return lax.dot_general(lhs, rhs, dims, preferred_element_type=F32)


def iota(shape, dim):
    return lax.broadcasted_iota(I32, shape, dim)


def parity_fields(v):
    return v & 1, (v >> 6) & 1, (v >> 3) & 1


def octant_rows(first=0):
    e = iota((8, 512), 0)
    d, a, b = parity_fields(iota((8, 512), 1))
    return (d == (e >> 2)) & (a == ((e >> 1) & 1)) & (b == (e & 1))


def row_codes():
    row = iota((512, 128), 0)
    code = ((row >> 6) & 3) * 16 + ((row >> 4) & 3) * 4 + (row & 3)
    cell = (row >> 8) * 4 + ((row >> 2) & 3)
    return code, cell


def place_fine(cell_ref, place):
    code, cell = row_codes()
    for q in range(4):
        code_q = jnp.where(cell == cell_ref[q], code, -1)
        for t in range(4):
            v = iota((1, 128), 1) + 128 * t
            vcode = (v >> 7) * 16 + ((v >> 4) & 3) * 4 + ((v >> 1) & 3)
            first = q * 512 + t * 128
            place[:, first : first + 128] = jnp.where(code_q == vcode, 1.0, 0.0).astype(BF)


def coarse_tile(cell_ref, t):
    code, cell = row_codes()
    lane = iota((512, 128), 1)
    wanted = jnp.where(lane < 64, cell_ref[2 * t], cell_ref[2 * t + 1])
    return jnp.where((cell == wanted) & (code == (lane & 63)), 1.0, 0.0).astype(BF)


def gather_kernel(cell_hbm, feat_hbm, vmask_hbm, cot_hbm, own, faces, ylo, yhi,
                  lhs, rhs, shuffle, cell_ref, feat_ref, vmask_ref, cot_ref, sems):
    moves = [
        pltpu.make_async_copy(source, target, sems.at[i])
        for i, (source, target) in enumerate(
            ((cell_hbm, cell_ref), (vmask_hbm, vmask_ref), (feat_hbm, feat_ref), (cot_hbm, cot_ref))
        )
    ]
    for move in moves:
        move.start()
    moves[0].wait()
    place_fine(cell_ref, lhs)
    for t in range(2):
        lhs[:, 2048 + t * 128 : 2048 + t * 128 + 128] = coarse_tile(cell_ref, t)
    for move in moves[1:]:
        move.wait()
    match = octant_rows()
    for q in range(4):
        cols = slice(q * 512, q * 512 + 512)
        m8 = jnp.where(match, vmask_ref[q : q + 1, :].astype(F32), 0.0)
        x = feat_ref[q].astype(F32)
        for e in range(8):
            rhs[e * 32 : e * 32 + 32, cols] = (x * m8[e : e + 1, :]).astype(BF)
        rhs[256:320, cols] = jnp.zeros((64, 512), BF)
        rhs[320:336, cols] = jnp.concatenate([m8, jnp.zeros((8, 512), F32)], axis=0).astype(BF)
        rhs[336:384, cols] = jnp.zeros((48, 512), BF)
    rhs[0:256, 2048:2304] = jnp.zeros((256, 256), BF)
    for j in range(32):
        shuffle[j, 0:4, :] = cot_ref[:, j * 128 : j * 128 + 128].astype(F32)
    low = iota((32, 128), 1) < 64
    for t in range(2):
        first, second = shuffle[:, 2 * t, :], shuffle[:, 2 * t + 1, :]
        cols = slice(2048 + t * 128, 2176 + t * 128)
        rhs[256:288, cols] = jnp.where(low, first, pltpu.roll(second, 64, 1)).astype(BF)
        rhs[288:320, cols] = jnp.where(low, pltpu.roll(first, 64, 1), second).astype(BF)
    rhs[320:384, 2048:2304] = jnp.zeros((64, 256), BF)
    field = dot(lhs[...], rhs[...], NT).astype(BF).reshape(8, 4, 16, 384)
    own[...] = field
    ylo[...] = field[:, 0]
    yhi[...] = field[:, 3]
    here = lax.axis_index("region")
    for p in range(faces.shape[0]):
        faces[p] = own[jnp.where(p < here, 0, 7)]


def x_halo(faces, place):
    here = lax.axis_index("region")
    count = faces.shape[0]
    for at, there in ((0, here - 1), (9, here + 1)):
        inside = (there >= 0) & (there < count)

        @pl.when(inside)
        def _():
            place(at, faces[jnp.clip(there, 0, count - 1)])

        @pl.when(jnp.logical_not(inside))
        def _():
            place(at, jnp.zeros(faces.shape[1:], BF))


def extend_kernel(faces, ylo, yhi, low, high):
    low[1:9] = ylo[...]
    high[1:9] = yhi[...]

    def place(at, face):
        low[at] = face[0]
        high[at] = face[3]

    x_halo(faces, place)


def tap_of(far, source, target):
    position = source if far == 0 else (2 if source == 0 else -1)
    tap = position - target
    return tap if -1 <= tap <= 1 else None


def weights_kernel(w1_ref, w2_ref, dw_ref, big1, big1t, big2, big2t, down_mat, rep, tiles, tiles_t):
    lane = iota((32, 128), 1)
    spread = jnp.where((lane & 31) == iota((32, 128), 0), 1.0, 0.0).astype(BF)
    eye = jnp.where(iota((32, 32), 0) == iota((32, 32), 1), 1.0, 0.0).astype(BF)
    group = [jnp.where((lane >> 5) == g, 1.0, 0.0).astype(BF) for g in range(4)]
    for w_ref, big, big_t in ((w1_ref, big1, big1t), (w2_ref, big2, big2t)):
        tiles[...] = dot(w_ref[...], spread).astype(BF)
        w3 = w_ref[...].reshape(27, 32, 32)
        for j in range(4):
            rep[:, j] = w3
        tiles_t[...] = dot(eye, rep[...].reshape(27 * 128, 32), NT).astype(BF)
        for s in range(8):
            sx, sy, sz = s >> 2, (s >> 1) & 1, s & 1
            for e in range(8):
                d, a, b = e >> 2, (e >> 1) & 1, e & 1
                first = s * 256 + e * 32
                for td in range(2):
                    plain = None
                    turned = None
                    for g in range(4):
                        taps = (tap_of(sx, a, g >> 1), tap_of(sy, b, g & 1), tap_of(sz, d, td))
                        if None in taps:
                            continue
                        k = 9 * (taps[0] + 1) + 3 * (taps[1] + 1) + taps[2] + 1
                        back = 26 - k
                        term = tiles[k * 32 : k * 32 + 32, :] * group[g]
                        term_t = tiles_t[:, back * 128 : back * 128 + 128] * group[g]
                        plain = term if plain is None else plain + term
                        turned = term_t if turned is None else turned + term_t
                    zero = jnp.zeros((32, 128), BF)
                    big[first : first + 32, td * 128 : td * 128 + 128] = zero if plain is None else plain
                    big_t[first : first + 32, td * 128 : td * 128 + 128] = zero if turned is None else turned
    column = iota((64, 64), 1)
    order = jnp.where(iota((64, 64), 0) == 2 * (column & 31) + (column >> 5), 1.0, 0.0).astype(BF)
    ordered = dot(dw_ref[...].reshape(256, 64), order).astype(BF)
    for e in range(8):
        k = 4 * ((e >> 1) & 1) + 2 * (e & 1) + (e >> 2)
        down_mat[e * 32 : e * 32 + 32, 0:64] = ordered[k * 32 : k * 32 + 32]
    down_mat[0:256, 64:128] = jnp.zeros((256, 64), BF)
    unit = iota((256, 128), 1) - 64 == (iota((256, 128), 0) >> 5)
    down_mat[256:512, :] = jnp.where(unit, 1.0, 0.0).astype(BF)


def lane_picks():
    lane = iota((16, 512), 1)
    low_a = jnp.where(((lane >> 6) & 1) == 0, 1.0, 0.0).astype(BF) > 0.5
    low_b = jnp.where(((lane >> 5) & 1) == 0, 1.0, 0.0).astype(BF) > 0.5
    return low_a[None], low_b[None]


def put_field(store, x, y0, value):
    ny = value.shape[0]
    z = iota((ny, 16, 128), 1)
    store[x, y0 : y0 + ny, :, 0:256] = value
    up = pltpu.roll(value[:, :, 0:128].astype(F32), 15, 1)
    store[x, y0 : y0 + ny, :, 256:384] = jnp.where(z == 15, 0.0, up).astype(BF)
    dn = pltpu.roll(value[:, :, 128:256].astype(F32), 1, 1)
    store[x, y0 : y0 + ny, :, 384:512] = jnp.where(z == 0, 0.0, dn).astype(BF)


def clear_edges(store):
    store[0] = jnp.zeros((8, 16, 512), BF)
    store[11] = jnp.zeros((8, 16, 512), BF)

    def edge(x, carry):
        store[x, 0] = jnp.zeros((16, 512), BF)
        store[x, 7] = jnp.zeros((16, 512), BF)
        return carry

    lax.fori_loop(1, 11, edge, 0)


def widen(store, wide, x, at, y0, ny, picks):
    low_a, low_b = picks
    low_a = jnp.broadcast_to(low_a, (ny, 16, 512))
    low_b = jnp.broadcast_to(low_b, (ny, 16, 512))

    def at_y(dx, dy):
        return store[x + dx, y0 + dy : y0 + dy + ny]

    wide[at, :, :, 0:512] = at_y(0, 0)
    wide[at, :, :, 512:1024] = jnp.where(low_b, at_y(0, 1), at_y(0, -1))
    wide[at, :, :, 1024:1536] = jnp.where(low_a, at_y(1, 0), at_y(-1, 0))
    upper = jnp.where(low_b, at_y(1, 1), at_y(1, -1))
    lower = jnp.where(low_b, at_y(-1, 1), at_y(-1, -1))
    wide[at, :, :, 1536:2048] = jnp.where(low_a, upper, lower)


def fold_taps(products, terms, first_tap, held):
    lane = iota((32, 128), 1)
    for k in range(27):
        tap = (k // 9 - 1, k // 3 % 3 - 1, k % 3 - 1)
        total = None
        for g in range(4):
            part = None
            for td in range(2):
                far, source, target = [], [], []
                for t, parity in ((tap[0], g >> 1), (tap[1], g & 1)):
                    b = parity if t == 0 else 1 - parity
                    far.append(0 if 0 <= b + t <= 1 else 1)
                    target.append(b)
                pos = td + tap[2]
                far_z = 0 if 0 <= pos <= 1 else 1
                source_d = pos & 1
                s = far[0] * 4 + far[1] * 2 + far_z
                rows = (td * 4 + target[0] * 2 + target[1]) * 32
                cols = s * 256 + source_d * 128
                block = products[rows : rows + 32, cols : cols + 128]
                part = block if part is None else part + block
            total = part if total is None else jnp.where((lane >> 5) == g, part, total)
        total = total + pltpu.roll(total, 64, 1)
        total = total + pltpu.roll(total, 32, 1)
        slot = (first_tap + k) % 4
        held = total if held is None else jnp.where((lane >> 5) == slot, total, held)
        if slot == 3:
            row = (first_tap + k) // 4 * 32
            terms[row : row + 32, :] = held.astype(terms.dtype)
            held = None
    return held


def main_kernel(own, faces, ylo, yhi, big1, big2, big2t, down_mat,
                terms, ef, summed,
                field, ex, eg, eh, mk, ax, ag, ah, turned, products, mixed):
    picks = lane_picks()
    field[1:9, 1:5] = own[...]
    field[:, 0] = ylo[...]
    field[:, 5] = yhi[...]

    def place(at, face):
        field[at, 1:5] = face

    x_halo(faces, place)
    for store in (ex, eg, eh, ef):
        clear_edges(store)

    for x in range(0, 10, 2):
        rows = field[x : x + 2]
        both = dot(rows[:, :, :, 256:384].reshape(192, 128), down_mat[...], NT)
        mask = both[:, 256:512]
        mk[x : x + 2] = mask.astype(BF).reshape(2, 6, 16, 256)
        grad = (both[:, 0:256] * mask).astype(BF).reshape(2, 6, 16, 256)
        for j in range(2):
            put_field(ex, x + j + 1, 1, rows[j, :, :, 0:256])
            put_field(eg, x + j + 1, 1, grad[j])
    for x in range(0, 10, 2):
        for j in range(2):
            widen(ex, ax, x + j + 1, x + j, 1, 6, picks)
            widen(eg, ag, x + j + 1, x + j, 1, 6, picks)
        mask = mk[x : x + 2].reshape(192, 256).astype(F32)
        pre = dot(ax[x : x + 2].reshape(192, 2048), big1[...]) * mask
        spread = dot(ag[x : x + 2].reshape(192, 2048), big2t[...])
        s = jax.nn.sigmoid(pre)
        hidden = (pre * s).astype(BF).reshape(2, 6, 16, 256)
        grad = (spread * s * (1.0 + pre * (1.0 - s)) * mask).astype(BF).reshape(2, 6, 16, 256)
        for j in range(2):
            put_field(eh, x + j + 1, 1, hidden[j])
            put_field(ef, x + j + 1, 1, grad[j])
    for x in range(0, 8, 4):
        for j in range(4):
            widen(eh, ah, x + j + 2, x + j, 2, 4, picks)
        pre = dot(ah[x : x + 4].reshape(256, 2048), big2[...])
        mask = mk[x + 1 : x + 5, 1:5].reshape(256, 256).astype(F32)
        inputs = field[x + 1 : x + 5, 1:5, :, 0:256].reshape(256, 256).astype(F32)
        summed[x * 64 : x * 64 + 256, :] = (inputs + pre * mask).astype(BF)

    held = None
    for source, grads in ((1, ef), (2, eg)):
        turned[...] = grads[2:10, 2:6, :, 0:256].reshape(512, 256).astype(F32).T.astype(BF)
        for s in range(8):
            cols = slice(s * 256, s * 256 + 256)
            wide = (ax[1:9, 1:5, :, cols] if source == 1 else ah[:, :, :, cols]).reshape(512, 256)
            products[0:256, cols] = dot(turned[...], wide)
        held = fold_taps(products, terms, 27 * (source - 1), held)
    terms[416:448, :] = held.astype(terms.dtype)
    cot = field[1:9, 1:5, :, 256:384].reshape(512, 128).astype(F32).T.astype(BF)
    grad_down = dot(cot, summed[...])
    for half in range(2):
        for odd in range(2):
            part = grad_down[odd * 32 : odd * 32 + 32, half * 128 : half * 128 + 128]
            mixed[pl.ds(half * 64 + odd, 32, stride=2), :] = part
    terms[448:576, :] = mixed[...].astype(terms.dtype)
    rest = terms.shape[0] - 576
    if rest:
        terms[576:, :] = jnp.zeros((rest, 128), terms.dtype)


def tail_kernel(cell_ref, own, ef, summed, big1t, down_mat, grad_features, down, ah, turned, dense, place_mat, shuffle):
    picks = lane_picks()

    for x in range(0, 8, 4):
        for j in range(4):
            widen(ef, ah, x + j + 2, x + j, 2, 4, picks)
        spread = dot(ah[x : x + 4].reshape(256, 2048), big1t[...])
        both = dot(own[x : x + 4, :, :, 256:384].reshape(256, 128), down_mat[...], NT)
        grad = (both[:, 0:256] + spread) * both[:, 256:512]
        dense[x * 64 : x * 64 + 256, :] = grad.astype(BF)
    place_fine(cell_ref, place_mat)
    turned[...] = dense[...].astype(F32).T.astype(BF)
    pick = jnp.where(octant_rows(), 1.0, 0.0)
    for q in range(4):
        moved = dot(turned[...], place_mat[:, q * 512 : q * 512 + 512])
        total = moved[0:32] * pick[0:1]
        for e in range(1, 8):
            total = total + moved[e * 32 : e * 32 + 32] * pick[e : e + 1]
        grad_features[q] = total.astype(BF)
    lowered = dot(summed[...], down_mat[0:256, :]).T.astype(BF)
    low = iota((32, 128), 1) < 64
    for t in range(2):
        moved = dot(lowered, coarse_tile(cell_ref, t))
        even, odd = moved[0:32], moved[32:64]
        shuffle[:, 2 * t, :] = jnp.where(low, even, pltpu.roll(odd, 64, 1))
        shuffle[:, 2 * t + 1, :] = jnp.where(low, pltpu.roll(even, 64, 1), odd)
    for j in range(32):
        down[:, j * 128 : j * 128 + 128] = shuffle[j, 0:4, :].astype(BF)


def reduce_kernel(parts, out):
    count = parts.shape[0]
    total = parts[0].astype(F32)
    for i in range(1, count):
        total = total + parts[i].astype(F32)
    total = total.astype(out.dtype)
    for i in range(out.shape[0]):
        out[i] = total


def finish_kernel(scale, sums, one, two, down):
    for m in range(14):
        block = (sums[m * 32 : m * 32 + 32, :].astype(F32) * scale).T
        for g in range(4):
            k = 4 * m + g
            if k < 27:
                one[k] = block[g * 32 : g * 32 + 32]
            elif k < 54:
                two[k - 27] = block[g * 32 : g * 32 + 32]
    for half in range(2):
        block = (sums[448 + 64 * half : 512 + 64 * half, :].astype(F32) * scale).T
        for g in range(4):
            down[4 * (g >> 1) + 2 * (g & 1) + half] = block[g * 32 : g * 32 + 32]


def vmem_call(kernel, outs, ins, scratch=(), smem_first=False, flops=0, limit=48, in_space=pltpu.VMEM):
    specs = [pl.BlockSpec(memory_space=in_space) for _ in ins]
    if smem_first:
        specs[0] = pl.BlockSpec(memory_space=pltpu.SMEM)
    moved = sum(math.prod(x.shape) * x.dtype.itemsize for x in tuple(ins) + tuple(outs))
    return pl.pallas_call(
        kernel,
        out_shape=tuple(outs),
        in_specs=specs,
        out_specs=tuple(pl.BlockSpec(memory_space=pltpu.VMEM) for _ in outs),
        scratch_shapes=list(scratch),
        compiler_params=pltpu.CompilerParams(vmem_limit_bytes=limit * 1024 * 1024),
        cost_estimate=pl.CostEstimate(flops=flops, bytes_accessed=moved, transcendentals=0),
    )(*ins)


def bf(*shape):
    return jax.ShapeDtypeStruct(shape, BF)


def f32(*shape):
    return jax.ShapeDtypeStruct(shape, F32)


def on_device(features, voxel_mask, brick_cell, conv_one, conv_two, down_weight, cotangent):
    regions, tiles = lax.axis_size("region"), lax.axis_size("tile")
    devices = regions * tiles
    slots = features.shape[0]
    own, faces, ylo, yhi = vmem_call(
        gather_kernel,
        [bf(8, 4, 16, 384), bf(regions, 4, 16, 384), bf(8, 16, 384), bf(8, 16, 384)],
        (brick_cell, features, voxel_mask, cotangent),
        [pltpu.VMEM((512, 2304), BF), pltpu.VMEM((384, 2304), BF), pltpu.VMEM((32, 8, 128), F32),
         pltpu.SMEM(brick_cell.shape, I32), pltpu.VMEM(features.shape, BF), pltpu.VMEM(voxel_mask.shape, I32),
         pltpu.VMEM(cotangent.shape, BF), pltpu.SemaphoreType.DMA((4,))],
        in_space=pltpu.HBM,
        flops=2 * 512 * 2304 * 384,
        limit=16,
    )
    faces = lax.all_to_all(faces, "region", 0, 0, tiled=True)
    low, high = vmem_call(extend_kernel, [bf(10, 16, 384), bf(10, 16, 384)], (faces, ylo, yhi), limit=4)
    ups = [(i, i + 1) for i in range(tiles - 1)]
    ylo = lax.ppermute(high, "tile", ups)
    yhi = lax.ppermute(low, "tile", [(j, i) for i, j in ups])
    big1, big1t, big2, big2t, down_mat = vmem_call(
        weights_kernel,
        [bf(2048, 256)] * 4 + [bf(512, 128)],
        (conv_one.reshape(864, 32), conv_two.reshape(864, 32), down_weight),
        [pltpu.VMEM((27, 4, 32, 32), BF), pltpu.VMEM((864, 128), BF), pltpu.VMEM((32, 3456), BF)],
        flops=2 * 2 * 32 * 3456 * 256,
        limit=16,
    )
    chunk = -(-576 // (8 * tiles)) * 8
    terms, ef, summed = vmem_call(
        main_kernel,
        [bf(tiles * chunk, 128), bf(12, 8, 16, 512), bf(512, 256)],
        (own, faces, ylo, yhi, big1, big2, big2t, down_mat),
        [
            pltpu.VMEM((10, 6, 16, 384), BF),
            pltpu.VMEM((12, 8, 16, 512), BF),
            pltpu.VMEM((12, 8, 16, 512), BF),
            pltpu.VMEM((12, 8, 16, 512), BF),
            pltpu.VMEM((10, 6, 16, 256), BF),
            pltpu.VMEM((10, 6, 16, 2048), BF),
            pltpu.VMEM((10, 6, 16, 2048), BF),
            pltpu.VMEM((8, 4, 16, 2048), BF),
            pltpu.VMEM((256, 512), BF),
            pltpu.VMEM((256, 2048), F32),
            pltpu.VMEM((128, 128), F32),
        ],
        flops=2 * 2048 * 256 * (960 * 2 + 512 * 3),
        limit=32,
    )
    parts = lax.all_to_all(terms.reshape(tiles, chunk, 128), "tile", 0, 0, tiled=True)
    (total,) = vmem_call(reduce_kernel, [f32(regions, chunk, 128)], (parts,), limit=4)
    parts = lax.all_to_all(total, "region", 0, 0, tiled=True)
    (total,) = vmem_call(reduce_kernel, [bf(tiles, chunk, 128)], (parts,), limit=4)
    sums = lax.all_to_all(total, "tile", 0, 0, tiled=True)
    grad_features, down = vmem_call(
        tail_kernel,
        [bf(slots, 32, 512), bf(slots, 4096)],
        (brick_cell, own, ef, summed, big1t, down_mat),
        [
            pltpu.VMEM((8, 4, 16, 2048), BF),
            pltpu.VMEM((256, 512), BF),
            pltpu.VMEM((512, 256), BF),
            pltpu.VMEM((512, 2048), BF),
            pltpu.VMEM((32, 8, 128), F32),
        ],
        smem_first=True,
        flops=2 * 2048 * 512 * 512,
        limit=16,
    )
    scale = 1.0 / math.sqrt(devices * slots * 512.0)
    grad_one, grad_two, grad_down = vmem_call(
        functools.partial(finish_kernel, scale),
        [f32(27, 32, 32), f32(27, 32, 32), f32(8, 32, 64)],
        (sums.reshape(tiles * chunk, 128),),
        limit=8,
    )
    return down, grad_features, grad_one, grad_two, grad_down


def solution(mesh):
    in_specs = (
        P(AXES, None, None),
        P(AXES, None),
        P(AXES),
        P(),
        P(),
        P(),
        P(AXES, None),
    )
    out_specs = (P(AXES, None), P(AXES, None, None), P(), P(), P())
    return jax.shard_map(
        on_device, mesh=mesh, in_specs=in_specs, out_specs=out_specs, check_vma=False
    )
```

```python
import functools
import math

import jax
import jax.numpy as jnp
from jax import lax
from jax.experimental import pallas as pl
from jax.experimental.pallas import tpu as pltpu
from jax.sharding import PartitionSpec as P


BF = jnp.bfloat16
F32 = jnp.float32
I32 = jnp.int32
NN = (((1,), (0,)), ((), ()))
NT = (((1,), (1,)), ((), ()))
AXES = ("region", "tile")


def dot(lhs, rhs, dims=NN):
    return lax.dot_general(lhs, rhs, dims, preferred_element_type=F32)


def iota(shape, dim):
    return lax.broadcasted_iota(I32, shape, dim)


def parity_fields(v):
    return v & 1, (v >> 6) & 1, (v >> 3) & 1


def octant_rows(first=0):
    e = iota((8, 512), 0)
    d, a, b = parity_fields(iota((8, 512), 1))
    return (d == (e >> 2)) & (a == ((e >> 1) & 1)) & (b == (e & 1))


def row_codes():
    row = iota((512, 128), 0)
    code = ((row >> 6) & 3) * 16 + ((row >> 4) & 3) * 4 + (row & 3)
    cell = (row >> 8) * 4 + ((row >> 2) & 3)
    return code, cell


def place_fine(cell_ref, place):
    code, cell = row_codes()
    for q in range(4):
        code_q = jnp.where(cell == cell_ref[q], code, -1)
        for t in range(4):
            v = iota((1, 128), 1) + 128 * t
            vcode = (v >> 7) * 16 + ((v >> 4) & 3) * 4 + ((v >> 1) & 3)
            first = q * 512 + t * 128
            place[:, first : first + 128] = jnp.where(code_q == vcode, 1.0, 0.0).astype(BF)


def coarse_tile(cell_ref, t):
    code, cell = row_codes()
    lane = iota((512, 128), 1)
    wanted = jnp.where(lane < 64, cell_ref[2 * t], cell_ref[2 * t + 1])
    return jnp.where((cell == wanted) & (code == (lane & 63)), 1.0, 0.0).astype(BF)


def gather_kernel(cell_hbm, feat_hbm, vmask_hbm, cot_hbm, own, faces,
                  lhs, rhs, shuffle, cell_ref, feat_ref, vmask_ref, cot_ref, sems):
    moves = [
        pltpu.make_async_copy(source, target, sems.at[i])
        for i, (source, target) in enumerate(
            ((cell_hbm, cell_ref), (vmask_hbm, vmask_ref), (feat_hbm, feat_ref), (cot_hbm, cot_ref))
        )
    ]
    for move in moves:
        move.start()
    moves[0].wait()
    place_fine(cell_ref, lhs)
    for t in range(2):
        lhs[:, 2048 + t * 128 : 2048 + t * 128 + 128] = coarse_tile(cell_ref, t)
    for move in moves[1:]:
        move.wait()
    match = octant_rows()
    for q in range(4):
        cols = slice(q * 512, q * 512 + 512)
        m8 = jnp.where(match, vmask_ref[q : q + 1, :].astype(F32), 0.0)
        x = feat_ref[q].astype(F32)
        for e in range(8):
            rhs[e * 32 : e * 32 + 32, cols] = (x * m8[e : e + 1, :]).astype(BF)
        rhs[256:320, cols] = jnp.zeros((64, 512), BF)
        rhs[320:336, cols] = jnp.concatenate([m8, jnp.zeros((8, 512), F32)], axis=0).astype(BF)
        rhs[336:384, cols] = jnp.zeros((48, 512), BF)
    rhs[0:256, 2048:2304] = jnp.zeros((256, 256), BF)
    for j in range(32):
        shuffle[j, 0:4, :] = cot_ref[:, j * 128 : j * 128 + 128].astype(F32)
    low = iota((32, 128), 1) < 64
    for t in range(2):
        first, second = shuffle[:, 2 * t, :], shuffle[:, 2 * t + 1, :]
        cols = slice(2048 + t * 128, 2176 + t * 128)
        rhs[256:288, cols] = jnp.where(low, first, pltpu.roll(second, 64, 1)).astype(BF)
        rhs[288:320, cols] = jnp.where(low, pltpu.roll(first, 64, 1), second).astype(BF)
    rhs[320:384, 2048:2304] = jnp.zeros((64, 256), BF)
    field = dot(lhs[...], rhs[...], NT).astype(BF).reshape(8, 4, 16, 384)
    own[...] = field
    here = lax.axis_index("region")
    for p in range(faces.shape[0]):
        faces[p] = own[jnp.where(p < here, 0, 7)]


def x_halo(faces, place):
    here = lax.axis_index("region")
    count = faces.shape[0]
    for at, there in ((0, here - 1), (9, here + 1)):
        inside = (there >= 0) & (there < count)

        @pl.when(inside)
        def _():
            place(at, faces[jnp.clip(there, 0, count - 1)])

        @pl.when(jnp.logical_not(inside))
        def _():
            place(at, jnp.zeros(faces.shape[1:], BF))


def extend_kernel(own, faces, far, near):
    odd = lax.rem(lax.axis_index("tile"), 2)

    def fill(low, high):
        low[1:9] = own[:, 0]
        high[1:9] = own[:, 3]

        def place(at, face):
            low[at] = face[0]
            high[at] = face[3]

        x_halo(faces, place)

    pl.when(odd == 1)(lambda: fill(near, far))
    pl.when(odd == 0)(lambda: fill(far, near))


def tap_of(far, source, target):
    position = source if far == 0 else (2 if source == 0 else -1)
    tap = position - target
    return tap if -1 <= tap <= 1 else None


def weights_kernel(w1_ref, w2_ref, dw_ref, big1, big1t, big2, big2t, down_mat, rep, tiles, tiles_t):
    lane = iota((32, 128), 1)
    spread = jnp.where((lane & 31) == iota((32, 128), 0), 1.0, 0.0).astype(BF)
    eye = jnp.where(iota((32, 32), 0) == iota((32, 32), 1), 1.0, 0.0).astype(BF)
    group = [jnp.where((lane >> 5) == g, 1.0, 0.0).astype(BF) for g in range(4)]
    for w_ref, big, big_t in ((w1_ref, big1, big1t), (w2_ref, big2, big2t)):
        tiles[...] = dot(w_ref[...], spread).astype(BF)
        w3 = w_ref[...].reshape(27, 32, 32)
        for j in range(4):
            rep[:, j] = w3
        tiles_t[...] = dot(eye, rep[...].reshape(27 * 128, 32), NT).astype(BF)
        for s in range(8):
            sx, sy, sz = s >> 2, (s >> 1) & 1, s & 1
            for e in range(8):
                d, a, b = e >> 2, (e >> 1) & 1, e & 1
                first = s * 256 + e * 32
                for td in range(2):
                    plain = None
                    turned = None
                    for g in range(4):
                        taps = (tap_of(sx, a, g >> 1), tap_of(sy, b, g & 1), tap_of(sz, d, td))
                        if None in taps:
                            continue
                        k = 9 * (taps[0] + 1) + 3 * (taps[1] + 1) + taps[2] + 1
                        back = 26 - k
                        term = tiles[k * 32 : k * 32 + 32, :] * group[g]
                        term_t = tiles_t[:, back * 128 : back * 128 + 128] * group[g]
                        plain = term if plain is None else plain + term
                        turned = term_t if turned is None else turned + term_t
                    zero = jnp.zeros((32, 128), BF)
                    big[first : first + 32, td * 128 : td * 128 + 128] = zero if plain is None else plain
                    big_t[first : first + 32, td * 128 : td * 128 + 128] = zero if turned is None else turned
    column = iota((64, 64), 1)
    order = jnp.where(iota((64, 64), 0) == 2 * (column & 31) + (column >> 5), 1.0, 0.0).astype(BF)
    ordered = dot(dw_ref[...].reshape(256, 64), order).astype(BF)
    for e in range(8):
        k = 4 * ((e >> 1) & 1) + 2 * (e & 1) + (e >> 2)
        down_mat[e * 32 : e * 32 + 32, 0:64] = ordered[k * 32 : k * 32 + 32]
    down_mat[0:256, 64:128] = jnp.zeros((256, 64), BF)
    unit = iota((256, 128), 1) - 64 == (iota((256, 128), 0) >> 5)
    down_mat[256:512, :] = jnp.where(unit, 1.0, 0.0).astype(BF)


def lane_picks():
    lane = iota((16, 512), 1)
    low_a = jnp.where(((lane >> 6) & 1) == 0, 1.0, 0.0).astype(BF) > 0.5
    low_b = jnp.where(((lane >> 5) & 1) == 0, 1.0, 0.0).astype(BF) > 0.5
    return low_a[None], low_b[None]


def put_field(store, x, y0, value):
    ny = value.shape[0]
    z = iota((ny, 16, 128), 1)
    store[x, y0 : y0 + ny, :, 0:256] = value
    up = pltpu.roll(value[:, :, 0:128].astype(F32), 15, 1)
    store[x, y0 : y0 + ny, :, 256:384] = jnp.where(z == 15, 0.0, up).astype(BF)
    dn = pltpu.roll(value[:, :, 128:256].astype(F32), 1, 1)
    store[x, y0 : y0 + ny, :, 384:512] = jnp.where(z == 0, 0.0, dn).astype(BF)


def clear_edges(store):
    store[0] = jnp.zeros((8, 16, 512), BF)
    store[11] = jnp.zeros((8, 16, 512), BF)

    def edge(x, carry):
        store[x, 0] = jnp.zeros((16, 512), BF)
        store[x, 7] = jnp.zeros((16, 512), BF)
        return carry

    lax.fori_loop(1, 11, edge, 0)


def widen(store, wide, x, at, y0, ny, picks):
    low_a, low_b = picks
    low_a = jnp.broadcast_to(low_a, (ny, 16, 512))
    low_b = jnp.broadcast_to(low_b, (ny, 16, 512))

    def at_y(dx, dy):
        return store[x + dx, y0 + dy : y0 + dy + ny]

    wide[at, :, :, 0:512] = at_y(0, 0)
    wide[at, :, :, 512:1024] = jnp.where(low_b, at_y(0, 1), at_y(0, -1))
    wide[at, :, :, 1024:1536] = jnp.where(low_a, at_y(1, 0), at_y(-1, 0))
    upper = jnp.where(low_b, at_y(1, 1), at_y(1, -1))
    lower = jnp.where(low_b, at_y(-1, 1), at_y(-1, -1))
    wide[at, :, :, 1536:2048] = jnp.where(low_a, upper, lower)


def fold_taps(products, terms, first_tap, held):
    lane = iota((32, 128), 1)
    for k in range(27):
        tap = (k // 9 - 1, k // 3 % 3 - 1, k % 3 - 1)
        total = None
        for g in range(4):
            part = None
            for td in range(2):
                far, source, target = [], [], []
                for t, parity in ((tap[0], g >> 1), (tap[1], g & 1)):
                    b = parity if t == 0 else 1 - parity
                    far.append(0 if 0 <= b + t <= 1 else 1)
                    target.append(b)
                pos = td + tap[2]
                far_z = 0 if 0 <= pos <= 1 else 1
                source_d = pos & 1
                s = far[0] * 4 + far[1] * 2 + far_z
                rows = (td * 4 + target[0] * 2 + target[1]) * 32
                cols = s * 256 + source_d * 128
                block = products[rows : rows + 32, cols : cols + 128]
                part = block if part is None else part + block
            total = part if total is None else jnp.where((lane >> 5) == g, part, total)
        total = total + pltpu.roll(total, 64, 1)
        total = total + pltpu.roll(total, 32, 1)
        slot = (first_tap + k) % 4
        held = total if held is None else jnp.where((lane >> 5) == slot, total, held)
        if slot == 3:
            row = (first_tap + k) // 4 * 32
            terms[row : row + 32, :] = held.astype(terms.dtype)
            held = None
    return held


def main_kernel(own, faces, far, near, big1, big2, big2t, down_mat,
                terms, ef, summed,
                field, ex, eg, eh, mk, ax, ag, ah, turned, products, mixed):
    picks = lane_picks()
    field[1:9, 1:5] = own[...]
    odd = lax.rem(lax.axis_index("tile"), 2)
    field[:, 5 * odd] = far[...]
    field[:, 5 - 5 * odd] = near[...]

    def place(at, face):
        field[at, 1:5] = face

    x_halo(faces, place)
    for store in (ex, eg, eh, ef):
        clear_edges(store)

    for x in range(0, 10, 2):
        rows = field[x : x + 2]
        both = dot(rows[:, :, :, 256:384].reshape(192, 128), down_mat[...], NT)
        mask = both[:, 256:512]
        mk[x : x + 2] = mask.astype(BF).reshape(2, 6, 16, 256)
        grad = (both[:, 0:256] * mask).astype(BF).reshape(2, 6, 16, 256)
        for j in range(2):
            put_field(ex, x + j + 1, 1, rows[j, :, :, 0:256])
            put_field(eg, x + j + 1, 1, grad[j])
    for x in range(0, 10, 2):
        for j in range(2):
            widen(ex, ax, x + j + 1, x + j, 1, 6, picks)
            widen(eg, ag, x + j + 1, x + j, 1, 6, picks)
        mask = mk[x : x + 2].reshape(192, 256).astype(F32)
        pre = dot(ax[x : x + 2].reshape(192, 2048), big1[...]) * mask
        spread = dot(ag[x : x + 2].reshape(192, 2048), big2t[...])
        s = jax.nn.sigmoid(pre)
        hidden = (pre * s).astype(BF).reshape(2, 6, 16, 256)
        grad = (spread * s * (1.0 + pre * (1.0 - s)) * mask).astype(BF).reshape(2, 6, 16, 256)
        for j in range(2):
            put_field(eh, x + j + 1, 1, hidden[j])
            put_field(ef, x + j + 1, 1, grad[j])
    for x in range(0, 8, 4):
        for j in range(4):
            widen(eh, ah, x + j + 2, x + j, 2, 4, picks)
        pre = dot(ah[x : x + 4].reshape(256, 2048), big2[...])
        mask = mk[x + 1 : x + 5, 1:5].reshape(256, 256).astype(F32)
        inputs = field[x + 1 : x + 5, 1:5, :, 0:256].reshape(256, 256).astype(F32)
        summed[x * 64 : x * 64 + 256, :] = (inputs + pre * mask).astype(BF)

    held = None
    for source, grads in ((1, ef), (2, eg)):
        turned[...] = grads[2:10, 2:6, :, 0:256].reshape(512, 256).astype(F32).T.astype(BF)
        for s in range(8):
            cols = slice(s * 256, s * 256 + 256)
            wide = (ax[1:9, 1:5, :, cols] if source == 1 else ah[:, :, :, cols]).reshape(512, 256)
            products[0:256, cols] = dot(turned[...], wide)
        held = fold_taps(products, terms, 27 * (source - 1), held)
    terms[416:448, :] = held.astype(terms.dtype)
    cot = field[1:9, 1:5, :, 256:384].reshape(512, 128).astype(F32).T.astype(BF)
    grad_down = dot(cot, summed[...])
    for half in range(2):
        for odd in range(2):
            part = grad_down[odd * 32 : odd * 32 + 32, half * 128 : half * 128 + 128]
            mixed[pl.ds(half * 64 + odd, 32, stride=2), :] = part
    terms[448:576, :] = mixed[...].astype(terms.dtype)
    rest = terms.shape[0] - 576
    if rest:
        terms[576:, :] = jnp.zeros((rest, 128), terms.dtype)


def tail_kernel(cell_ref, own, ef, summed, big1t, down_mat, grad_features, down, ah, turned, dense, place_mat, shuffle):
    picks = lane_picks()

    for x in range(0, 8, 4):
        for j in range(4):
            widen(ef, ah, x + j + 2, x + j, 2, 4, picks)
        spread = dot(ah[x : x + 4].reshape(256, 2048), big1t[...])
        both = dot(own[x : x + 4, :, :, 256:384].reshape(256, 128), down_mat[...], NT)
        grad = (both[:, 0:256] + spread) * both[:, 256:512]
        dense[x * 64 : x * 64 + 256, :] = grad.astype(BF)
    place_fine(cell_ref, place_mat)
    turned[...] = dense[...].astype(F32).T.astype(BF)
    pick = jnp.where(octant_rows(), 1.0, 0.0)
    for q in range(4):
        moved = dot(turned[...], place_mat[:, q * 512 : q * 512 + 512])
        total = moved[0:32] * pick[0:1]
        for e in range(1, 8):
            total = total + moved[e * 32 : e * 32 + 32] * pick[e : e + 1]
        grad_features[q] = total.astype(BF)
    lowered = dot(summed[...], down_mat[0:256, :]).T.astype(BF)
    low = iota((32, 128), 1) < 64
    for t in range(2):
        moved = dot(lowered, coarse_tile(cell_ref, t))
        even, odd = moved[0:32], moved[32:64]
        shuffle[:, 2 * t, :] = jnp.where(low, even, pltpu.roll(odd, 64, 1))
        shuffle[:, 2 * t + 1, :] = jnp.where(low, pltpu.roll(even, 64, 1), odd)
    for j in range(32):
        down[:, j * 128 : j * 128 + 128] = shuffle[j, 0:4, :].astype(BF)


def reduce_kernel(parts, out):
    count = parts.shape[0]
    total = parts[0].astype(F32)
    for i in range(1, count):
        total = total + parts[i].astype(F32)
    total = total.astype(out.dtype)
    for i in range(out.shape[0]):
        out[i] = total


def finish_kernel(scale, sums, one, two, down):
    for m in range(14):
        block = (sums[m * 32 : m * 32 + 32, :].astype(F32) * scale).T
        for g in range(4):
            k = 4 * m + g
            if k < 27:
                one[k] = block[g * 32 : g * 32 + 32]
            elif k < 54:
                two[k - 27] = block[g * 32 : g * 32 + 32]
    for half in range(2):
        block = (sums[448 + 64 * half : 512 + 64 * half, :].astype(F32) * scale).T
        for g in range(4):
            down[4 * (g >> 1) + 2 * (g & 1) + half] = block[g * 32 : g * 32 + 32]


def vmem_call(kernel, outs, ins, scratch=(), smem_first=False, flops=0, limit=48, in_space=pltpu.VMEM):
    specs = [pl.BlockSpec(memory_space=in_space) for _ in ins]
    if smem_first:
        specs[0] = pl.BlockSpec(memory_space=pltpu.SMEM)
    moved = sum(math.prod(x.shape) * x.dtype.itemsize for x in tuple(ins) + tuple(outs))
    return pl.pallas_call(
        kernel,
        out_shape=tuple(outs),
        in_specs=specs,
        out_specs=tuple(pl.BlockSpec(memory_space=pltpu.VMEM) for _ in outs),
        scratch_shapes=list(scratch),
        compiler_params=pltpu.CompilerParams(vmem_limit_bytes=limit * 1024 * 1024),
        cost_estimate=pl.CostEstimate(flops=flops, bytes_accessed=moved, transcendentals=0),
    )(*ins)


def bf(*shape):
    return jax.ShapeDtypeStruct(shape, BF)


def f32(*shape):
    return jax.ShapeDtypeStruct(shape, F32)


def on_device(features, voxel_mask, brick_cell, conv_one, conv_two, down_weight, cotangent):
    regions, tiles = lax.axis_size("region"), lax.axis_size("tile")
    devices = regions * tiles
    slots = features.shape[0]
    own, faces = vmem_call(
        gather_kernel,
        [bf(8, 4, 16, 384), bf(regions, 4, 16, 384)],
        (brick_cell, features, voxel_mask, cotangent),
        [pltpu.VMEM((512, 2304), BF), pltpu.VMEM((384, 2304), BF), pltpu.VMEM((32, 8, 128), F32),
         pltpu.SMEM(brick_cell.shape, I32), pltpu.VMEM(features.shape, BF), pltpu.VMEM(voxel_mask.shape, I32),
         pltpu.VMEM(cotangent.shape, BF), pltpu.SemaphoreType.DMA((4,))],
        in_space=pltpu.HBM,
        flops=2 * 512 * 2304 * 384,
        limit=60,
    )
    faces = lax.all_to_all(faces, "region", 0, 0, tiled=True)
    far, near = vmem_call(extend_kernel, [bf(10, 16, 384), bf(10, 16, 384)], (own, faces), limit=4)

    def swap(face, start):
        pairs = [(i, i + 1) for i in range(start, tiles - 1, 2)]
        return lax.ppermute(face, "tile", pairs + [(j, i) for i, j in pairs])

    far = swap(far, 1)
    near = swap(near, 0)
    big1, big1t, big2, big2t, down_mat = vmem_call(
        weights_kernel,
        [bf(2048, 256)] * 4 + [bf(512, 128)],
        (conv_one.reshape(864, 32), conv_two.reshape(864, 32), down_weight),
        [pltpu.VMEM((27, 4, 32, 32), BF), pltpu.VMEM((864, 128), BF), pltpu.VMEM((32, 3456), BF)],
        flops=2 * 2 * 32 * 3456 * 256,
        limit=16,
    )
    chunk = -(-576 // (8 * tiles)) * 8
    terms, ef, summed = vmem_call(
        main_kernel,
        [bf(tiles * chunk, 128), bf(12, 8, 16, 512), bf(512, 256)],
        (own, faces, far, near, big1, big2, big2t, down_mat),
        [
            pltpu.VMEM((10, 6, 16, 384), BF),
            pltpu.VMEM((12, 8, 16, 512), BF),
            pltpu.VMEM((12, 8, 16, 512), BF),
            pltpu.VMEM((12, 8, 16, 512), BF),
            pltpu.VMEM((10, 6, 16, 256), BF),
            pltpu.VMEM((10, 6, 16, 2048), BF),
            pltpu.VMEM((10, 6, 16, 2048), BF),
            pltpu.VMEM((8, 4, 16, 2048), BF),
            pltpu.VMEM((256, 512), BF),
            pltpu.VMEM((256, 2048), F32),
            pltpu.VMEM((128, 128), F32),
        ],
        flops=2 * 2048 * 256 * (960 * 2 + 512 * 3),
        limit=32,
    )
    parts = lax.all_to_all(terms.reshape(tiles, chunk, 128), "tile", 0, 0, tiled=True)
    (total,) = vmem_call(reduce_kernel, [bf(regions, chunk, 128)], (parts,), limit=4)
    parts = lax.all_to_all(total, "region", 0, 0, tiled=True)
    (total,) = vmem_call(reduce_kernel, [bf(tiles, chunk, 128)], (parts,), limit=4)
    sums = lax.all_to_all(total, "tile", 0, 0, tiled=True)
    grad_features, down = vmem_call(
        tail_kernel,
        [bf(slots, 32, 512), bf(slots, 4096)],
        (brick_cell, own, ef, summed, big1t, down_mat),
        [
            pltpu.VMEM((8, 4, 16, 2048), BF),
            pltpu.VMEM((256, 512), BF),
            pltpu.VMEM((512, 256), BF),
            pltpu.VMEM((512, 2048), BF),
            pltpu.VMEM((32, 8, 128), F32),
        ],
        smem_first=True,
        flops=2 * 2048 * 512 * 512,
        limit=16,
    )
    scale = 1.0 / math.sqrt(devices * slots * 512.0)
    grad_one, grad_two, grad_down = vmem_call(
        functools.partial(finish_kernel, scale),
        [f32(27, 32, 32), f32(27, 32, 32), f32(8, 32, 64)],
        (sums.reshape(tiles * chunk, 128),),
        limit=8,
    )
    return down, grad_features, grad_one, grad_two, grad_down


def solution(mesh):
    in_specs = (
        P(AXES, None, None),
        P(AXES, None),
        P(AXES),
        P(),
        P(),
        P(),
        P(AXES, None),
    )
    out_specs = (P(AXES, None), P(AXES, None, None), P(), P(), P())
    return jax.shard_map(
        on_device, mesh=mesh, in_specs=in_specs, out_specs=out_specs, check_vma=False
    )
```

```python
import functools
import math

import jax
import jax.numpy as jnp
from jax import lax
from jax.experimental import pallas as pl
from jax.experimental.pallas import tpu as pltpu
from jax.sharding import PartitionSpec as P


BF = jnp.bfloat16
F32 = jnp.float32
I32 = jnp.int32
NN = (((1,), (0,)), ((), ()))
NT = (((1,), (1,)), ((), ()))
AXES = ("region", "tile")


def dot(lhs, rhs, dims=NN):
    return lax.dot_general(lhs, rhs, dims, preferred_element_type=F32)


def iota(shape, dim):
    return lax.broadcasted_iota(I32, shape, dim)


def parity_fields(v):
    return v & 1, (v >> 6) & 1, (v >> 3) & 1


def octant_rows(first=0):
    e = iota((8, 512), 0)
    d, a, b = parity_fields(iota((8, 512), 1))
    return (d == (e >> 2)) & (a == ((e >> 1) & 1)) & (b == (e & 1))


def row_codes():
    row = iota((512, 128), 0)
    code = ((row >> 6) & 3) * 16 + ((row >> 4) & 3) * 4 + (row & 3)
    cell = (row >> 8) * 4 + ((row >> 2) & 3)
    return code, cell


def place_fine(cell_ref, place):
    code, cell = row_codes()
    for q in range(4):
        code_q = jnp.where(cell == cell_ref[q], code, -1)
        for t in range(4):
            v = iota((1, 128), 1) + 128 * t
            vcode = (v >> 7) * 16 + ((v >> 4) & 3) * 4 + ((v >> 1) & 3)
            first = q * 512 + t * 128
            place[:, first : first + 128] = jnp.where(code_q == vcode, 1.0, 0.0).astype(BF)


def coarse_tile(cell_ref, t):
    code, cell = row_codes()
    lane = iota((512, 128), 1)
    wanted = jnp.where(lane < 64, cell_ref[2 * t], cell_ref[2 * t + 1])
    return jnp.where((cell == wanted) & (code == (lane & 63)), 1.0, 0.0).astype(BF)


def gather_kernel(cell_hbm, feat_hbm, vmask_hbm, cot_hbm, own, faces,
                  lhs, rhs, cots, box, shuffle, cell_ref, feat_ref, vmask_ref, cot_ref, sems):
    moves = [
        pltpu.make_async_copy(source, target, sems.at[i])
        for i, (source, target) in enumerate(
            ((cell_hbm, cell_ref), (vmask_hbm, vmask_ref), (feat_hbm, feat_ref), (cot_hbm, cot_ref))
        )
    ]
    for move in moves:
        move.start()
    row = iota((128, 128), 0)
    code = (row >> 5) * 16 + ((row >> 3) & 3) * 4 + (row & 3)
    for t in range(4):
        v = iota((1, 128), 1) + 128 * t
        vcode = (v >> 7) * 16 + ((v >> 4) & 3) * 4 + ((v >> 1) & 3)
        lhs[:, t * 128 : t * 128 + 128] = jnp.where(code == vcode, 1.0, 0.0).astype(BF)
    box[...] = jnp.zeros((8, 4, 16, 384), F32)
    for move in moves:
        move.wait()
    match = octant_rows()
    for q in range(4):
        cols = slice(q * 512, q * 512 + 512)
        m8 = jnp.where(match, vmask_ref[q : q + 1, :].astype(F32), 0.0)
        x = feat_ref[q].astype(F32)
        for e in range(8):
            rhs[e * 32 : e * 32 + 32, cols] = (x * m8[e : e + 1, :]).astype(BF)
        rhs[256:320, cols] = jnp.zeros((64, 512), BF)
        rhs[320:336, cols] = jnp.concatenate([m8, jnp.zeros((8, 512), F32)], axis=0).astype(BF)
        rhs[336:384, cols] = jnp.zeros((48, 512), BF)
    cots[64:128, :] = jnp.zeros((64, 256), BF)
    for j in range(32):
        shuffle[j, 0:4, :] = cot_ref[:, j * 128 : j * 128 + 128].astype(F32)
    low = iota((32, 128), 1) < 64
    for t in range(2):
        first, second = shuffle[:, 2 * t, :], shuffle[:, 2 * t + 1, :]
        cols = slice(t * 128, t * 128 + 128)
        cots[0:32, cols] = jnp.where(low, first, pltpu.roll(second, 64, 1)).astype(BF)
        cots[32:64, cols] = jnp.where(low, pltpu.roll(first, 64, 1), second).astype(BF)
    wide_code = iota((128, 256), 0)
    wide_code = (wide_code >> 5) * 16 + ((wide_code >> 3) & 3) * 4 + (wide_code & 3)
    z_part = iota((16, 128), 0) >> 2
    for q in range(4):
        cell = cell_ref[q]
        here_z = jnp.where(cell < 0, -1, cell & 3)
        half = pl.ds(4 * (jnp.maximum(cell, 0) >> 2), 4)
        pick = jnp.where(iota((128, 256), 1) - 64 * q == wide_code, 1.0, 0.0).astype(BF)
        fine = dot(lhs[...], rhs[:, q * 512 : q * 512 + 512], NT)
        third = fine[:, 256:384] + dot(pick, cots[...], NT)
        for t, part in enumerate((fine[:, 0:128], fine[:, 128:256], third)):
            part = part.reshape(4, 4, 8, 128)
            part = jnp.concatenate([part, part], axis=2)
            part = jnp.where((z_part == here_z)[None, None], part, 0.0)
            cols = slice(t * 128, t * 128 + 128)
            box[half, :, :, cols] = box[half, :, :, cols] + part
    field = box[...].astype(BF)
    own[...] = field
    here = lax.axis_index("region")
    for p in range(faces.shape[0]):
        faces[p] = own[jnp.where(p < here, 0, 7)]


def x_halo(faces, place):
    here = lax.axis_index("region")
    count = faces.shape[0]
    for at, there in ((0, here - 1), (9, here + 1)):
        inside = (there >= 0) & (there < count)

        @pl.when(inside)
        def _():
            place(at, faces[jnp.clip(there, 0, count - 1)])

        @pl.when(jnp.logical_not(inside))
        def _():
            place(at, jnp.zeros(faces.shape[1:], BF))


def extend_kernel(own, faces, far, near, own_on):
    own_on[...] = own[...]
    odd = lax.rem(lax.axis_index("tile"), 2)

    def fill(low, high):
        low[1:9] = own[:, 0]
        high[1:9] = own[:, 3]

        def place(at, face):
            low[at] = face[0]
            high[at] = face[3]

        x_halo(faces, place)

    pl.when(odd == 1)(lambda: fill(near, far))
    pl.when(odd == 0)(lambda: fill(far, near))


def tap_of(far, source, target):
    position = source if far == 0 else (2 if source == 0 else -1)
    tap = position - target
    return tap if -1 <= tap <= 1 else None


def weights_kernel(w1_ref, w2_ref, dw_ref, big1, big1t, big2, big2t, down_mat, rep, tiles, tiles_t):
    lane = iota((32, 128), 1)
    spread = jnp.where((lane & 31) == iota((32, 128), 0), 1.0, 0.0).astype(BF)
    eye = jnp.where(iota((32, 32), 0) == iota((32, 32), 1), 1.0, 0.0).astype(BF)
    group = [jnp.where((lane >> 5) == g, 1.0, 0.0).astype(BF) for g in range(4)]
    for w_ref, big, big_t in ((w1_ref, big1, big1t), (w2_ref, big2, big2t)):
        tiles[...] = dot(w_ref[...], spread).astype(BF)
        w3 = w_ref[...].reshape(27, 32, 32)
        for j in range(4):
            rep[:, j] = w3
        tiles_t[...] = dot(eye, rep[...].reshape(27 * 128, 32), NT).astype(BF)
        for s in range(8):
            sx, sy, sz = s >> 2, (s >> 1) & 1, s & 1
            for e in range(8):
                d, a, b = e >> 2, (e >> 1) & 1, e & 1
                first = s * 256 + e * 32
                for td in range(2):
                    plain = None
                    turned = None
                    for g in range(4):
                        taps = (tap_of(sx, a, g >> 1), tap_of(sy, b, g & 1), tap_of(sz, d, td))
                        if None in taps:
                            continue
                        k = 9 * (taps[0] + 1) + 3 * (taps[1] + 1) + taps[2] + 1
                        back = 26 - k
                        term = tiles[k * 32 : k * 32 + 32, :] * group[g]
                        term_t = tiles_t[:, back * 128 : back * 128 + 128] * group[g]
                        plain = term if plain is None else plain + term
                        turned = term_t if turned is None else turned + term_t
                    zero = jnp.zeros((32, 128), BF)
                    big[first : first + 32, td * 128 : td * 128 + 128] = zero if plain is None else plain
                    big_t[first : first + 32, td * 128 : td * 128 + 128] = zero if turned is None else turned
    column = iota((64, 64), 1)
    order = jnp.where(iota((64, 64), 0) == 2 * (column & 31) + (column >> 5), 1.0, 0.0).astype(BF)
    ordered = dot(dw_ref[...].reshape(256, 64), order).astype(BF)
    for e in range(8):
        k = 4 * ((e >> 1) & 1) + 2 * (e & 1) + (e >> 2)
        down_mat[e * 32 : e * 32 + 32, 0:64] = ordered[k * 32 : k * 32 + 32]
    down_mat[0:256, 64:128] = jnp.zeros((256, 64), BF)
    unit = iota((256, 128), 1) - 64 == (iota((256, 128), 0) >> 5)
    down_mat[256:512, :] = jnp.where(unit, 1.0, 0.0).astype(BF)


def lane_picks():
    lane = iota((16, 512), 1)
    low_a = jnp.where(((lane >> 6) & 1) == 0, 1.0, 0.0).astype(BF) > 0.5
    low_b = jnp.where(((lane >> 5) & 1) == 0, 1.0, 0.0).astype(BF) > 0.5
    return low_a[None], low_b[None]


def put_field(store, x, y0, value):
    ny = value.shape[0]
    z = iota((ny, 16, 128), 1)
    store[x, y0 : y0 + ny, :, 0:256] = value
    up = pltpu.roll(value[:, :, 0:128].astype(F32), 15, 1)
    store[x, y0 : y0 + ny, :, 256:384] = jnp.where(z == 15, 0.0, up).astype(BF)
    dn = pltpu.roll(value[:, :, 128:256].astype(F32), 1, 1)
    store[x, y0 : y0 + ny, :, 384:512] = jnp.where(z == 0, 0.0, dn).astype(BF)


def clear_edges(store):
    store[0] = jnp.zeros((8, 16, 512), BF)
    store[11] = jnp.zeros((8, 16, 512), BF)

    def edge(x, carry):
        store[x, 0] = jnp.zeros((16, 512), BF)
        store[x, 7] = jnp.zeros((16, 512), BF)
        return carry

    lax.fori_loop(1, 11, edge, 0)


def widen(store, wide, x, at, y0, ny, picks):
    low_a, low_b = picks
    low_a = jnp.broadcast_to(low_a, (ny, 16, 512))
    low_b = jnp.broadcast_to(low_b, (ny, 16, 512))

    def at_y(dx, dy):
        return store[x + dx, y0 + dy : y0 + dy + ny]

    wide[at, :, :, 0:512] = at_y(0, 0)
    wide[at, :, :, 512:1024] = jnp.where(low_b, at_y(0, 1), at_y(0, -1))
    wide[at, :, :, 1024:1536] = jnp.where(low_a, at_y(1, 0), at_y(-1, 0))
    upper = jnp.where(low_b, at_y(1, 1), at_y(1, -1))
    lower = jnp.where(low_b, at_y(-1, 1), at_y(-1, -1))
    wide[at, :, :, 1536:2048] = jnp.where(low_a, upper, lower)


def fold_taps(products, terms, first_tap, held):
    lane = iota((32, 128), 1)
    for k in range(27):
        tap = (k // 9 - 1, k // 3 % 3 - 1, k % 3 - 1)
        total = None
        for g in range(4):
            part = None
            for td in range(2):
                far, source, target = [], [], []
                for t, parity in ((tap[0], g >> 1), (tap[1], g & 1)):
                    b = parity if t == 0 else 1 - parity
                    far.append(0 if 0 <= b + t <= 1 else 1)
                    target.append(b)
                pos = td + tap[2]
                far_z = 0 if 0 <= pos <= 1 else 1
                source_d = pos & 1
                s = far[0] * 4 + far[1] * 2 + far_z
                rows = (td * 4 + target[0] * 2 + target[1]) * 32
                cols = s * 256 + source_d * 128
                block = products[rows : rows + 32, cols : cols + 128]
                part = block if part is None else part + block
            total = part if total is None else jnp.where((lane >> 5) == g, part, total)
        total = total + pltpu.roll(total, 64, 1)
        total = total + pltpu.roll(total, 32, 1)
        slot = (first_tap + k) % 4
        held = total if held is None else jnp.where((lane >> 5) == slot, total, held)
        if slot == 3:
            row = (first_tap + k) // 4 * 32
            terms[row : row + 32, :] = held.astype(terms.dtype)
            held = None
    return held


def main_kernel(own, faces, far, near, big1, big2, big2t, down_mat,
                terms, ef, summed,
                field, ex, eg, eh, mk, ax, ag, ah, turned, products, mixed):
    picks = lane_picks()
    field[1:9, 1:5] = own[...]
    odd = lax.rem(lax.axis_index("tile"), 2)
    field[:, 5 * odd] = far[...]
    field[:, 5 - 5 * odd] = near[...]

    def place(at, face):
        field[at, 1:5] = face

    x_halo(faces, place)
    for store in (ex, eg, eh, ef):
        clear_edges(store)

    for x in range(0, 10, 2):
        rows = field[x : x + 2]
        both = dot(rows[:, :, :, 256:384].reshape(192, 128), down_mat[...], NT)
        mask = both[:, 256:512]
        mk[x : x + 2] = mask.astype(BF).reshape(2, 6, 16, 256)
        grad = (both[:, 0:256] * mask).astype(BF).reshape(2, 6, 16, 256)
        for j in range(2):
            put_field(ex, x + j + 1, 1, rows[j, :, :, 0:256])
            put_field(eg, x + j + 1, 1, grad[j])
    for x in range(0, 10, 2):
        for j in range(2):
            widen(ex, ax, x + j + 1, x + j, 1, 6, picks)
            widen(eg, ag, x + j + 1, x + j, 1, 6, picks)
        mask = mk[x : x + 2].reshape(192, 256).astype(F32)
        pre = dot(ax[x : x + 2].reshape(192, 2048), big1[...]) * mask
        spread = dot(ag[x : x + 2].reshape(192, 2048), big2t[...])
        s = jax.nn.sigmoid(pre)
        hidden = (pre * s).astype(BF).reshape(2, 6, 16, 256)
        grad = (spread * s * (1.0 + pre * (1.0 - s)) * mask).astype(BF).reshape(2, 6, 16, 256)
        for j in range(2):
            put_field(eh, x + j + 1, 1, hidden[j])
            put_field(ef, x + j + 1, 1, grad[j])
    for x in range(0, 8, 4):
        for j in range(4):
            widen(eh, ah, x + j + 2, x + j, 2, 4, picks)
        pre = dot(ah[x : x + 4].reshape(256, 2048), big2[...])
        mask = mk[x + 1 : x + 5, 1:5].reshape(256, 256).astype(F32)
        inputs = field[x + 1 : x + 5, 1:5, :, 0:256].reshape(256, 256).astype(F32)
        summed[x * 64 : x * 64 + 256, :] = (inputs + pre * mask).astype(BF)

    held = None
    for source, grads in ((1, ef), (2, eg)):
        turned[...] = grads[2:10, 2:6, :, 0:256].reshape(512, 256).astype(F32).T.astype(BF)
        for s in range(8):
            cols = slice(s * 256, s * 256 + 256)
            wide = (ax[1:9, 1:5, :, cols] if source == 1 else ah[:, :, :, cols]).reshape(512, 256)
            products[0:256, cols] = dot(turned[...], wide)
        held = fold_taps(products, terms, 27 * (source - 1), held)
    terms[416:448, :] = held.astype(terms.dtype)
    cot = field[1:9, 1:5, :, 256:384].reshape(512, 128).astype(F32).T.astype(BF)
    grad_down = dot(cot, summed[...])
    for half in range(2):
        for odd in range(2):
            part = grad_down[odd * 32 : odd * 32 + 32, half * 128 : half * 128 + 128]
            mixed[pl.ds(half * 64 + odd, 32, stride=2), :] = part
    terms[448:576, :] = mixed[...].astype(terms.dtype)
    rest = terms.shape[0] - 576
    if rest:
        terms[576:, :] = jnp.zeros((rest, 128), terms.dtype)


def tail_kernel(cell_ref, own, ef, summed, big1t, down_mat, grad_features, down, ah, turned, dense, place_mat, shuffle):
    picks = lane_picks()

    for x in range(0, 8, 4):
        for j in range(4):
            widen(ef, ah, x + j + 2, x + j, 2, 4, picks)
        spread = dot(ah[x : x + 4].reshape(256, 2048), big1t[...])
        both = dot(own[x : x + 4, :, :, 256:384].reshape(256, 128), down_mat[...], NT)
        grad = (both[:, 0:256] + spread) * both[:, 256:512]
        dense[x * 64 : x * 64 + 256, :] = grad.astype(BF)
    place_fine(cell_ref, place_mat)
    turned[...] = dense[...].astype(F32).T.astype(BF)
    pick = jnp.where(octant_rows(), 1.0, 0.0)
    for q in range(4):
        moved = dot(turned[...], place_mat[:, q * 512 : q * 512 + 512])
        total = moved[0:32] * pick[0:1]
        for e in range(1, 8):
            total = total + moved[e * 32 : e * 32 + 32] * pick[e : e + 1]
        grad_features[q] = total.astype(BF)
    lowered = dot(summed[...], down_mat[0:256, :]).T.astype(BF)
    low = iota((32, 128), 1) < 64
    for t in range(2):
        moved = dot(lowered, coarse_tile(cell_ref, t))
        even, odd = moved[0:32], moved[32:64]
        shuffle[:, 2 * t, :] = jnp.where(low, even, pltpu.roll(odd, 64, 1))
        shuffle[:, 2 * t + 1, :] = jnp.where(low, pltpu.roll(even, 64, 1), odd)
    for j in range(32):
        down[:, j * 128 : j * 128 + 128] = shuffle[j, 0:4, :].astype(BF)


def reduce_kernel(parts, out):
    count = parts.shape[0]
    total = parts[0].astype(F32)
    for i in range(1, count):
        total = total + parts[i].astype(F32)
    total = total.astype(out.dtype)
    for i in range(out.shape[0]):
        out[i] = total


def finish_kernel(scale, sums, one, two, down):
    for m in range(14):
        block = (sums[m * 32 : m * 32 + 32, :].astype(F32) * scale).T
        for g in range(4):
            k = 4 * m + g
            if k < 27:
                one[k] = block[g * 32 : g * 32 + 32]
            elif k < 54:
                two[k - 27] = block[g * 32 : g * 32 + 32]
    for half in range(2):
        block = (sums[448 + 64 * half : 512 + 64 * half, :].astype(F32) * scale).T
        for g in range(4):
            down[4 * (g >> 1) + 2 * (g & 1) + half] = block[g * 32 : g * 32 + 32]


def vmem_call(kernel, outs, ins, scratch=(), smem_first=False, flops=0, limit=48, in_space=pltpu.VMEM):
    specs = [pl.BlockSpec(memory_space=in_space) for _ in ins]
    if smem_first:
        specs[0] = pl.BlockSpec(memory_space=pltpu.SMEM)
    moved = sum(math.prod(x.shape) * x.dtype.itemsize for x in tuple(ins) + tuple(outs))
    return pl.pallas_call(
        kernel,
        out_shape=tuple(outs),
        in_specs=specs,
        out_specs=tuple(pl.BlockSpec(memory_space=pltpu.VMEM) for _ in outs),
        scratch_shapes=list(scratch),
        compiler_params=pltpu.CompilerParams(vmem_limit_bytes=limit * 1024 * 1024),
        cost_estimate=pl.CostEstimate(flops=flops, bytes_accessed=moved, transcendentals=0),
    )(*ins)


def bf(*shape):
    return jax.ShapeDtypeStruct(shape, BF)


def f32(*shape):
    return jax.ShapeDtypeStruct(shape, F32)


def on_device(features, voxel_mask, brick_cell, conv_one, conv_two, down_weight, cotangent):
    regions, tiles = lax.axis_size("region"), lax.axis_size("tile")
    devices = regions * tiles
    slots = features.shape[0]
    own, faces = vmem_call(
        gather_kernel,
        [bf(8, 4, 16, 384), bf(regions, 4, 16, 384)],
        (brick_cell, features, voxel_mask, cotangent),
        [pltpu.VMEM((128, 512), BF), pltpu.VMEM((384, 2048), BF), pltpu.VMEM((128, 256), BF),
         pltpu.VMEM((8, 4, 16, 384), F32), pltpu.VMEM((32, 8, 128), F32),
         pltpu.SMEM(brick_cell.shape, I32), pltpu.VMEM(features.shape, BF), pltpu.VMEM(voxel_mask.shape, I32),
         pltpu.VMEM(cotangent.shape, BF), pltpu.SemaphoreType.DMA((4,))],
        in_space=pltpu.HBM,
        flops=2 * 128 * 4 * 768 * 384,
        limit=60,
    )
    faces = lax.all_to_all(faces, "region", 0, 0, tiled=True)
    far, near, own = vmem_call(
        extend_kernel, [bf(10, 16, 384), bf(10, 16, 384), bf(8, 4, 16, 384)], (own, faces), limit=4
    )

    def swap(face, start):
        pairs = [(i, i + 1) for i in range(start, tiles - 1, 2)]
        return lax.ppermute(face, "tile", pairs + [(j, i) for i, j in pairs])

    far = swap(far, 1)
    near = swap(near, 0)
    big1, big1t, big2, big2t, down_mat = vmem_call(
        weights_kernel,
        [bf(2048, 256)] * 4 + [bf(512, 128)],
        (conv_one.reshape(864, 32), conv_two.reshape(864, 32), down_weight),
        [pltpu.VMEM((27, 4, 32, 32), BF), pltpu.VMEM((864, 128), BF), pltpu.VMEM((32, 3456), BF)],
        flops=2 * 2 * 32 * 3456 * 256,
        limit=16,
    )
    chunk = -(-576 // (8 * tiles)) * 8
    terms, ef, summed = vmem_call(
        main_kernel,
        [bf(tiles * chunk, 128), bf(12, 8, 16, 512), bf(512, 256)],
        (own, faces, far, near, big1, big2, big2t, down_mat),
        [
            pltpu.VMEM((10, 6, 16, 384), BF),
            pltpu.VMEM((12, 8, 16, 512), BF),
            pltpu.VMEM((12, 8, 16, 512), BF),
            pltpu.VMEM((12, 8, 16, 512), BF),
            pltpu.VMEM((10, 6, 16, 256), BF),
            pltpu.VMEM((10, 6, 16, 2048), BF),
            pltpu.VMEM((10, 6, 16, 2048), BF),
            pltpu.VMEM((8, 4, 16, 2048), BF),
            pltpu.VMEM((256, 512), BF),
            pltpu.VMEM((256, 2048), F32),
            pltpu.VMEM((128, 128), F32),
        ],
        flops=2 * 2048 * 256 * (960 * 2 + 512 * 3),
        limit=32,
    )
    parts = lax.all_to_all(terms.reshape(tiles, chunk, 128), "tile", 0, 0, tiled=True)
    (total,) = vmem_call(reduce_kernel, [bf(regions, chunk, 128)], (parts,), limit=4)
    parts = lax.all_to_all(total, "region", 0, 0, tiled=True)
    (total,) = vmem_call(reduce_kernel, [bf(tiles, chunk, 128)], (parts,), limit=4)
    sums = lax.all_to_all(total, "tile", 0, 0, tiled=True)
    grad_features, down = vmem_call(
        tail_kernel,
        [bf(slots, 32, 512), bf(slots, 4096)],
        (brick_cell, own, ef, summed, big1t, down_mat),
        [
            pltpu.VMEM((8, 4, 16, 2048), BF),
            pltpu.VMEM((256, 512), BF),
            pltpu.VMEM((512, 256), BF),
            pltpu.VMEM((512, 2048), BF),
            pltpu.VMEM((32, 8, 128), F32),
        ],
        smem_first=True,
        flops=2 * 2048 * 512 * 512,
        limit=16,
    )
    scale = 1.0 / math.sqrt(devices * slots * 512.0)
    grad_one, grad_two, grad_down = vmem_call(
        functools.partial(finish_kernel, scale),
        [f32(27, 32, 32), f32(27, 32, 32), f32(8, 32, 64)],
        (sums.reshape(tiles * chunk, 128),),
        limit=8,
    )
    return down, grad_features, grad_one, grad_two, grad_down


def solution(mesh):
    in_specs = (
        P(AXES, None, None),
        P(AXES, None),
        P(AXES),
        P(),
        P(),
        P(),
        P(AXES, None),
    )
    out_specs = (P(AXES, None), P(AXES, None, None), P(), P(), P())
    return jax.shard_map(
        on_device, mesh=mesh, in_specs=in_specs, out_specs=out_specs, check_vma=False
    )
```

```python
import functools
import math

import jax
import jax.numpy as jnp
from jax import lax
from jax.experimental import pallas as pl
from jax.experimental.pallas import tpu as pltpu
from jax.sharding import PartitionSpec as P


BF = jnp.bfloat16
F32 = jnp.float32
I32 = jnp.int32
NN = (((1,), (0,)), ((), ()))
NT = (((1,), (1,)), ((), ()))
AXES = ("region", "tile")


def dot(lhs, rhs, dims=NN):
    return lax.dot_general(lhs, rhs, dims, preferred_element_type=F32)


def iota(shape, dim):
    return lax.broadcasted_iota(I32, shape, dim)


def parity_fields(v):
    return v & 1, (v >> 6) & 1, (v >> 3) & 1


def octant_rows(first=0):
    e = iota((8, 512), 0)
    d, a, b = parity_fields(iota((8, 512), 1))
    return (d == (e >> 2)) & (a == ((e >> 1) & 1)) & (b == (e & 1))


def row_codes():
    row = iota((512, 128), 0)
    code = ((row >> 6) & 3) * 16 + ((row >> 4) & 3) * 4 + (row & 3)
    cell = (row >> 8) * 4 + ((row >> 2) & 3)
    return code, cell


def place_fine(cell_ref, place):
    code, cell = row_codes()
    for q in range(4):
        code_q = jnp.where(cell == cell_ref[q], code, -1)
        for t in range(4):
            v = iota((1, 128), 1) + 128 * t
            vcode = (v >> 7) * 16 + ((v >> 4) & 3) * 4 + ((v >> 1) & 3)
            first = q * 512 + t * 128
            place[:, first : first + 128] = jnp.where(code_q == vcode, 1.0, 0.0).astype(BF)


def coarse_tile(cell_ref, t):
    code, cell = row_codes()
    lane = iota((512, 128), 1)
    wanted = jnp.where(lane < 64, cell_ref[2 * t], cell_ref[2 * t + 1])
    return jnp.where((cell == wanted) & (code == (lane & 63)), 1.0, 0.0).astype(BF)


def gather_kernel(cell_hbm, feat_hbm, vmask_hbm, cot_hbm, own, faces,
                  lhs, rhs, cots, box, shuffle, cell_ref, feat_ref, vmask_ref, cot_ref, sems):
    moves = [
        pltpu.make_async_copy(source, target, sems.at[i])
        for i, (source, target) in enumerate(
            ((cell_hbm, cell_ref), (vmask_hbm, vmask_ref), (feat_hbm, feat_ref), (cot_hbm, cot_ref))
        )
    ]
    for move in moves:
        move.start()
    row = iota((128, 128), 0)
    code = (row >> 5) * 16 + ((row >> 3) & 3) * 4 + (row & 3)
    for t in range(4):
        v = iota((1, 128), 1) + 128 * t
        vcode = (v >> 7) * 16 + ((v >> 4) & 3) * 4 + ((v >> 1) & 3)
        lhs[:, t * 128 : t * 128 + 128] = jnp.where(code == vcode, 1.0, 0.0).astype(BF)
    box[...] = jnp.zeros((8, 4, 16, 384), F32)
    for move in moves:
        move.wait()
    match = octant_rows()
    for q in range(4):
        cols = slice(q * 512, q * 512 + 512)
        m8 = jnp.where(match, vmask_ref[q : q + 1, :].astype(F32), 0.0)
        x = feat_ref[q].astype(F32)
        for e in range(8):
            rhs[e * 32 : e * 32 + 32, cols] = (x * m8[e : e + 1, :]).astype(BF)
        rhs[256:320, cols] = jnp.zeros((64, 512), BF)
        rhs[320:336, cols] = jnp.concatenate([m8, jnp.zeros((8, 512), F32)], axis=0).astype(BF)
        rhs[336:384, cols] = jnp.zeros((48, 512), BF)
    cots[64:128, :] = jnp.zeros((64, 256), BF)
    for j in range(32):
        shuffle[j, 0:4, :] = cot_ref[:, j * 128 : j * 128 + 128].astype(F32)
    low = iota((32, 128), 1) < 64
    for t in range(2):
        first, second = shuffle[:, 2 * t, :], shuffle[:, 2 * t + 1, :]
        cols = slice(t * 128, t * 128 + 128)
        cots[0:32, cols] = jnp.where(low, first, pltpu.roll(second, 64, 1)).astype(BF)
        cots[32:64, cols] = jnp.where(low, pltpu.roll(first, 64, 1), second).astype(BF)
    wide_code = iota((128, 256), 0)
    wide_code = (wide_code >> 5) * 16 + ((wide_code >> 3) & 3) * 4 + (wide_code & 3)
    z_part = iota((16, 128), 0) >> 2
    for q in range(4):
        cell = cell_ref[q]
        here_z = jnp.where(cell < 0, -1, cell & 3)
        half = pl.ds(4 * (jnp.maximum(cell, 0) >> 2), 4)
        pick = jnp.where(iota((128, 256), 1) - 64 * q == wide_code, 1.0, 0.0).astype(BF)
        fine = dot(lhs[...], rhs[:, q * 512 : q * 512 + 512], NT)
        third = fine[:, 256:384] + dot(pick, cots[...], NT)
        for t, part in enumerate((fine[:, 0:128], fine[:, 128:256], third)):
            part = part.reshape(4, 4, 8, 128)
            part = jnp.concatenate([part, part], axis=2)
            part = jnp.where((z_part == here_z)[None, None], part, 0.0)
            cols = slice(t * 128, t * 128 + 128)
            box[half, :, :, cols] = box[half, :, :, cols] + part
    field = box[...].astype(BF)
    own[...] = field
    here = lax.axis_index("region")
    for p in range(faces.shape[0]):
        faces[p] = own[jnp.where(p < here, 0, 7)]


def x_halo(faces, place):
    here = lax.axis_index("region")
    count = faces.shape[0]
    for at, there in ((0, here - 1), (9, here + 1)):
        inside = (there >= 0) & (there < count)

        @pl.when(inside)
        def _():
            place(at, faces[jnp.clip(there, 0, count - 1)])

        @pl.when(jnp.logical_not(inside))
        def _():
            place(at, jnp.zeros(faces.shape[1:], BF))


def extend_kernel(own, faces, far, near, own_on):
    own_on[...] = own[...]
    odd = lax.rem(lax.axis_index("tile"), 2)

    def fill(low, high):
        low[1:9] = own[:, 0]
        high[1:9] = own[:, 3]

        def place(at, face):
            low[at] = face[0]
            high[at] = face[3]

        x_halo(faces, place)

    pl.when(odd == 1)(lambda: fill(near, far))
    pl.when(odd == 0)(lambda: fill(far, near))


def tap_of(far, source, target):
    position = source if far == 0 else (2 if source == 0 else -1)
    tap = position - target
    return tap if -1 <= tap <= 1 else None


def weights_kernel(w1_ref, w2_ref, dw_ref, big1, big1t, big2, big2t, down_mat, rep, tiles, tiles_t):
    lane = iota((32, 128), 1)
    spread = jnp.where((lane & 31) == iota((32, 128), 0), 1.0, 0.0).astype(BF)
    eye = jnp.where(iota((32, 32), 0) == iota((32, 32), 1), 1.0, 0.0).astype(BF)
    group = [jnp.where((lane >> 5) == g, 1.0, 0.0).astype(BF) for g in range(4)]
    for w_ref, big, big_t in ((w1_ref, big1, big1t), (w2_ref, big2, big2t)):
        tiles[...] = dot(w_ref[...], spread).astype(BF)
        w3 = w_ref[...].reshape(27, 32, 32)
        for j in range(4):
            rep[:, j] = w3
        tiles_t[...] = dot(eye, rep[...].reshape(27 * 128, 32), NT).astype(BF)
        for s in range(8):
            sx, sy, sz = s >> 2, (s >> 1) & 1, s & 1
            for e in range(8):
                d, a, b = e >> 2, (e >> 1) & 1, e & 1
                first = s * 256 + e * 32
                for td in range(2):
                    plain = None
                    turned = None
                    for g in range(4):
                        taps = (tap_of(sx, a, g >> 1), tap_of(sy, b, g & 1), tap_of(sz, d, td))
                        if None in taps:
                            continue
                        k = 9 * (taps[0] + 1) + 3 * (taps[1] + 1) + taps[2] + 1
                        back = 26 - k
                        term = tiles[k * 32 : k * 32 + 32, :] * group[g]
                        term_t = tiles_t[:, back * 128 : back * 128 + 128] * group[g]
                        plain = term if plain is None else plain + term
                        turned = term_t if turned is None else turned + term_t
                    zero = jnp.zeros((32, 128), BF)
                    big[first : first + 32, td * 128 : td * 128 + 128] = zero if plain is None else plain
                    big_t[first : first + 32, td * 128 : td * 128 + 128] = zero if turned is None else turned
    column = iota((64, 64), 1)
    order = jnp.where(iota((64, 64), 0) == 2 * (column & 31) + (column >> 5), 1.0, 0.0).astype(BF)
    ordered = dot(dw_ref[...].reshape(256, 64), order).astype(BF)
    for e in range(8):
        k = 4 * ((e >> 1) & 1) + 2 * (e & 1) + (e >> 2)
        down_mat[e * 32 : e * 32 + 32, 0:64] = ordered[k * 32 : k * 32 + 32]
    down_mat[0:256, 64:128] = jnp.zeros((256, 64), BF)
    unit = iota((256, 128), 1) - 64 == (iota((256, 128), 0) >> 5)
    down_mat[256:512, :] = jnp.where(unit, 1.0, 0.0).astype(BF)


def lane_picks():
    lane = iota((16, 512), 1)
    low_a = jnp.where(((lane >> 6) & 1) == 0, 1.0, 0.0).astype(BF) > 0.5
    low_b = jnp.where(((lane >> 5) & 1) == 0, 1.0, 0.0).astype(BF) > 0.5
    return low_a[None], low_b[None]


def put_field(store, x, y0, value):
    ny = value.shape[0]
    z = iota((ny, 16, 128), 1)
    store[x, y0 : y0 + ny, :, 0:256] = value
    up = pltpu.roll(value[:, :, 0:128].astype(F32), 15, 1)
    store[x, y0 : y0 + ny, :, 256:384] = jnp.where(z == 15, 0.0, up).astype(BF)
    dn = pltpu.roll(value[:, :, 128:256].astype(F32), 1, 1)
    store[x, y0 : y0 + ny, :, 384:512] = jnp.where(z == 0, 0.0, dn).astype(BF)


def clear_edges(store):
    store[0] = jnp.zeros((8, 16, 512), BF)
    store[11] = jnp.zeros((8, 16, 512), BF)

    def edge(x, carry):
        store[x, 0] = jnp.zeros((16, 512), BF)
        store[x, 7] = jnp.zeros((16, 512), BF)
        return carry

    lax.fori_loop(1, 11, edge, 0)


def widen(store, wide, x, at, y0, ny, picks):
    low_a, low_b = picks
    low_a = jnp.broadcast_to(low_a, (ny, 16, 512))
    low_b = jnp.broadcast_to(low_b, (ny, 16, 512))

    def at_y(dx, dy):
        return store[x + dx, y0 + dy : y0 + dy + ny]

    wide[at, :, :, 0:512] = at_y(0, 0)
    wide[at, :, :, 512:1024] = jnp.where(low_b, at_y(0, 1), at_y(0, -1))
    wide[at, :, :, 1024:1536] = jnp.where(low_a, at_y(1, 0), at_y(-1, 0))
    upper = jnp.where(low_b, at_y(1, 1), at_y(1, -1))
    lower = jnp.where(low_b, at_y(-1, 1), at_y(-1, -1))
    wide[at, :, :, 1536:2048] = jnp.where(low_a, upper, lower)


def fold_taps(products, terms, first_tap, held):
    lane = iota((32, 128), 1)
    for k in range(27):
        tap = (k // 9 - 1, k // 3 % 3 - 1, k % 3 - 1)
        total = None
        for g in range(4):
            part = None
            for td in range(2):
                far, source, target = [], [], []
                for t, parity in ((tap[0], g >> 1), (tap[1], g & 1)):
                    b = parity if t == 0 else 1 - parity
                    far.append(0 if 0 <= b + t <= 1 else 1)
                    target.append(b)
                pos = td + tap[2]
                far_z = 0 if 0 <= pos <= 1 else 1
                source_d = pos & 1
                s = far[0] * 4 + far[1] * 2 + far_z
                rows = (td * 4 + target[0] * 2 + target[1]) * 32
                cols = s * 256 + source_d * 128
                block = products[rows : rows + 32, cols : cols + 128]
                part = block if part is None else part + block
            total = part if total is None else jnp.where((lane >> 5) == g, part, total)
        total = total + pltpu.roll(total, 64, 1)
        total = total + pltpu.roll(total, 32, 1)
        slot = (first_tap + k) % 4
        held = total if held is None else jnp.where((lane >> 5) == slot, total, held)
        if slot == 3:
            row = (first_tap + k) // 4 * 32
            terms[row : row + 32, :] = held.astype(terms.dtype)
            held = None
    return held


def main_kernel(own, faces, far, near, big1, big2, big2t, down_mat,
                give, keep, ef, summed,
                terms, field, ex, eg, eh, mk, ax, ag, ah, turned, products, mixed):
    picks = lane_picks()
    field[1:9, 1:5] = own[...]
    odd = lax.rem(lax.axis_index("tile"), 2)
    field[:, 5 * odd] = far[...]
    field[:, 5 - 5 * odd] = near[...]

    def place(at, face):
        field[at, 1:5] = face

    x_halo(faces, place)
    for store in (ex, eg, eh, ef):
        clear_edges(store)

    for x in range(0, 10, 2):
        rows = field[x : x + 2]
        both = dot(rows[:, :, :, 256:384].reshape(192, 128), down_mat[...], NT)
        mask = both[:, 256:512]
        mk[x : x + 2] = mask.astype(BF).reshape(2, 6, 16, 256)
        grad = (both[:, 0:256] * mask).astype(BF).reshape(2, 6, 16, 256)
        for j in range(2):
            put_field(ex, x + j + 1, 1, rows[j, :, :, 0:256])
            put_field(eg, x + j + 1, 1, grad[j])
    for x in range(0, 10, 2):
        for j in range(2):
            widen(ex, ax, x + j + 1, x + j, 1, 6, picks)
            widen(eg, ag, x + j + 1, x + j, 1, 6, picks)
        mask = mk[x : x + 2].reshape(192, 256).astype(F32)
        pre = dot(ax[x : x + 2].reshape(192, 2048), big1[...]) * mask
        spread = dot(ag[x : x + 2].reshape(192, 2048), big2t[...])
        s = jax.nn.sigmoid(pre)
        hidden = (pre * s).astype(BF).reshape(2, 6, 16, 256)
        grad = (spread * s * (1.0 + pre * (1.0 - s)) * mask).astype(BF).reshape(2, 6, 16, 256)
        for j in range(2):
            put_field(eh, x + j + 1, 1, hidden[j])
            put_field(ef, x + j + 1, 1, grad[j])
    for x in range(0, 8, 4):
        for j in range(4):
            widen(eh, ah, x + j + 2, x + j, 2, 4, picks)
        pre = dot(ah[x : x + 4].reshape(256, 2048), big2[...])
        mask = mk[x + 1 : x + 5, 1:5].reshape(256, 256).astype(F32)
        inputs = field[x + 1 : x + 5, 1:5, :, 0:256].reshape(256, 256).astype(F32)
        summed[x * 64 : x * 64 + 256, :] = (inputs + pre * mask).astype(BF)

    held = None
    for source, grads in ((1, ef), (2, eg)):
        turned[...] = grads[2:10, 2:6, :, 0:256].reshape(512, 256).astype(F32).T.astype(BF)
        for s in range(8):
            cols = slice(s * 256, s * 256 + 256)
            wide = (ax[1:9, 1:5, :, cols] if source == 1 else ah[:, :, :, cols]).reshape(512, 256)
            products[0:256, cols] = dot(turned[...], wide)
        held = fold_taps(products, terms, 27 * (source - 1), held)
    terms[416:448, :] = held.astype(terms.dtype)
    cot = field[1:9, 1:5, :, 256:384].reshape(512, 128).astype(F32).T.astype(BF)
    grad_down = dot(cot, summed[...])
    for i in range(2):
        for j in range(2):
            mixed[pl.ds(i * 64 + j, 32, stride=2), :] = grad_down[j * 32 : j * 32 + 32, i * 128 : i * 128 + 128]
    terms[448:576, :] = mixed[...].astype(terms.dtype)
    rest = terms.shape[0] - 576
    if rest:
        terms[576:, :] = jnp.zeros((rest, 128), terms.dtype)
    half = give.shape[0]
    give[...] = terms[pl.ds(pl.multiple_of((1 - odd) * half, 8), half), :]
    keep[...] = terms[pl.ds(pl.multiple_of(odd * half, 8), half), :]


def tail_kernel(cell_ref, own, ef, summed, big1t, down_mat, grad_features, down, ah, turned, dense, place_mat, shuffle):
    picks = lane_picks()

    for x in range(0, 8, 4):
        for j in range(4):
            widen(ef, ah, x + j + 2, x + j, 2, 4, picks)
        spread = dot(ah[x : x + 4].reshape(256, 2048), big1t[...])
        both = dot(own[x : x + 4, :, :, 256:384].reshape(256, 128), down_mat[...], NT)
        grad = (both[:, 0:256] + spread) * both[:, 256:512]
        dense[x * 64 : x * 64 + 256, :] = grad.astype(BF)
    place_fine(cell_ref, place_mat)
    turned[...] = dense[...].astype(F32).T.astype(BF)
    pick = jnp.where(octant_rows(), 1.0, 0.0)
    for q in range(4):
        moved = dot(turned[...], place_mat[:, q * 512 : q * 512 + 512])
        total = moved[0:32] * pick[0:1]
        for e in range(1, 8):
            total = total + moved[e * 32 : e * 32 + 32] * pick[e : e + 1]
        grad_features[q] = total.astype(BF)
    lowered = dot(summed[...], down_mat[0:256, :]).T.astype(BF)
    low = iota((32, 128), 1) < 64
    for t in range(2):
        moved = dot(lowered, coarse_tile(cell_ref, t))
        even, odd = moved[0:32], moved[32:64]
        shuffle[:, 2 * t, :] = jnp.where(low, even, pltpu.roll(odd, 64, 1))
        shuffle[:, 2 * t + 1, :] = jnp.where(low, pltpu.roll(even, 64, 1), odd)
    for j in range(32):
        down[:, j * 128 : j * 128 + 128] = shuffle[j, 0:4, :].astype(BF)


def pair_kernel(mine, other, out):
    out[...] = (mine[...] + other[...]).astype(out.dtype).reshape(out.shape)


def reduce_kernel(parts, out):
    count = parts.shape[0]
    total = parts[0].astype(F32)
    for i in range(1, count):
        total = total + parts[i].astype(F32)
    total = total.astype(out.dtype)
    for i in range(out.shape[0]):
        out[i] = total


def finish_kernel(scale, mine, other, one, two, down, sums):
    odd = lax.rem(lax.axis_index("tile"), 2)
    half = mine.shape[0]
    sums[pl.ds(pl.multiple_of(odd * half, 8), half), :] = mine[...].astype(F32)
    sums[pl.ds(pl.multiple_of((1 - odd) * half, 8), half), :] = other[...].astype(F32)
    for m in range(14):
        block = (sums[m * 32 : m * 32 + 32, :] * scale).T
        for g in range(4):
            k = 4 * m + g
            if k < 27:
                one[k] = block[g * 32 : g * 32 + 32]
            elif k < 54:
                two[k - 27] = block[g * 32 : g * 32 + 32]
    for half in range(2):
        block = (sums[448 + 64 * half : 512 + 64 * half, :] * scale).T
        for g in range(4):
            down[4 * (g >> 1) + 2 * (g & 1) + half] = block[g * 32 : g * 32 + 32]


def vmem_call(kernel, outs, ins, scratch=(), smem_first=False, flops=0, limit=48, in_space=pltpu.VMEM):
    specs = [pl.BlockSpec(memory_space=in_space) for _ in ins]
    if smem_first:
        specs[0] = pl.BlockSpec(memory_space=pltpu.SMEM)
    moved = sum(math.prod(x.shape) * x.dtype.itemsize for x in tuple(ins) + tuple(outs))
    return pl.pallas_call(
        kernel,
        out_shape=tuple(outs),
        in_specs=specs,
        out_specs=tuple(pl.BlockSpec(memory_space=pltpu.VMEM) for _ in outs),
        scratch_shapes=list(scratch),
        compiler_params=pltpu.CompilerParams(vmem_limit_bytes=limit * 1024 * 1024),
        cost_estimate=pl.CostEstimate(flops=flops, bytes_accessed=moved, transcendentals=0),
    )(*ins)


def bf(*shape):
    return jax.ShapeDtypeStruct(shape, BF)


def f32(*shape):
    return jax.ShapeDtypeStruct(shape, F32)


def on_device(features, voxel_mask, brick_cell, conv_one, conv_two, down_weight, cotangent):
    regions, tiles = lax.axis_size("region"), lax.axis_size("tile")
    devices = regions * tiles
    slots = features.shape[0]
    own, faces = vmem_call(
        gather_kernel,
        [bf(8, 4, 16, 384), bf(regions, 4, 16, 384)],
        (brick_cell, features, voxel_mask, cotangent),
        [pltpu.VMEM((128, 512), BF), pltpu.VMEM((384, 2048), BF), pltpu.VMEM((128, 256), BF),
         pltpu.VMEM((8, 4, 16, 384), F32), pltpu.VMEM((32, 8, 128), F32),
         pltpu.SMEM(brick_cell.shape, I32), pltpu.VMEM(features.shape, BF), pltpu.VMEM(voxel_mask.shape, I32),
         pltpu.VMEM(cotangent.shape, BF), pltpu.SemaphoreType.DMA((4,))],
        in_space=pltpu.HBM,
        flops=2 * 128 * 4 * 768 * 384,
        limit=60,
    )
    faces = lax.all_to_all(faces, "region", 0, 0, tiled=True)
    far, near, own = vmem_call(
        extend_kernel, [bf(10, 16, 384), bf(10, 16, 384), bf(8, 4, 16, 384)], (own, faces), limit=4
    )

    def swap(face, start):
        pairs = [(i, i + 1) for i in range(start, tiles - 1, 2)]
        return lax.ppermute(face, "tile", pairs + [(j, i) for i, j in pairs])

    far = swap(far, 1)
    near = swap(near, 0)
    big1, big1t, big2, big2t, down_mat = vmem_call(
        weights_kernel,
        [bf(2048, 256)] * 4 + [bf(512, 128)],
        (conv_one.reshape(864, 32), conv_two.reshape(864, 32), down_weight),
        [pltpu.VMEM((27, 4, 32, 32), BF), pltpu.VMEM((864, 128), BF), pltpu.VMEM((32, 3456), BF)],
        flops=2 * 2 * 32 * 3456 * 256,
        limit=16,
    )
    chunk = -(-576 // (8 * tiles)) * 8
    half = tiles // 2 * chunk
    give, keep, ef, summed = vmem_call(
        main_kernel,
        [f32(half, 128), f32(half, 128), bf(12, 8, 16, 512), bf(512, 256)],
        (own, faces, far, near, big1, big2, big2t, down_mat),
        [
            pltpu.VMEM((tiles * chunk, 128), F32),
            pltpu.VMEM((10, 6, 16, 384), BF),
            pltpu.VMEM((12, 8, 16, 512), BF),
            pltpu.VMEM((12, 8, 16, 512), BF),
            pltpu.VMEM((12, 8, 16, 512), BF),
            pltpu.VMEM((10, 6, 16, 256), BF),
            pltpu.VMEM((10, 6, 16, 2048), BF),
            pltpu.VMEM((10, 6, 16, 2048), BF),
            pltpu.VMEM((8, 4, 16, 2048), BF),
            pltpu.VMEM((256, 512), BF),
            pltpu.VMEM((256, 2048), F32),
            pltpu.VMEM((128, 128), F32),
        ],
        flops=2 * 2048 * 256 * (960 * 2 + 512 * 3),
        limit=32,
    )
    groups = [list(range(core, tiles, 2)) for core in range(2)]
    (pairs,) = vmem_call(pair_kernel, [bf(tiles // 2, chunk, 128)], (keep, swap(give, 0)), limit=4)
    parts = lax.all_to_all(pairs, "tile", 0, 0, axis_index_groups=groups, tiled=True)
    (total,) = vmem_call(reduce_kernel, [bf(regions, chunk, 128)], (parts,), limit=4)
    parts = lax.all_to_all(total, "region", 0, 0, tiled=True)
    (total,) = vmem_call(reduce_kernel, [bf(tiles // 2, chunk, 128)], (parts,), limit=4)
    mine = lax.all_to_all(total, "tile", 0, 0, axis_index_groups=groups, tiled=True)
    mine = mine.reshape(half, 128)
    other = swap(mine, 0)
    grad_features, down = vmem_call(
        tail_kernel,
        [bf(slots, 32, 512), bf(slots, 4096)],
        (brick_cell, own, ef, summed, big1t, down_mat),
        [
            pltpu.VMEM((8, 4, 16, 2048), BF),
            pltpu.VMEM((256, 512), BF),
            pltpu.VMEM((512, 256), BF),
            pltpu.VMEM((512, 2048), BF),
            pltpu.VMEM((32, 8, 128), F32),
        ],
        smem_first=True,
        flops=2 * 2048 * 512 * 512,
        limit=16,
    )
    scale = 1.0 / math.sqrt(devices * slots * 512.0)
    grad_one, grad_two, grad_down = vmem_call(
        functools.partial(finish_kernel, scale),
        [f32(27, 32, 32), f32(27, 32, 32), f32(8, 32, 64)],
        (mine, other),
        [pltpu.VMEM((tiles * chunk, 128), F32)],
        limit=8,
    )
    return down, grad_features, grad_one, grad_two, grad_down


def solution(mesh):
    in_specs = (
        P(AXES, None, None),
        P(AXES, None),
        P(AXES),
        P(),
        P(),
        P(),
        P(AXES, None),
    )
    out_specs = (P(AXES, None), P(AXES, None, None), P(), P(), P())
    return jax.shard_map(
        on_device, mesh=mesh, in_specs=in_specs, out_specs=out_specs, check_vma=False
    )
```

```python
import functools
import math

import jax
import jax.numpy as jnp
from jax import lax
from jax.experimental import pallas as pl
from jax.experimental.pallas import tpu as pltpu
from jax.sharding import PartitionSpec as P


BF = jnp.bfloat16
F32 = jnp.float32
I32 = jnp.int32
NN = (((1,), (0,)), ((), ()))
NT = (((1,), (1,)), ((), ()))
AXES = ("region", "tile")


def dot(lhs, rhs, dims=NN):
    return lax.dot_general(lhs, rhs, dims, preferred_element_type=F32)


def iota(shape, dim):
    return lax.broadcasted_iota(I32, shape, dim)


def parity_fields(v):
    return v & 1, (v >> 6) & 1, (v >> 3) & 1


def octant_rows(first=0):
    e = iota((8, 512), 0)
    d, a, b = parity_fields(iota((8, 512), 1))
    return (d == (e >> 2)) & (a == ((e >> 1) & 1)) & (b == (e & 1))


def row_codes():
    row = iota((512, 128), 0)
    code = ((row >> 6) & 3) * 16 + ((row >> 4) & 3) * 4 + (row & 3)
    cell = (row >> 8) * 4 + ((row >> 2) & 3)
    return code, cell


def place_fine(cell_ref, place):
    code, cell = row_codes()
    for q in range(4):
        code_q = jnp.where(cell == cell_ref[q], code, -1)
        for t in range(4):
            v = iota((1, 128), 1) + 128 * t
            vcode = (v >> 7) * 16 + ((v >> 4) & 3) * 4 + ((v >> 1) & 3)
            first = q * 512 + t * 128
            place[:, first : first + 128] = jnp.where(code_q == vcode, 1.0, 0.0).astype(BF)


def coarse_tile(cell_ref, t):
    code, cell = row_codes()
    lane = iota((512, 128), 1)
    wanted = jnp.where(lane < 64, cell_ref[2 * t], cell_ref[2 * t + 1])
    return jnp.where((cell == wanted) & (code == (lane & 63)), 1.0, 0.0).astype(BF)


def gather_kernel(cell_hbm, feat_hbm, vmask_hbm, cot_hbm, own, faces,
                  lhs, rhs, cots, box, shuffle, cell_ref, feat_ref, vmask_ref, cot_ref, sems):
    moves = [
        pltpu.make_async_copy(source, target, sems.at[i])
        for i, (source, target) in enumerate(
            ((cell_hbm, cell_ref), (vmask_hbm, vmask_ref), (feat_hbm, feat_ref), (cot_hbm, cot_ref))
        )
    ]
    for move in moves:
        move.start()
    row = iota((128, 128), 0)
    code = (row >> 5) * 16 + ((row >> 3) & 3) * 4 + (row & 3)
    for t in range(4):
        v = iota((1, 128), 1) + 128 * t
        vcode = (v >> 7) * 16 + ((v >> 4) & 3) * 4 + ((v >> 1) & 3)
        lhs[:, t * 128 : t * 128 + 128] = jnp.where(code == vcode, 1.0, 0.0).astype(BF)
    box[...] = jnp.zeros((8, 4, 16, 384), F32)
    for move in moves:
        move.wait()
    match = octant_rows()
    for q in range(4):
        cols = slice(q * 512, q * 512 + 512)
        m8 = jnp.where(match, vmask_ref[q : q + 1, :].astype(F32), 0.0)
        x = feat_ref[q].astype(F32)
        for e in range(8):
            rhs[e * 32 : e * 32 + 32, cols] = (x * m8[e : e + 1, :]).astype(BF)
        rhs[256:320, cols] = jnp.zeros((64, 512), BF)
        rhs[320:336, cols] = jnp.concatenate([m8, jnp.zeros((8, 512), F32)], axis=0).astype(BF)
        rhs[336:384, cols] = jnp.zeros((48, 512), BF)
    cots[64:128, :] = jnp.zeros((64, 256), BF)
    for j in range(32):
        shuffle[j, 0:4, :] = cot_ref[:, j * 128 : j * 128 + 128].astype(F32)
    low = iota((32, 128), 1) < 64
    for t in range(2):
        first, second = shuffle[:, 2 * t, :], shuffle[:, 2 * t + 1, :]
        cols = slice(t * 128, t * 128 + 128)
        cots[0:32, cols] = jnp.where(low, first, pltpu.roll(second, 64, 1)).astype(BF)
        cots[32:64, cols] = jnp.where(low, pltpu.roll(first, 64, 1), second).astype(BF)
    wide_code = iota((128, 256), 0)
    wide_code = (wide_code >> 5) * 16 + ((wide_code >> 3) & 3) * 4 + (wide_code & 3)
    z_part = iota((16, 128), 0) >> 2
    for q in range(4):
        cell = cell_ref[q]
        here_z = jnp.where(cell < 0, -1, cell & 3)
        half = pl.ds(4 * (jnp.maximum(cell, 0) >> 2), 4)
        pick = jnp.where(iota((128, 256), 1) - 64 * q == wide_code, 1.0, 0.0).astype(BF)
        fine = dot(lhs[...], rhs[:, q * 512 : q * 512 + 512], NT)
        third = fine[:, 256:384] + dot(pick, cots[...], NT)
        for t, part in enumerate((fine[:, 0:128], fine[:, 128:256], third)):
            part = part.reshape(4, 4, 8, 128)
            part = jnp.concatenate([part, part], axis=2)
            part = jnp.where((z_part == here_z)[None, None], part, 0.0)
            cols = slice(t * 128, t * 128 + 128)
            box[half, :, :, cols] = box[half, :, :, cols] + part
    field = box[...].astype(BF)
    own[...] = field
    here = lax.axis_index("region")
    for p in range(faces.shape[0]):
        faces[p] = own[jnp.where(p < here, 0, 7)]


def x_halo(faces, place):
    here = lax.axis_index("region")
    count = faces.shape[0]
    for at, there in ((0, here - 1), (9, here + 1)):
        inside = (there >= 0) & (there < count)

        @pl.when(inside)
        def _():
            place(at, faces[jnp.clip(there, 0, count - 1)])

        @pl.when(jnp.logical_not(inside))
        def _():
            place(at, jnp.zeros(faces.shape[1:], BF))


def extend_kernel(own, faces, far, near, own_on):
    own_on[...] = own[...]
    odd = lax.rem(lax.axis_index("tile"), 2)

    def fill(low, high):
        low[1:9] = own[:, 0]
        high[1:9] = own[:, 3]

        def place(at, face):
            low[at] = face[0]
            high[at] = face[3]

        x_halo(faces, place)

    pl.when(odd == 1)(lambda: fill(near, far))
    pl.when(odd == 0)(lambda: fill(far, near))


def tap_of(far, source, target):
    position = source if far == 0 else (2 if source == 0 else -1)
    tap = position - target
    return tap if -1 <= tap <= 1 else None


def weights_kernel(w1_ref, w2_ref, dw_ref, big1, big1t, big2, big2t, down_mat, rep, tiles, tiles_t):
    lane = iota((32, 128), 1)
    spread = jnp.where((lane & 31) == iota((32, 128), 0), 1.0, 0.0).astype(BF)
    eye = jnp.where(iota((32, 32), 0) == iota((32, 32), 1), 1.0, 0.0).astype(BF)
    group = [jnp.where((lane >> 5) == g, 1.0, 0.0).astype(BF) for g in range(4)]
    for w_ref, big, big_t in ((w1_ref, big1, big1t), (w2_ref, big2, big2t)):
        tiles[...] = dot(w_ref[...], spread).astype(BF)
        w3 = w_ref[...].reshape(27, 32, 32)
        for j in range(4):
            rep[:, j] = w3
        tiles_t[...] = dot(eye, rep[...].reshape(27 * 128, 32), NT).astype(BF)
        for s in range(8):
            sx, sy, sz = s >> 2, (s >> 1) & 1, s & 1
            for e in range(8):
                d, a, b = e >> 2, (e >> 1) & 1, e & 1
                first = s * 256 + e * 32
                for td in range(2):
                    plain = None
                    turned = None
                    for g in range(4):
                        taps = (tap_of(sx, a, g >> 1), tap_of(sy, b, g & 1), tap_of(sz, d, td))
                        if None in taps:
                            continue
                        k = 9 * (taps[0] + 1) + 3 * (taps[1] + 1) + taps[2] + 1
                        back = 26 - k
                        term = tiles[k * 32 : k * 32 + 32, :] * group[g]
                        term_t = tiles_t[:, back * 128 : back * 128 + 128] * group[g]
                        plain = term if plain is None else plain + term
                        turned = term_t if turned is None else turned + term_t
                    zero = jnp.zeros((32, 128), BF)
                    big[first : first + 32, td * 128 : td * 128 + 128] = zero if plain is None else plain
                    big_t[first : first + 32, td * 128 : td * 128 + 128] = zero if turned is None else turned
    column = iota((64, 64), 1)
    order = jnp.where(iota((64, 64), 0) == 2 * (column & 31) + (column >> 5), 1.0, 0.0).astype(BF)
    ordered = dot(dw_ref[...].reshape(256, 64), order).astype(BF)
    for e in range(8):
        k = 4 * ((e >> 1) & 1) + 2 * (e & 1) + (e >> 2)
        down_mat[e * 32 : e * 32 + 32, 0:64] = ordered[k * 32 : k * 32 + 32]
    down_mat[0:256, 64:128] = jnp.zeros((256, 64), BF)
    unit = iota((256, 128), 1) - 64 == (iota((256, 128), 0) >> 5)
    down_mat[256:512, :] = jnp.where(unit, 1.0, 0.0).astype(BF)


def lane_picks():
    lane = iota((16, 512), 1)
    low_a = jnp.where(((lane >> 6) & 1) == 0, 1.0, 0.0).astype(BF) > 0.5
    low_b = jnp.where(((lane >> 5) & 1) == 0, 1.0, 0.0).astype(BF) > 0.5
    return low_a[None], low_b[None]


def put_field(store, x, y0, value):
    ny = value.shape[0]
    z = iota((ny, 16, 128), 1)
    store[x, y0 : y0 + ny, :, 0:256] = value
    up = pltpu.roll(value[:, :, 0:128].astype(F32), 15, 1)
    store[x, y0 : y0 + ny, :, 256:384] = jnp.where(z == 15, 0.0, up).astype(BF)
    dn = pltpu.roll(value[:, :, 128:256].astype(F32), 1, 1)
    store[x, y0 : y0 + ny, :, 384:512] = jnp.where(z == 0, 0.0, dn).astype(BF)


def clear_edges(store):
    store[0] = jnp.zeros((8, 16, 512), BF)
    store[11] = jnp.zeros((8, 16, 512), BF)

    def edge(x, carry):
        store[x, 0] = jnp.zeros((16, 512), BF)
        store[x, 7] = jnp.zeros((16, 512), BF)
        return carry

    lax.fori_loop(1, 11, edge, 0)


def widen(store, wide, x, at, y0, ny, picks):
    low_a, low_b = picks
    low_a = jnp.broadcast_to(low_a, (ny, 16, 512))
    low_b = jnp.broadcast_to(low_b, (ny, 16, 512))

    def at_y(dx, dy):
        return store[x + dx, y0 + dy : y0 + dy + ny]

    wide[at, :, :, 0:512] = at_y(0, 0)
    wide[at, :, :, 512:1024] = jnp.where(low_b, at_y(0, 1), at_y(0, -1))
    wide[at, :, :, 1024:1536] = jnp.where(low_a, at_y(1, 0), at_y(-1, 0))
    upper = jnp.where(low_b, at_y(1, 1), at_y(1, -1))
    lower = jnp.where(low_b, at_y(-1, 1), at_y(-1, -1))
    wide[at, :, :, 1536:2048] = jnp.where(low_a, upper, lower)


def fold_taps(products, terms, first_tap, held):
    lane = iota((32, 128), 1)
    for k in range(27):
        tap = (k // 9 - 1, k // 3 % 3 - 1, k % 3 - 1)
        total = None
        for g in range(4):
            part = None
            for td in range(2):
                far, source, target = [], [], []
                for t, parity in ((tap[0], g >> 1), (tap[1], g & 1)):
                    b = parity if t == 0 else 1 - parity
                    far.append(0 if 0 <= b + t <= 1 else 1)
                    target.append(b)
                pos = td + tap[2]
                far_z = 0 if 0 <= pos <= 1 else 1
                source_d = pos & 1
                s = far[0] * 4 + far[1] * 2 + far_z
                rows = (td * 4 + target[0] * 2 + target[1]) * 32
                cols = s * 256 + source_d * 128
                block = products[rows : rows + 32, cols : cols + 128]
                part = block if part is None else part + block
            total = part if total is None else jnp.where((lane >> 5) == g, part, total)
        total = total + pltpu.roll(total, 64, 1)
        total = total + pltpu.roll(total, 32, 1)
        slot = (first_tap + k) % 4
        held = total if held is None else jnp.where((lane >> 5) == slot, total, held)
        if slot == 3:
            row = (first_tap + k) // 4 * 32
            terms[row : row + 32, :] = held.astype(terms.dtype)
            held = None
    return held


def main_kernel(own, faces, far, near, big1, big2, big2t, down_mat,
                give, keep, ef, summed,
                terms, field, ex, eg, eh, mk, ax, ag, ah, turned, products, mixed):
    picks = lane_picks()
    field[1:9, 1:5] = own[...]
    odd = lax.rem(lax.axis_index("tile"), 2)
    field[:, 5 * odd] = far[...]
    field[:, 5 - 5 * odd] = near[...]

    def place(at, face):
        field[at, 1:5] = face

    x_halo(faces, place)
    for store in (ex, eg, eh, ef):
        clear_edges(store)

    for x in range(0, 10, 2):
        rows = field[x : x + 2]
        both = dot(rows[:, :, :, 256:384].reshape(192, 128), down_mat[...], NT)
        mask = both[:, 256:512]
        mk[x : x + 2] = mask.astype(BF).reshape(2, 6, 16, 256)
        grad = (both[:, 0:256] * mask).astype(BF).reshape(2, 6, 16, 256)
        for j in range(2):
            put_field(ex, x + j + 1, 1, rows[j, :, :, 0:256])
            put_field(eg, x + j + 1, 1, grad[j])
    for x in range(0, 10, 2):
        for j in range(2):
            widen(ex, ax, x + j + 1, x + j, 1, 6, picks)
            widen(eg, ag, x + j + 1, x + j, 1, 6, picks)
        mask = mk[x : x + 2].reshape(192, 256).astype(F32)
        pre = dot(ax[x : x + 2].reshape(192, 2048), big1[...]) * mask
        spread = dot(ag[x : x + 2].reshape(192, 2048), big2t[...])
        s = jax.nn.sigmoid(pre)
        hidden = (pre * s).astype(BF).reshape(2, 6, 16, 256)
        grad = (spread * s * (1.0 + pre * (1.0 - s)) * mask).astype(BF).reshape(2, 6, 16, 256)
        for j in range(2):
            put_field(eh, x + j + 1, 1, hidden[j])
            put_field(ef, x + j + 1, 1, grad[j])
    for x in range(0, 8, 4):
        for j in range(4):
            widen(eh, ah, x + j + 2, x + j, 2, 4, picks)
        pre = dot(ah[x : x + 4].reshape(256, 2048), big2[...])
        mask = mk[x + 1 : x + 5, 1:5].reshape(256, 256).astype(F32)
        inputs = field[x + 1 : x + 5, 1:5, :, 0:256].reshape(256, 256).astype(F32)
        summed[x * 64 : x * 64 + 256, :] = (inputs + pre * mask).astype(BF)

    held = None
    for source, grads in ((1, ef), (2, eg)):
        turned[...] = grads[2:10, 2:6, :, 0:256].reshape(512, 256).astype(F32).T.astype(BF)
        for s in range(8):
            cols = slice(s * 256, s * 256 + 256)
            wide = (ax[1:9, 1:5, :, cols] if source == 1 else ah[:, :, :, cols]).reshape(512, 256)
            products[0:256, cols] = dot(turned[...], wide)
        held = fold_taps(products, terms, 27 * (source - 1), held)
    terms[416:448, :] = held.astype(terms.dtype)
    cot = field[1:9, 1:5, :, 256:384].reshape(512, 128).astype(F32).T.astype(BF)
    grad_down = dot(cot, summed[...])
    for i in range(2):
        for j in range(2):
            mixed[pl.ds(i * 64 + j, 32, stride=2), :] = grad_down[j * 32 : j * 32 + 32, i * 128 : i * 128 + 128]
    terms[448:576, :] = mixed[...].astype(terms.dtype)
    rest = terms.shape[0] - 576
    if rest:
        terms[576:, :] = jnp.zeros((rest, 128), terms.dtype)
    half = give.shape[0]
    give[...] = terms[pl.ds(pl.multiple_of((1 - odd) * half, 8), half), :]
    keep[...] = terms[pl.ds(pl.multiple_of(odd * half, 8), half), :]


def tail_kernel(cell_ref, own, ef, summed, big1t, down_mat, grad_features, down, token, ah, turned, dense, place_mat, shuffle):
    picks = lane_picks()

    for x in range(0, 8, 4):
        for j in range(4):
            widen(ef, ah, x + j + 2, x + j, 2, 4, picks)
        spread = dot(ah[x : x + 4].reshape(256, 2048), big1t[...])
        both = dot(own[x : x + 4, :, :, 256:384].reshape(256, 128), down_mat[...], NT)
        grad = (both[:, 0:256] + spread) * both[:, 256:512]
        dense[x * 64 : x * 64 + 256, :] = grad.astype(BF)
    place_fine(cell_ref, place_mat)
    turned[...] = dense[...].astype(F32).T.astype(BF)
    pick = jnp.where(octant_rows(), 1.0, 0.0)
    for q in range(4):
        moved = dot(turned[...], place_mat[:, q * 512 : q * 512 + 512])
        total = moved[0:32] * pick[0:1]
        for e in range(1, 8):
            total = total + moved[e * 32 : e * 32 + 32] * pick[e : e + 1]
        grad_features[q] = total.astype(BF)
    lowered = dot(summed[...], down_mat[0:256, :]).T.astype(BF)
    low = iota((32, 128), 1) < 64
    for t in range(2):
        moved = dot(lowered, coarse_tile(cell_ref, t))
        even, odd = moved[0:32], moved[32:64]
        shuffle[:, 2 * t, :] = jnp.where(low, even, pltpu.roll(odd, 64, 1))
        shuffle[:, 2 * t + 1, :] = jnp.where(low, pltpu.roll(even, 64, 1), odd)
    for j in range(32):
        down[:, j * 128 : j * 128 + 128] = shuffle[j, 0:4, :].astype(BF)
    token[...] = jnp.zeros((8, 128), F32)


def after_kernel(mine, token, out):
    del token
    out[...] = mine[...]


def pair_kernel(mine, other, out):
    out[...] = (mine[...] + other[...]).astype(out.dtype).reshape(out.shape)


def reduce_kernel(parts, out):
    count = parts.shape[0]
    total = parts[0].astype(F32)
    for i in range(1, count):
        total = total + parts[i].astype(F32)
    total = total.astype(out.dtype)
    for i in range(out.shape[0]):
        out[i] = total


def finish_kernel(scale, mine, other, one, two, down, sums):
    odd = lax.rem(lax.axis_index("tile"), 2)
    half = mine.shape[0]
    sums[pl.ds(pl.multiple_of(odd * half, 8), half), :] = mine[...].astype(F32)
    sums[pl.ds(pl.multiple_of((1 - odd) * half, 8), half), :] = other[...].astype(F32)
    for m in range(14):
        block = (sums[m * 32 : m * 32 + 32, :] * scale).T
        for g in range(4):
            k = 4 * m + g
            if k < 27:
                one[k] = block[g * 32 : g * 32 + 32]
            elif k < 54:
                two[k - 27] = block[g * 32 : g * 32 + 32]
    for half in range(2):
        block = (sums[448 + 64 * half : 512 + 64 * half, :] * scale).T
        for g in range(4):
            down[4 * (g >> 1) + 2 * (g & 1) + half] = block[g * 32 : g * 32 + 32]


def vmem_call(kernel, outs, ins, scratch=(), smem_first=False, flops=0, limit=48, in_space=pltpu.VMEM):
    specs = [pl.BlockSpec(memory_space=in_space) for _ in ins]
    if smem_first:
        specs[0] = pl.BlockSpec(memory_space=pltpu.SMEM)
    moved = sum(math.prod(x.shape) * x.dtype.itemsize for x in tuple(ins) + tuple(outs))
    return pl.pallas_call(
        kernel,
        out_shape=tuple(outs),
        in_specs=specs,
        out_specs=tuple(pl.BlockSpec(memory_space=pltpu.VMEM) for _ in outs),
        scratch_shapes=list(scratch),
        compiler_params=pltpu.CompilerParams(vmem_limit_bytes=limit * 1024 * 1024),
        cost_estimate=pl.CostEstimate(flops=flops, bytes_accessed=moved, transcendentals=0),
    )(*ins)


def bf(*shape):
    return jax.ShapeDtypeStruct(shape, BF)


def f32(*shape):
    return jax.ShapeDtypeStruct(shape, F32)


def on_device(features, voxel_mask, brick_cell, conv_one, conv_two, down_weight, cotangent):
    regions, tiles = lax.axis_size("region"), lax.axis_size("tile")
    devices = regions * tiles
    slots = features.shape[0]
    own, faces = vmem_call(
        gather_kernel,
        [bf(8, 4, 16, 384), bf(regions, 4, 16, 384)],
        (brick_cell, features, voxel_mask, cotangent),
        [pltpu.VMEM((128, 512), BF), pltpu.VMEM((384, 2048), BF), pltpu.VMEM((128, 256), BF),
         pltpu.VMEM((8, 4, 16, 384), F32), pltpu.VMEM((32, 8, 128), F32),
         pltpu.SMEM(brick_cell.shape, I32), pltpu.VMEM(features.shape, BF), pltpu.VMEM(voxel_mask.shape, I32),
         pltpu.VMEM(cotangent.shape, BF), pltpu.SemaphoreType.DMA((4,))],
        in_space=pltpu.HBM,
        flops=2 * 128 * 4 * 768 * 384,
        limit=60,
    )
    faces = lax.all_to_all(faces, "region", 0, 0, tiled=True)
    far, near, own = vmem_call(
        extend_kernel, [bf(10, 16, 384), bf(10, 16, 384), bf(8, 4, 16, 384)], (own, faces), limit=4
    )

    def swap(face, start):
        pairs = [(i, i + 1) for i in range(start, tiles - 1, 2)]
        return lax.ppermute(face, "tile", pairs + [(j, i) for i, j in pairs])

    far = swap(far, 1)
    near = swap(near, 0)
    big1, big1t, big2, big2t, down_mat = vmem_call(
        weights_kernel,
        [bf(2048, 256)] * 4 + [bf(512, 128)],
        (conv_one.reshape(864, 32), conv_two.reshape(864, 32), down_weight),
        [pltpu.VMEM((27, 4, 32, 32), BF), pltpu.VMEM((864, 128), BF), pltpu.VMEM((32, 3456), BF)],
        flops=2 * 2 * 32 * 3456 * 256,
        limit=16,
    )
    chunk = -(-576 // (8 * tiles)) * 8
    half = tiles // 2 * chunk
    give, keep, ef, summed = vmem_call(
        main_kernel,
        [f32(half, 128), f32(half, 128), bf(12, 8, 16, 512), bf(512, 256)],
        (own, faces, far, near, big1, big2, big2t, down_mat),
        [
            pltpu.VMEM((tiles * chunk, 128), F32),
            pltpu.VMEM((10, 6, 16, 384), BF),
            pltpu.VMEM((12, 8, 16, 512), BF),
            pltpu.VMEM((12, 8, 16, 512), BF),
            pltpu.VMEM((12, 8, 16, 512), BF),
            pltpu.VMEM((10, 6, 16, 256), BF),
            pltpu.VMEM((10, 6, 16, 2048), BF),
            pltpu.VMEM((10, 6, 16, 2048), BF),
            pltpu.VMEM((8, 4, 16, 2048), BF),
            pltpu.VMEM((256, 512), BF),
            pltpu.VMEM((256, 2048), F32),
            pltpu.VMEM((128, 128), F32),
        ],
        flops=2 * 2048 * 256 * (960 * 2 + 512 * 3),
        limit=32,
    )
    groups = [list(range(core, tiles, 2)) for core in range(2)]
    (pairs,) = vmem_call(pair_kernel, [bf(tiles // 2, chunk, 128)], (keep, swap(give, 0)), limit=4)
    parts = lax.all_to_all(pairs, "tile", 0, 0, axis_index_groups=groups, tiled=True)
    (total,) = vmem_call(reduce_kernel, [bf(regions, chunk, 128)], (parts,), limit=4)
    parts = lax.all_to_all(total, "region", 0, 0, tiled=True)
    (total,) = vmem_call(reduce_kernel, [bf(tiles // 2, chunk, 128)], (parts,), limit=4)
    mine = lax.all_to_all(total, "tile", 0, 0, axis_index_groups=groups, tiled=True)
    mine = mine.reshape(half, 128)
    grad_features, down, token = vmem_call(
        tail_kernel,
        [bf(slots, 32, 512), bf(slots, 4096), f32(8, 128)],
        (brick_cell, own, ef, summed, big1t, down_mat),
        [
            pltpu.VMEM((8, 4, 16, 2048), BF),
            pltpu.VMEM((256, 512), BF),
            pltpu.VMEM((512, 256), BF),
            pltpu.VMEM((512, 2048), BF),
            pltpu.VMEM((32, 8, 128), F32),
        ],
        smem_first=True,
        flops=2 * 2048 * 512 * 512,
        limit=16,
    )
    (mine,) = vmem_call(after_kernel, [bf(half, 128)], (mine, token), limit=4)
    other = swap(mine, 0)
    scale = 1.0 / math.sqrt(devices * slots * 512.0)
    grad_one, grad_two, grad_down = vmem_call(
        functools.partial(finish_kernel, scale),
        [f32(27, 32, 32), f32(27, 32, 32), f32(8, 32, 64)],
        (mine, other),
        [pltpu.VMEM((tiles * chunk, 128), F32)],
        limit=8,
    )
    return down, grad_features, grad_one, grad_two, grad_down


def solution(mesh):
    in_specs = (
        P(AXES, None, None),
        P(AXES, None),
        P(AXES),
        P(),
        P(),
        P(),
        P(AXES, None),
    )
    out_specs = (P(AXES, None), P(AXES, None, None), P(), P(), P())
    return jax.shard_map(
        on_device, mesh=mesh, in_specs=in_specs, out_specs=out_specs, check_vma=False
    )
```

```python
import functools
import math

import jax
import jax.numpy as jnp
from jax import lax
from jax.experimental import pallas as pl
from jax.experimental.pallas import tpu as pltpu
from jax.sharding import PartitionSpec as P


BF = jnp.bfloat16
F32 = jnp.float32
I32 = jnp.int32
NN = (((1,), (0,)), ((), ()))
NT = (((1,), (1,)), ((), ()))
AXES = ("region", "tile")


def dot(lhs, rhs, dims=NN):
    return lax.dot_general(lhs, rhs, dims, preferred_element_type=F32)


def iota(shape, dim):
    return lax.broadcasted_iota(I32, shape, dim)


def parity_fields(v):
    return v & 1, (v >> 6) & 1, (v >> 3) & 1


def octant_rows(first=0):
    e = iota((8, 512), 0)
    d, a, b = parity_fields(iota((8, 512), 1))
    return (d == (e >> 2)) & (a == ((e >> 1) & 1)) & (b == (e & 1))


def row_codes():
    row = iota((512, 128), 0)
    code = ((row >> 6) & 3) * 16 + ((row >> 4) & 3) * 4 + (row & 3)
    cell = (row >> 8) * 4 + ((row >> 2) & 3)
    return code, cell


def place_fine(cell_ref, place):
    code, cell = row_codes()
    for q in range(4):
        code_q = jnp.where(cell == cell_ref[q], code, -1)
        for t in range(4):
            v = iota((1, 128), 1) + 128 * t
            vcode = (v >> 7) * 16 + ((v >> 4) & 3) * 4 + ((v >> 1) & 3)
            first = q * 512 + t * 128
            place[:, first : first + 128] = jnp.where(code_q == vcode, 1.0, 0.0).astype(BF)


def coarse_tile(cell_ref, t):
    code, cell = row_codes()
    lane = iota((512, 128), 1)
    wanted = jnp.where(lane < 64, cell_ref[2 * t], cell_ref[2 * t + 1])
    return jnp.where((cell == wanted) & (code == (lane & 63)), 1.0, 0.0).astype(BF)


def gather_kernel(cell_hbm, feat_hbm, vmask_hbm, cot_hbm, own, faces,
                  lhs, rhs, cots, box, shuffle, cell_ref, feat_ref, vmask_ref, cot_ref, sems):
    moves = [
        pltpu.make_async_copy(source, target, sems.at[i])
        for i, (source, target) in enumerate(
            ((cell_hbm, cell_ref), (vmask_hbm, vmask_ref), (feat_hbm, feat_ref), (cot_hbm, cot_ref))
        )
    ]
    for move in moves:
        move.start()
    row = iota((128, 128), 0)
    code = (row >> 5) * 16 + ((row >> 3) & 3) * 4 + (row & 3)
    for t in range(4):
        v = iota((1, 128), 1) + 128 * t
        vcode = (v >> 7) * 16 + ((v >> 4) & 3) * 4 + ((v >> 1) & 3)
        lhs[:, t * 128 : t * 128 + 128] = jnp.where(code == vcode, 1.0, 0.0).astype(BF)
    box[...] = jnp.zeros((8, 4, 16, 384), F32)
    for move in moves:
        move.wait()
    match = octant_rows()
    for q in range(4):
        cols = slice(q * 512, q * 512 + 512)
        m8 = jnp.where(match, vmask_ref[q : q + 1, :].astype(F32), 0.0)
        x = feat_ref[q].astype(F32)
        for e in range(8):
            rhs[e * 32 : e * 32 + 32, cols] = (x * m8[e : e + 1, :]).astype(BF)
        rhs[256:320, cols] = jnp.zeros((64, 512), BF)
        rhs[320:336, cols] = jnp.concatenate([m8, jnp.zeros((8, 512), F32)], axis=0).astype(BF)
        rhs[336:384, cols] = jnp.zeros((48, 512), BF)
    cots[64:128, :] = jnp.zeros((64, 256), BF)
    for j in range(32):
        shuffle[j, 0:4, :] = cot_ref[:, j * 128 : j * 128 + 128].astype(F32)
    low = iota((32, 128), 1) < 64
    for t in range(2):
        first, second = shuffle[:, 2 * t, :], shuffle[:, 2 * t + 1, :]
        cols = slice(t * 128, t * 128 + 128)
        cots[0:32, cols] = jnp.where(low, first, pltpu.roll(second, 64, 1)).astype(BF)
        cots[32:64, cols] = jnp.where(low, pltpu.roll(first, 64, 1), second).astype(BF)
    wide_code = iota((128, 256), 0)
    wide_code = (wide_code >> 5) * 16 + ((wide_code >> 3) & 3) * 4 + (wide_code & 3)
    z_part = iota((16, 128), 0) >> 2
    for q in range(4):
        cell = cell_ref[q]
        here_z = jnp.where(cell < 0, -1, cell & 3)
        half = pl.ds(4 * (jnp.maximum(cell, 0) >> 2), 4)
        pick = jnp.where(iota((128, 256), 1) - 64 * q == wide_code, 1.0, 0.0).astype(BF)
        fine = dot(lhs[...], rhs[:, q * 512 : q * 512 + 512], NT)
        third = fine[:, 256:384] + dot(pick, cots[...], NT)
        for t, part in enumerate((fine[:, 0:128], fine[:, 128:256], third)):
            part = part.reshape(4, 4, 8, 128)
            part = jnp.concatenate([part, part], axis=2)
            part = jnp.where((z_part == here_z)[None, None], part, 0.0)
            cols = slice(t * 128, t * 128 + 128)
            box[half, :, :, cols] = box[half, :, :, cols] + part
    field = box[...].astype(BF)
    own[...] = field
    here = lax.axis_index("region")
    for p in range(faces.shape[0]):
        faces[p] = own[jnp.where(p < here, 0, 7)]


def x_halo(faces, place):
    here = lax.axis_index("region")
    count = faces.shape[0]
    for at, there in ((0, here - 1), (9, here + 1)):
        inside = (there >= 0) & (there < count)

        @pl.when(inside)
        def _():
            place(at, faces[jnp.clip(there, 0, count - 1)])

        @pl.when(jnp.logical_not(inside))
        def _():
            place(at, jnp.zeros(faces.shape[1:], BF))


def extend_kernel(own, faces, far, near, own_on):
    own_on[...] = own[...]
    odd = lax.rem(lax.axis_index("tile"), 2)

    def fill(low, high):
        low[1:9] = own[:, 0]
        high[1:9] = own[:, 3]

        def place(at, face):
            low[at] = face[0]
            high[at] = face[3]

        x_halo(faces, place)

    pl.when(odd == 1)(lambda: fill(near, far))
    pl.when(odd == 0)(lambda: fill(far, near))


def tap_of(far, source, target):
    position = source if far == 0 else (2 if source == 0 else -1)
    tap = position - target
    return tap if -1 <= tap <= 1 else None


def weights_kernel(w1_ref, w2_ref, dw_ref, big1, big1t, big2, big2t, down_mat, rep, tiles, tiles_t):
    lane = iota((32, 128), 1)
    spread = jnp.where((lane & 31) == iota((32, 128), 0), 1.0, 0.0).astype(BF)
    eye = jnp.where(iota((32, 32), 0) == iota((32, 32), 1), 1.0, 0.0).astype(BF)
    group = [jnp.where((lane >> 5) == g, 1.0, 0.0).astype(BF) for g in range(4)]
    for w_ref, big, big_t in ((w1_ref, big1, big1t), (w2_ref, big2, big2t)):
        tiles[...] = dot(w_ref[...], spread).astype(BF)
        w3 = w_ref[...].reshape(27, 32, 32)
        for j in range(4):
            rep[:, j] = w3
        tiles_t[...] = dot(eye, rep[...].reshape(27 * 128, 32), NT).astype(BF)
        for s in range(8):
            sx, sy, sz = s >> 2, (s >> 1) & 1, s & 1
            for e in range(8):
                d, a, b = e >> 2, (e >> 1) & 1, e & 1
                first = s * 256 + e * 32
                for td in range(2):
                    plain = None
                    turned = None
                    for g in range(4):
                        taps = (tap_of(sx, a, g >> 1), tap_of(sy, b, g & 1), tap_of(sz, d, td))
                        if None in taps:
                            continue
                        k = 9 * (taps[0] + 1) + 3 * (taps[1] + 1) + taps[2] + 1
                        back = 26 - k
                        term = tiles[k * 32 : k * 32 + 32, :] * group[g]
                        term_t = tiles_t[:, back * 128 : back * 128 + 128] * group[g]
                        plain = term if plain is None else plain + term
                        turned = term_t if turned is None else turned + term_t
                    zero = jnp.zeros((32, 128), BF)
                    big[first : first + 32, td * 128 : td * 128 + 128] = zero if plain is None else plain
                    big_t[first : first + 32, td * 128 : td * 128 + 128] = zero if turned is None else turned
    column = iota((64, 64), 1)
    order = jnp.where(iota((64, 64), 0) == 2 * (column & 31) + (column >> 5), 1.0, 0.0).astype(BF)
    ordered = dot(dw_ref[...].reshape(256, 64), order).astype(BF)
    for e in range(8):
        k = 4 * ((e >> 1) & 1) + 2 * (e & 1) + (e >> 2)
        down_mat[e * 32 : e * 32 + 32, 0:64] = ordered[k * 32 : k * 32 + 32]
    down_mat[0:256, 64:128] = jnp.zeros((256, 64), BF)
    unit = iota((256, 128), 1) - 64 == (iota((256, 128), 0) >> 5)
    down_mat[256:512, :] = jnp.where(unit, 1.0, 0.0).astype(BF)


def lane_picks():
    lane = iota((16, 512), 1)
    low_a = jnp.where(((lane >> 6) & 1) == 0, 1.0, 0.0).astype(BF) > 0.5
    low_b = jnp.where(((lane >> 5) & 1) == 0, 1.0, 0.0).astype(BF) > 0.5
    return low_a[None], low_b[None]


def put_field(store, x, y0, value):
    ny = value.shape[0]
    z = iota((ny, 16, 128), 1)
    store[x, y0 : y0 + ny, :, 0:256] = value
    up = pltpu.roll(value[:, :, 0:128].astype(F32), 15, 1)
    store[x, y0 : y0 + ny, :, 256:384] = jnp.where(z == 15, 0.0, up).astype(BF)
    dn = pltpu.roll(value[:, :, 128:256].astype(F32), 1, 1)
    store[x, y0 : y0 + ny, :, 384:512] = jnp.where(z == 0, 0.0, dn).astype(BF)


def clear_edges(store):
    store[0] = jnp.zeros((8, 16, 512), BF)
    store[11] = jnp.zeros((8, 16, 512), BF)

    def edge(x, carry):
        store[x, 0] = jnp.zeros((16, 512), BF)
        store[x, 7] = jnp.zeros((16, 512), BF)
        return carry

    lax.fori_loop(1, 11, edge, 0)


def widen(store, wide, x, at, y0, ny, picks):
    low_a, low_b = picks
    low_a = jnp.broadcast_to(low_a, (ny, 16, 512))
    low_b = jnp.broadcast_to(low_b, (ny, 16, 512))

    def at_y(dx, dy):
        return store[x + dx, y0 + dy : y0 + dy + ny]

    wide[at, :, :, 0:512] = at_y(0, 0)
    wide[at, :, :, 512:1024] = jnp.where(low_b, at_y(0, 1), at_y(0, -1))
    wide[at, :, :, 1024:1536] = jnp.where(low_a, at_y(1, 0), at_y(-1, 0))
    upper = jnp.where(low_b, at_y(1, 1), at_y(1, -1))
    lower = jnp.where(low_b, at_y(-1, 1), at_y(-1, -1))
    wide[at, :, :, 1536:2048] = jnp.where(low_a, upper, lower)


def fold_taps(products, terms, first_tap, held):
    lane = iota((32, 128), 1)
    for k in range(27):
        tap = (k // 9 - 1, k // 3 % 3 - 1, k % 3 - 1)
        total = None
        for g in range(4):
            part = None
            for td in range(2):
                far, source, target = [], [], []
                for t, parity in ((tap[0], g >> 1), (tap[1], g & 1)):
                    b = parity if t == 0 else 1 - parity
                    far.append(0 if 0 <= b + t <= 1 else 1)
                    target.append(b)
                pos = td + tap[2]
                far_z = 0 if 0 <= pos <= 1 else 1
                source_d = pos & 1
                s = far[0] * 4 + far[1] * 2 + far_z
                rows = (td * 4 + target[0] * 2 + target[1]) * 32
                cols = s * 256 + source_d * 128
                block = products[rows : rows + 32, cols : cols + 128]
                part = block if part is None else part + block
            total = part if total is None else jnp.where((lane >> 5) == g, part, total)
        total = total + pltpu.roll(total, 64, 1)
        total = total + pltpu.roll(total, 32, 1)
        slot = (first_tap + k) % 4
        held = total if held is None else jnp.where((lane >> 5) == slot, total, held)
        if slot == 3:
            row = (first_tap + k) // 4 * 32
            terms[row : row + 32, :] = held.astype(terms.dtype)
            held = None
    return held


def main_kernel(own, faces, far, near, big1, big2, big2t, down_mat,
                terms, ef, summed,
                field, ex, eg, eh, mk, ax, ag, ah, turned, products, mixed):
    picks = lane_picks()
    field[1:9, 1:5] = own[...]
    odd = lax.rem(lax.axis_index("tile"), 2)
    field[:, 5 * odd] = far[...]
    field[:, 5 - 5 * odd] = near[...]

    def place(at, face):
        field[at, 1:5] = face

    x_halo(faces, place)
    for store in (ex, eg, eh, ef):
        clear_edges(store)

    for x in range(0, 10, 2):
        rows = field[x : x + 2]
        both = dot(rows[:, :, :, 256:384].reshape(192, 128), down_mat[...], NT)
        mask = both[:, 256:512]
        mk[x : x + 2] = mask.astype(BF).reshape(2, 6, 16, 256)
        grad = (both[:, 0:256] * mask).astype(BF).reshape(2, 6, 16, 256)
        for j in range(2):
            put_field(ex, x + j + 1, 1, rows[j, :, :, 0:256])
            put_field(eg, x + j + 1, 1, grad[j])
    for x in range(0, 10, 5):
        for j in range(5):
            widen(ex, ax, x + j + 1, x + j, 1, 6, picks)
            widen(eg, ag, x + j + 1, x + j, 1, 6, picks)
        mask = mk[x : x + 5].reshape(480, 256).astype(F32)
        pre = dot(ax[x : x + 5].reshape(480, 2048), big1[...]) * mask
        spread = dot(ag[x : x + 5].reshape(480, 2048), big2t[...])
        s = jax.nn.sigmoid(pre)
        hidden = (pre * s).astype(BF).reshape(5, 6, 16, 256)
        grad = (spread * s * (1.0 + pre * (1.0 - s)) * mask).astype(BF).reshape(5, 6, 16, 256)
        for j in range(5):
            put_field(eh, x + j + 1, 1, hidden[j])
            put_field(ef, x + j + 1, 1, grad[j])
    for x in range(0, 8, 4):
        for j in range(4):
            widen(eh, ah, x + j + 2, x + j, 2, 4, picks)
        pre = dot(ah[x : x + 4].reshape(256, 2048), big2[...])
        mask = mk[x + 1 : x + 5, 1:5].reshape(256, 256).astype(F32)
        inputs = field[x + 1 : x + 5, 1:5, :, 0:256].reshape(256, 256).astype(F32)
        summed[x * 64 : x * 64 + 256, :] = (inputs + pre * mask).astype(BF)

    held = None
    for source, grads in ((1, ef), (2, eg)):
        turned[...] = grads[2:10, 2:6, :, 0:256].reshape(512, 256).astype(F32).T.astype(BF)
        for s in range(8):
            cols = slice(s * 256, s * 256 + 256)
            wide = (ax[1:9, 1:5, :, cols] if source == 1 else ah[:, :, :, cols]).reshape(512, 256)
            products[0:256, cols] = dot(turned[...], wide)
        held = fold_taps(products, terms, 27 * (source - 1), held)
    terms[416:448, :] = held.astype(terms.dtype)
    cot = field[1:9, 1:5, :, 256:384].reshape(512, 128).astype(F32).T.astype(BF)
    grad_down = dot(cot, summed[...])
    for half in range(2):
        for odd in range(2):
            part = grad_down[odd * 32 : odd * 32 + 32, half * 128 : half * 128 + 128]
            mixed[pl.ds(half * 64 + odd, 32, stride=2), :] = part
    terms[448:576, :] = mixed[...].astype(terms.dtype)
    rest = terms.shape[0] - 576
    if rest:
        terms[576:, :] = jnp.zeros((rest, 128), terms.dtype)


def tail_kernel(cell_ref, own, ef, summed, big1t, down_mat, grad_features, down, ah, turned, dense, place_mat, shuffle):
    picks = lane_picks()

    for x in range(0, 8, 4):
        for j in range(4):
            widen(ef, ah, x + j + 2, x + j, 2, 4, picks)
        spread = dot(ah[x : x + 4].reshape(256, 2048), big1t[...])
        both = dot(own[x : x + 4, :, :, 256:384].reshape(256, 128), down_mat[...], NT)
        grad = (both[:, 0:256] + spread) * both[:, 256:512]
        dense[x * 64 : x * 64 + 256, :] = grad.astype(BF)
    place_fine(cell_ref, place_mat)
    turned[...] = dense[...].astype(F32).T.astype(BF)
    pick = jnp.where(octant_rows(), 1.0, 0.0)
    for q in range(4):
        moved = dot(turned[...], place_mat[:, q * 512 : q * 512 + 512])
        total = moved[0:32] * pick[0:1]
        for e in range(1, 8):
            total = total + moved[e * 32 : e * 32 + 32] * pick[e : e + 1]
        grad_features[q] = total.astype(BF)
    lowered = dot(summed[...], down_mat[0:256, :]).T.astype(BF)
    low = iota((32, 128), 1) < 64
    for t in range(2):
        moved = dot(lowered, coarse_tile(cell_ref, t))
        even, odd = moved[0:32], moved[32:64]
        shuffle[:, 2 * t, :] = jnp.where(low, even, pltpu.roll(odd, 64, 1))
        shuffle[:, 2 * t + 1, :] = jnp.where(low, pltpu.roll(even, 64, 1), odd)
    for j in range(32):
        down[:, j * 128 : j * 128 + 128] = shuffle[j, 0:4, :].astype(BF)


def reduce_kernel(parts, out):
    count = parts.shape[0]
    total = parts[0].astype(F32)
    for i in range(1, count):
        total = total + parts[i].astype(F32)
    total = total.astype(out.dtype)
    for i in range(out.shape[0]):
        out[i] = total


def finish_kernel(scale, sums, one, two, down):
    for m in range(14):
        block = (sums[m * 32 : m * 32 + 32, :].astype(F32) * scale).T
        for g in range(4):
            k = 4 * m + g
            if k < 27:
                one[k] = block[g * 32 : g * 32 + 32]
            elif k < 54:
                two[k - 27] = block[g * 32 : g * 32 + 32]
    for half in range(2):
        block = (sums[448 + 64 * half : 512 + 64 * half, :].astype(F32) * scale).T
        for g in range(4):
            down[4 * (g >> 1) + 2 * (g & 1) + half] = block[g * 32 : g * 32 + 32]


def vmem_call(kernel, outs, ins, scratch=(), smem_first=False, flops=0, limit=48, in_space=pltpu.VMEM):
    specs = [pl.BlockSpec(memory_space=in_space) for _ in ins]
    if smem_first:
        specs[0] = pl.BlockSpec(memory_space=pltpu.SMEM)
    moved = sum(math.prod(x.shape) * x.dtype.itemsize for x in tuple(ins) + tuple(outs))
    return pl.pallas_call(
        kernel,
        out_shape=tuple(outs),
        in_specs=specs,
        out_specs=tuple(pl.BlockSpec(memory_space=pltpu.VMEM) for _ in outs),
        scratch_shapes=list(scratch),
        compiler_params=pltpu.CompilerParams(vmem_limit_bytes=limit * 1024 * 1024),
        cost_estimate=pl.CostEstimate(flops=flops, bytes_accessed=moved, transcendentals=0),
    )(*ins)


def bf(*shape):
    return jax.ShapeDtypeStruct(shape, BF)


def f32(*shape):
    return jax.ShapeDtypeStruct(shape, F32)


def on_device(features, voxel_mask, brick_cell, conv_one, conv_two, down_weight, cotangent):
    regions, tiles = lax.axis_size("region"), lax.axis_size("tile")
    devices = regions * tiles
    slots = features.shape[0]
    own, faces = vmem_call(
        gather_kernel,
        [bf(8, 4, 16, 384), bf(regions, 4, 16, 384)],
        (brick_cell, features, voxel_mask, cotangent),
        [pltpu.VMEM((128, 512), BF), pltpu.VMEM((384, 2048), BF), pltpu.VMEM((128, 256), BF),
         pltpu.VMEM((8, 4, 16, 384), F32), pltpu.VMEM((32, 8, 128), F32),
         pltpu.SMEM(brick_cell.shape, I32), pltpu.VMEM(features.shape, BF), pltpu.VMEM(voxel_mask.shape, I32),
         pltpu.VMEM(cotangent.shape, BF), pltpu.SemaphoreType.DMA((4,))],
        in_space=pltpu.HBM,
        flops=2 * 128 * 4 * 768 * 384,
        limit=60,
    )
    faces = lax.all_to_all(faces, "region", 0, 0, tiled=True)
    far, near, own = vmem_call(
        extend_kernel, [bf(10, 16, 384), bf(10, 16, 384), bf(8, 4, 16, 384)], (own, faces), limit=4
    )

    def swap(face, start):
        pairs = [(i, i + 1) for i in range(start, tiles - 1, 2)]
        return lax.ppermute(face, "tile", pairs + [(j, i) for i, j in pairs])

    far = swap(far, 1)
    near = swap(near, 0)
    big1, big1t, big2, big2t, down_mat = vmem_call(
        weights_kernel,
        [bf(2048, 256)] * 4 + [bf(512, 128)],
        (conv_one.reshape(864, 32), conv_two.reshape(864, 32), down_weight),
        [pltpu.VMEM((27, 4, 32, 32), BF), pltpu.VMEM((864, 128), BF), pltpu.VMEM((32, 3456), BF)],
        flops=2 * 2 * 32 * 3456 * 256,
        limit=16,
    )
    chunk = -(-576 // (8 * tiles)) * 8
    terms, ef, summed = vmem_call(
        main_kernel,
        [bf(tiles * chunk, 128), bf(12, 8, 16, 512), bf(512, 256)],
        (own, faces, far, near, big1, big2, big2t, down_mat),
        [
            pltpu.VMEM((10, 6, 16, 384), BF),
            pltpu.VMEM((12, 8, 16, 512), BF),
            pltpu.VMEM((12, 8, 16, 512), BF),
            pltpu.VMEM((12, 8, 16, 512), BF),
            pltpu.VMEM((10, 6, 16, 256), BF),
            pltpu.VMEM((10, 6, 16, 2048), BF),
            pltpu.VMEM((10, 6, 16, 2048), BF),
            pltpu.VMEM((8, 4, 16, 2048), BF),
            pltpu.VMEM((256, 512), BF),
            pltpu.VMEM((256, 2048), F32),
            pltpu.VMEM((128, 128), F32),
        ],
        flops=2 * 2048 * 256 * (960 * 2 + 512 * 3),
        limit=32,
    )
    parts = lax.all_to_all(terms.reshape(tiles, chunk, 128), "tile", 0, 0, tiled=True)
    (total,) = vmem_call(reduce_kernel, [bf(regions, chunk, 128)], (parts,), limit=4)
    parts = lax.all_to_all(total, "region", 0, 0, tiled=True)
    (total,) = vmem_call(reduce_kernel, [bf(tiles, chunk, 128)], (parts,), limit=4)
    sums = lax.all_to_all(total, "tile", 0, 0, tiled=True)
    grad_features, down = vmem_call(
        tail_kernel,
        [bf(slots, 32, 512), bf(slots, 4096)],
        (brick_cell, own, ef, summed, big1t, down_mat),
        [
            pltpu.VMEM((8, 4, 16, 2048), BF),
            pltpu.VMEM((256, 512), BF),
            pltpu.VMEM((512, 256), BF),
            pltpu.VMEM((512, 2048), BF),
            pltpu.VMEM((32, 8, 128), F32),
        ],
        smem_first=True,
        flops=2 * 2048 * 512 * 512,
        limit=16,
    )
    scale = 1.0 / math.sqrt(devices * slots * 512.0)
    grad_one, grad_two, grad_down = vmem_call(
        functools.partial(finish_kernel, scale),
        [f32(27, 32, 32), f32(27, 32, 32), f32(8, 32, 64)],
        (sums.reshape(tiles * chunk, 128),),
        limit=8,
    )
    return down, grad_features, grad_one, grad_two, grad_down


def solution(mesh):
    in_specs = (
        P(AXES, None, None),
        P(AXES, None),
        P(AXES),
        P(),
        P(),
        P(),
        P(AXES, None),
    )
    out_specs = (P(AXES, None), P(AXES, None, None), P(), P(), P())
    return jax.shard_map(
        on_device, mesh=mesh, in_specs=in_specs, out_specs=out_specs, check_vma=False
    )
```
